32 devices in a mesh: dp: 8 (over y, x, core), fsdp: 4 (over z).
Axes of the slice: x: 2, y: 2, z: 4, core: 2. Of those that a mesh axis runs over, the one named last changes fastest.
Arguments:
- hidden_in: bfloat16 [2, 2, 256, 64, 768], P(None, None, ('dp', 'fsdp')), may hold values from -6 to 6
- lengths: int32 [2, 2, 256], P(None, None, ('dp', 'fsdp')), may hold values from 4 to 64, as said below
- partner: int32 [2, 256], replicated, may hold values from 0 to 255, each once within a row
- language: int32 [2, 256], replicated, may hold values from 0 to 7
- token_cotangent: bfloat16 [2, 2, 256, 64, 768], P(None, None, ('dp', 'fsdp')), may hold values from -6 to 6
- query_weight: bfloat16 [768, 768], P(('dp', 'fsdp')), may hold values from -0.21875 to 0.21875
- key_weight: bfloat16 [768, 768], P(('dp', 'fsdp')), may hold values from -0.21875 to 0.21875
- value_weight: bfloat16 [768, 768], P(('dp', 'fsdp')), may hold values from -0.21875 to 0.21875
- attn_out_weight: bfloat16 [768, 768], P(('dp', 'fsdp')), may hold values from -0.875 to 0.875
- query_bias: bfloat16 [768], P(('dp', 'fsdp')), may hold values from -3 to 3
- value_bias: bfloat16 [768], P(('dp', 'fsdp')), may hold values from -3 to 3
- attn_out_bias: bfloat16 [768], P(('dp', 'fsdp')), may hold values from -3 to 3
- ln1_gain: bfloat16 [768], P(('dp', 'fsdp')), may hold values from 0.5 to 1.5
- ln1_shift: bfloat16 [768], P(('dp', 'fsdp')), may hold values from -3 to 3
- in_weight: bfloat16 [768, 3072], P(('dp', 'fsdp')), may hold values from -0.21875 to 0.21875
- in_bias: bfloat16 [3072], P(('dp', 'fsdp')), may hold values from -3 to 3
- out_weight: bfloat16 [3072, 768], P(('dp', 'fsdp')), may hold values from -0.109375 to 0.109375
- out_bias: bfloat16 [768], P(('dp', 'fsdp')), may hold values from -3 to 3
- ln2_gain: bfloat16 [768], P(('dp', 'fsdp')), may hold values from 0.5 to 1.5
- ln2_shift: bfloat16 [768], P(('dp', 'fsdp')), may hold values from -3 to 3
- pool_weight: bfloat16 [768, 768], P(('dp', 'fsdp')), may hold values from -0.21875 to 0.21875
- pool_bias: bfloat16 [768], P(('dp', 'fsdp')), may hold values from -3 to 3
Outputs:
- block_out: bfloat16 [2, 2, 256, 64, 768], P(None, None, ('dp', 'fsdp'))
- input_grad: float32 [2, 2, 256, 64, 768], P(None, None, ('dp', 'fsdp'))
- grad_query_weight: float32 [768, 768], P(('dp', 'fsdp'))
- grad_key_weight: float32 [768, 768], P(('dp', 'fsdp'))
- grad_value_weight: float32 [768, 768], P(('dp', 'fsdp'))
- grad_attn_out_weight: float32 [768, 768], P(('dp', 'fsdp'))
- grad_query_bias: float32 [768], P(('dp', 'fsdp'))
- grad_value_bias: float32 [768], P(('dp', 'fsdp'))
- grad_attn_out_bias: float32 [768], P(('dp', 'fsdp'))
- grad_ln1_gain: float32 [768], P(('dp', 'fsdp'))
- grad_ln1_shift: float32 [768], P(('dp', 'fsdp'))
- grad_in_weight: float32 [768, 3072], P(('dp', 'fsdp'))
- grad_in_bias: float32 [3072], P(('dp', 'fsdp'))
- grad_out_weight: float32 [3072, 768], P(('dp', 'fsdp'))
- grad_out_bias: float32 [768], P(('dp', 'fsdp'))
- grad_ln2_gain: float32 [768], P(('dp', 'fsdp'))
- grad_ln2_shift: float32 [768], P(('dp', 'fsdp'))
- grad_pool_weight: float32 [768, 768], P(('dp', 'fsdp'))
- grad_pool_bias: float32 [768], P(('dp', 'fsdp'))
The draws below stay inside these ranges and needn't reach their ends.
Inputs may be any that keep to these rules, and one draw needn't show every extreme that they name: `lengths`: positions at or past a sentence's length are padding; position 0 is its first token, which the pooler reads. Each row is a permutation: source sentence i of micro-batch m translates to target sentence partner[m, i] of the same micro-batch. language[m, i] is the language of source sentence i and of its translation.
All inputs are finite; a program needn't handle non-finite values.
Results may differ from the reference program's by a relative error of at most 0.018.
The reference program's roundings to bfloat16 on the way count: a program that leaves them out, or rounds other values in their place, can miss the bound.
Values may be sent and summed in bfloat16 or wider, within the bound.
A program may use at most 320 MiB of HBM per device.

```python
import math
import jax
import jax.numpy as jnp
from jax import lax

D = 768
FF = 3072
HEAD_DIM = 64
SEQ = 64
MB = 2
LANGS = 8
PAIRS = 256


def draw_lengths(key, part):
    key = jax.random.fold_in(key, 11)
    first_key, second_key = jax.random.split(key)
    drawn = jax.random.randint(first_key, (MB, 2, PAIRS), 4, SEQ + 1)
    chosen = jax.random.randint(second_key, (), 0, MB * 2 * PAIRS)
    flat_index = jnp.arange(MB * 2 * PAIRS).reshape(MB, 2, PAIRS)
    return jnp.where(flat_index == chosen, SEQ, drawn).astype(jnp.int32)


def set_ends(values, rng, smallest, high):
    extent = values.shape
    place = [jax.random.randint(jax.random.fold_in(rng, axis), (), 0, extent[axis]) for axis in range(len(extent))]
    values = values.at[tuple(place)].set(smallest)
    longest = extent.index(max(extent))
    place[longest] = (place[longest] + 1) % extent[longest]
    return values.at[tuple(place)].set(high)


def block_scale(rng, extent, shards, smallest, top_value):
    def one(axis_at, shards_of):
        steps = jax.random.uniform(jax.random.fold_in(jax.random.fold_in(rng, 6), axis_at), (shards_of,), jnp.float32, smallest / len(shards), top_value / len(shards))
        return jnp.repeat(jnp.exp(steps), extent[axis_at] // shards_of).reshape((-1,) + (1,) * (len(extent) - axis_at - 1))

    factor_of = one(*shards[0])
    for cut in shards[1:]:
        factor_of = factor_of * one(*cut)
    return factor_of


def normal_values(stream_key, dims, deviation, limit, cuts=(), dtype=jnp.bfloat16):
    array = jax.random.normal(stream_key, dims, jnp.float32) * deviation
    if len(cuts) > 0:
        array = block_scale(stream_key, dims, cuts, -0.22, 0.18) * array
    return jnp.clip(array, min=-limit, max=limit).astype(dtype)


def setup_inputs(seed: int = 0) -> dict:
    key_list = jax.random.split(jax.random.key(seed), 23)
    return {
        "hidden_in": normal_values(key_list[0], (MB, 2, PAIRS, SEQ, D), 1.0, 6.0, ((2, 32),)),
        "lengths": draw_lengths(jax.random.fold_in(key_list[22], 71), 0),
        "partner": jax.vmap(lambda own: jax.random.permutation(own, PAIRS))(jax.random.split(key_list[2], MB)).reshape((MB, PAIRS)).astype(jnp.int32),
        "language": set_ends(jax.random.randint(key_list[3], (MB, PAIRS), 0, LANGS), jax.random.fold_in(key_list[3], 1), 0, LANGS - 1).astype(jnp.int32),
        "token_cotangent": normal_values(key_list[4], (MB, 2, PAIRS, SEQ, D), 1.0, 6.0, ((2, 32),)),
        "query_weight": normal_values(key_list[5], (D, D), D ** -0.5, 0.21875, ((0, 32),)),
        "key_weight": normal_values(key_list[6], (D, D), D ** -0.5, 0.21875, ((0, 32),)),
        "value_weight": normal_values(key_list[7], (D, D), D ** -0.5, 0.21875, ((0, 32),)),
        "attn_out_weight": normal_values(key_list[8], (D, D), (D // 16) ** -0.5, 0.875, ((0, 32),)),
        "query_bias": normal_values(key_list[9], (D,), 0.5, 3.0, ((0, 32),)),
        "value_bias": normal_values(key_list[10], (D,), 0.5, 3.0, ((0, 32),)),
        "attn_out_bias": normal_values(key_list[11], (D,), 0.5, 3.0, ((0, 32),)),
        "ln1_gain": jnp.clip(1.0 + 0.1 * jax.random.normal(key_list[12], (D,), jnp.float32), 0.5, 1.5).astype(jnp.bfloat16),
        "ln1_shift": normal_values(key_list[13], (D,), 0.5, 3.0, ((0, 32),)),
        "in_weight": normal_values(key_list[14], (D, FF), D ** -0.5, 0.21875, ((0, 32),)),
        "in_bias": normal_values(key_list[15], (FF,), 0.5, 3.0, ((0, 32),)),
        "out_weight": normal_values(key_list[16], (FF, D), FF ** -0.5, 0.109375, ((0, 32),)),
        "out_bias": normal_values(key_list[17], (D,), 0.5, 3.0, ((0, 32),)),
        "ln2_gain": jnp.clip(1.0 + 0.1 * jax.random.normal(key_list[18], (D,), jnp.float32), 0.5, 1.5).astype(jnp.bfloat16),
        "ln2_shift": normal_values(key_list[19], (D,), 0.5, 3.0, ((0, 32),)),
        "pool_weight": normal_values(key_list[20], (D, D), D ** -0.5, 0.21875, ((0, 32),)),
        "pool_bias": normal_values(key_list[21], (D,), 0.5, 3.0, ((0, 32),)),
    }


@jax.custom_vjp
def low(v):
    return lax.optimization_barrier(v.astype(jnp.bfloat16)).astype(jnp.float32)

@jax.custom_vjp
def low_back(v):
    return v

def low_keep(v):
    return (low(v), None)

def low_pass(kept, grad):
    return (grad,)

def back_keep(v):
    return (v, None)

def back_low(kept, grad):
    return (low(grad),)
low.defvjp(low_keep, low_pass)
low_back.defvjp(back_keep, back_low)
LN_EPS = 1e-06
UNIT_EPS = 1e-06
SIM_SCALE = 10.0
MARGIN = 0.3
MASKED = -1e+30

def both_ways(tensor):
    return low(low_back(tensor))

def product(first_mat, second_mat):
    return jnp.matmul(first_mat, second_mat, precision=lax.Precision.HIGHEST)

def layer_norm(row_data, gain_vec, shift_vec):
    centred = row_data - lax.optimization_barrier(jnp.mean(row_data, -1, keepdims=True))
    return centred * lax.rsqrt(lax.optimization_barrier(jnp.mean(centred * centred, -1, keepdims=True)) + LN_EPS) * gain_vec + shift_vec

def encode(params, sentences, sent_lengths):
    query_weight, key_weight, value_weight, attn_out_weight, query_bias, value_bias, attn_out_bias, ln1_gain, ln1_shift, in_weight, in_bias, out_weight, out_bias, ln2_gain, ln2_shift, pool_weight, pool_bias = params
    sentence_count, seq_len, model_width = sentences.shape
    head_shape = (sentence_count, seq_len, model_width // HEAD_DIM, HEAD_DIM)
    queries = both_ways(product(sentences, query_weight) + query_bias).reshape(head_shape)
    key_rows = both_ways(product(sentences, key_weight)).reshape(head_shape)
    values = both_ways(product(sentences, value_weight) + value_bias).reshape(head_shape)
    scores = jnp.einsum('gqhe,gkhe->ghqk', queries, key_rows, precision=lax.Precision.HIGHEST) * HEAD_DIM ** (-0.5)
    scores = low_back(scores)
    key_valid = jnp.arange(seq_len)[None, :] < sent_lengths[:, None]
    scores = jnp.where(key_valid[:, None, None, :], scores, MASKED)
    probabilities = low(jax.nn.softmax(scores, axis=-1))
    mixture = jnp.einsum('ghqk,gkhe->gqhe', probabilities, values, precision=lax.Precision.HIGHEST)
    mixture = both_ways(mixture.reshape(sentence_count, seq_len, model_width))
    first_sum = sentences + low_back(product(mixture, attn_out_weight)) + attn_out_bias
    hidden = layer_norm(first_sum, ln1_gain, ln1_shift)
    inner_act = low_back(product(low(hidden), in_weight)) + in_bias
    active = low(jax.nn.gelu(inner_act, approximate=False))
    second_sum = hidden + low_back(product(active, out_weight)) + out_bias
    output = layer_norm(second_sum, ln2_gain, ln2_shift)
    pooled = jnp.tanh(low_back(product(low(output[:, 0]), pool_weight)) + pool_bias)
    unit_vec = pooled * lax.rsqrt(lax.optimization_barrier(jnp.sum(pooled * pooled, -1, keepdims=True)) + UNIT_EPS)
    return (output, low(unit_vec))

def pair_loss(sources, targets, partner_row, language_row):
    pair_count = sources.shape[0]
    similar = low_back(SIM_SCALE * product(sources, targets.T))
    positive = partner_row[:, None] == jnp.arange(pair_count)[None, :]
    target_language = jnp.zeros((pair_count,), jnp.int32).at[partner_row].set(language_row)
    included = language_row[:, None] == target_language[None, :]
    scored = jnp.where(included, similar - SIM_SCALE * MARGIN * positive, MASKED)
    row_total = jax.nn.logsumexp(scored, axis=1)
    col_total = jax.nn.logsumexp(scored, axis=0)
    matched = jnp.sum(jnp.where(positive, scored, 0.0))
    return jnp.sum(row_total) + jnp.sum(col_total) - 2.0 * matched

def reference(hidden_in, lengths, partner, language, token_cotangent, query_weight, key_weight, value_weight, attn_out_weight, query_bias, value_bias, attn_out_bias, ln1_gain, ln1_shift, in_weight, in_bias, out_weight, out_bias, ln2_gain, ln2_shift, pool_weight, pool_bias):
    params = tuple((weight_arr.astype(jnp.float32) for weight_arr in (query_weight, key_weight, value_weight, attn_out_weight, query_bias, value_bias, attn_out_bias, ln1_gain, ln1_shift, in_weight, in_bias, out_weight, out_bias, ln2_gain, ln2_shift, pool_weight, pool_bias)))

    def forward(weights, inputs):
        group_size = math.gcd(PAIRS, 32)
        groups = PAIRS // group_size
        shaped = jnp.moveaxis(inputs.reshape(MB, 2, groups, group_size, SEQ, D), 2, 1)
        shaped = shaped.reshape(MB * groups, 2 * group_size, SEQ, D)
        group_lengths = jnp.moveaxis(lengths.reshape(MB, 2, groups, group_size), 2, 1)
        group_lengths = group_lengths.reshape(MB * groups, 2 * group_size)

        def one_group(pieces):
            return encode(weights, pieces[0], pieces[1])
        outputs, unit_vecs = lax.map(jax.checkpoint(one_group), (shaped, group_lengths))
        outputs = jnp.moveaxis(outputs.reshape(MB, groups, 2, group_size, SEQ, D), 1, 2)
        outputs = outputs.reshape(MB, 2, PAIRS, SEQ, D)
        unit_vecs = jnp.moveaxis(unit_vecs.reshape(MB, groups, 2, group_size, D), 1, 2)
        unit_vecs = unit_vecs.reshape(MB, 2, PAIRS, D)
        loss_sum = jnp.zeros((), jnp.float32)
        for micro_step in range(MB):
            loss_sum = loss_sum + pair_loss(unit_vecs[micro_step, 0], unit_vecs[micro_step, 1], partner[micro_step], language[micro_step])
        return (outputs, loss_sum)
    (outputs, loss_sum), pull_back = jax.vjp(forward, params, hidden_in.astype(jnp.float32))
    gradients, input_grad = pull_back((token_cotangent.astype(jnp.float32), jnp.ones((), jnp.float32)))
    return (outputs.astype(jnp.bfloat16), input_grad, gradients[0], gradients[1], gradients[2], gradients[3], gradients[4], gradients[5], gradients[6], gradients[7], gradients[8], gradients[9], gradients[10], gradients[11], gradients[12], gradients[13], gradients[14], gradients[15], gradients[16])
```

```python
import functools

import jax
import jax.numpy as jnp
from jax import lax
from jax.experimental import pallas as pl
from jax.experimental.pallas import tpu as pltpu
from jax.sharding import PartitionSpec as P

HEAD_DIM = 64


LN_EPS = 1e-06
UNIT_EPS = 1e-06
SIM_SCALE = 10.0
MARGIN = 0.3
MASKED = -1e30
MIB = 1024 * 1024


MESH_ID = pl.DeviceIdType.MESH
AXES = ("dp", "fsdp")


class Layout:
    def __init__(self, mesh_shape):
        slow, fast = mesh_shape["dp"], mesh_shape["fsdp"]
        self.slow, self.count = slow, slow * fast
        if slow == 8:
            self.dims = (2, 2, 2, fast)
            self.orders = ((3, 1, 0, 2), (3, 0, 1, 2))
        else:
            self.dims = (slow, fast)
            self.orders = ((1, 0), (1, 0))
        self.sends = sum(size - 1 for size in self.dims)

    def own(self):
        digits = [lax.axis_index("fsdp")]
        rest = lax.axis_index("dp")
        for size in self.dims[-2::-1]:
            digits.insert(0, rest % size)
            rest = rest // size
        return digits

    def device(self, digits):
        slow = digits[0]
        for size, digit in zip(self.dims[1:-1], digits[1:-1]):
            slow = slow * size + digit
        return (slow, digits[-1])

    def shifted(self, own, dim, step):
        size = self.dims[dim]
        out = list(own)
        out[dim] = (own[dim] + step) % size
        return out

    def first_slot(self, order, stage):
        return sum(self.dims[dim] - 1 for dim in order[:stage])

    def greet(self, own):
        barrier = pltpu.get_barrier_semaphore()
        for dim, size in enumerate(self.dims):
            for step in range(1, size):
                pl.semaphore_signal(
                    barrier,
                    inc=1,
                    device_id=self.device(self.shifted(own, dim, step)),
                    device_id_type=MESH_ID,
                )
        pl.semaphore_wait(barrier, self.sends)


class GatherJob:
    def __init__(self, layout, own, order, shard, full, sems, columns=None):
        self.layout, self.own, self.order = layout, own, order
        self.shard, self.full, self.columns = shard, full, columns
        self.send_sems, self.recv_sems, self.local_sem = sems

    def block(self, digits, done):
        index = tuple(
            slice(None) if dim in done else digits[dim] for dim in range(len(self.layout.dims))
        )
        if self.columns is not None:
            index = index + (slice(None), pl.ds(*self.columns))
        return self.full.at[index]

    def piece(self):
        if self.columns is not None:
            return self.shard.at[:, pl.ds(*self.columns)]
        return self.shard

    def copies(self, stage, sending):
        dim, done = self.order[stage], self.order[:stage]
        base = self.layout.first_slot(self.order, stage)
        out = []
        for step in range(1, self.layout.dims[dim]):
            slot = base + step - 1
            other = self.layout.shifted(self.own, dim, step if sending else -step)
            target = self.block(self.own if sending else other, done)
            source = self.piece() if sending and stage == 0 else target
            out.append(
                pltpu.make_async_remote_copy(
                    src_ref=source,
                    dst_ref=target,
                    send_sem=self.send_sems.at[slot],
                    recv_sem=self.recv_sems.at[slot],
                    device_id=self.layout.device(other),
                    device_id_type=MESH_ID,
                )
            )
        return out

    def local(self):
        return pltpu.make_async_copy(self.piece(), self.block(self.own, ()), self.local_sem)

    def advance(self, stage):
        if stage == 0:
            self.local().start()
        else:
            for copy in self.copies(stage - 1, False):
                copy.wait_recv()
            if stage == 1:
                self.local().wait()
        if stage < len(self.order):
            for copy in self.copies(stage, True):
                copy.start()

    def finish(self):
        for stage in range(len(self.order)):
            for copy in self.copies(stage, True):
                copy.wait_send()


def run_rounds(jobs, stages, width=2):
    rounds = []
    last = stages + (len(jobs) - 1) // width
    for step in range(last + 1):
        todo = []
        for index, job in enumerate(jobs):
            stage = step - index // width
            if 0 <= stage <= stages:
                todo.append((job, stage))
        rounds.append(todo)
    return rounds


class ScatterJob:
    def __init__(self, layout, own, order, part, sums, lands, result, sems, columns=None):
        self.layout, self.own, self.order = layout, own, order
        self.part, self.sums, self.lands, self.result = part, sums, lands, result
        self.send_sems, self.recv_sems, self.local_sem = sems
        self.columns = columns

    def tail(self):
        if self.columns is not None:
            return (slice(None), pl.ds(*self.columns))
        return ()

    def local(self):
        dim = self.order[0]
        index = [slice(None)] * len(self.layout.dims)
        index[dim] = self.own[dim]
        return pltpu.make_async_copy(
            self.part.at[tuple(index) + self.tail()], self.sums[0], self.local_sem
        )

    def copies(self, stage):
        dim = self.order[stage]
        base = self.layout.first_slot(self.order, stage)
        left = [d for d in range(len(self.layout.dims)) if d not in self.order[:stage]]
        out = []
        for step in range(1, self.layout.dims[dim]):
            slot = base + step - 1
            there = self.layout.shifted(self.own, dim, step)
            index = tuple(there[dim] if d == dim else slice(None) for d in left)
            if stage == 0:
                source = self.part.at[index + self.tail()]
            else:
                source = self.sums[stage - 1].at[index]
            out.append(
                pltpu.make_async_remote_copy(
                    src_ref=source,
                    dst_ref=self.lands[stage].at[step - 1],
                    send_sem=self.send_sems.at[slot],
                    recv_sem=self.recv_sems.at[slot],
                    device_id=self.layout.device(there),
                    device_id_type=MESH_ID,
                )
            )
        return out

    def add(self, stage):
        dim = self.order[stage]
        left = [d for d in range(len(self.layout.dims)) if d not in self.order[:stage]]
        rest = [d for d in left if d != dim]
        sizes = [self.layout.dims[d] for d in rest]
        total = 1
        for size in sizes:
            total *= size

        def body(flat):
            digits = []
            for size in reversed(sizes):
                digits.insert(0, flat % size)
                flat = flat // size
            if stage == 0:
                own_index = tuple(digits)
                value = self.sums[0][own_index].astype(jnp.float32)
            else:
                where = dict(zip(rest, digits))
                where[dim] = self.own[dim]
                value = self.sums[stage - 1][tuple(where[d] for d in left)].astype(jnp.float32)
            for step in range(1, self.layout.dims[dim]):
                value = value + self.lands[stage][(step - 1,) + tuple(digits)].astype(jnp.float32)
            if rest:
                target = self.sums[stage]
                target[tuple(digits)] = value.astype(target.dtype)
            elif self.columns is not None:
                self.result[:, pl.ds(*self.columns)] = value
            else:
                self.result[...] = value

        if total == 1:
            body(0)
        else:
            pl.loop(0, total)(body)

    def advance(self, stage):
        if stage == 0:
            self.local().start()
        else:
            for copy in self.copies(stage - 1):
                copy.wait_recv()
            if stage == 1:
                self.local().wait()
            self.add(stage - 1)
        if stage < len(self.order):
            for copy in self.copies(stage):
                copy.start()

    def finish(self):
        for stage in range(len(self.order)):
            for copy in self.copies(stage):
                copy.wait_send()


def scatter_buffers(layout, order, rows, columns, dtype):
    sums, lands = [], []
    for stage, dim in enumerate(order):
        rest = tuple(
            size for d, size in enumerate(layout.dims) if d not in order[: stage + 1]
        )
        lands.append(pltpu.VMEM((layout.dims[dim] - 1,) + rest + (rows, columns), dtype))
        if stage < len(order) - 1:
            sums.append(pltpu.VMEM(rest + (rows, columns), dtype))
    return sums + lands


def gather_kernel(layout, plan, count, *refs):
    shards, fulls = refs[:count], refs[count : 2 * count]
    send_sems, recv_sems, local_sems = refs[2 * count :]
    own = layout.own()
    layout.greet(own)
    jobs = [
        GatherJob(
            layout,
            own,
            layout.orders[way],
            shards[which],
            fulls[which],
            (send_sems.at[at], recv_sems.at[at], local_sems.at[at]),
            columns,
        )
        for at, (which, way, columns) in enumerate(plan)
    ]
    for todo in run_rounds(jobs, len(layout.dims)):
        for job, stage in todo:
            job.advance(stage)
    for job in jobs:
        job.finish()


def gather_all(layout, arrays, plan, collective_id):
    anywhere = pl.BlockSpec(memory_space=pl.ANY)
    return pl.pallas_call(
        functools.partial(gather_kernel, layout, plan, len(arrays)),
        out_shape=[jax.ShapeDtypeStruct(layout.dims + a.shape, a.dtype) for a in arrays],
        in_specs=[anywhere] * len(arrays),
        out_specs=[anywhere] * len(arrays),
        scratch_shapes=[
            pltpu.SemaphoreType.DMA((len(plan), layout.sends)),
            pltpu.SemaphoreType.DMA((len(plan), layout.sends)),
            pltpu.SemaphoreType.DMA((len(plan),)),
        ],
        compiler_params=pltpu.CompilerParams(
            collective_id=collective_id, has_side_effects=True, vmem_limit_bytes=16 * MIB
        ),
    )(*arrays)


def scatter_kernel(layout, plan, count, buffers, *refs):
    parts, results = refs[:count], refs[count : 2 * count]
    scratch, (send_sems, recv_sems, local_sems) = refs[2 * count : -3], refs[-3:]
    own = layout.own()
    layout.greet(own)
    jobs = []
    stages = len(layout.dims)
    for at, (which, way, columns) in enumerate(plan):
        mine = scratch[at * buffers : (at + 1) * buffers]
        jobs.append(
            ScatterJob(
                layout,
                own,
                layout.orders[way][::-1],
                parts[which],
                mine[: stages - 1],
                mine[stages - 1 :],
                results[which],
                (send_sems.at[at], recv_sems.at[at], local_sems.at[at]),
                columns,
            )
        )
    for todo in run_rounds(jobs, stages):
        for job, stage in todo:
            job.advance(stage)
    for job in jobs:
        job.finish()


def scatter_all(layout, arrays, plan, collective_id):
    stages = len(layout.dims)
    scratch = []
    for which, way, columns in plan:
        rows, width = arrays[which].shape[-2:]
        width = width if columns is None else columns[1]
        scratch += scatter_buffers(
            layout, layout.orders[way][::-1], rows, width, arrays[which].dtype
        )
    return pl.pallas_call(
        functools.partial(scatter_kernel, layout, plan, len(arrays), 2 * stages - 1),
        out_shape=[jax.ShapeDtypeStruct(a.shape[-2:], jnp.float32) for a in arrays],
        in_specs=[pl.BlockSpec(memory_space=pl.ANY)] * len(arrays),
        out_specs=[pl.BlockSpec(memory_space=pltpu.VMEM)] * len(arrays),
        scratch_shapes=scratch
        + [
            pltpu.SemaphoreType.DMA((len(plan), layout.sends)),
            pltpu.SemaphoreType.DMA((len(plan), layout.sends)),
            pltpu.SemaphoreType.DMA((len(plan),)),
        ],
        compiler_params=pltpu.CompilerParams(
            collective_id=collective_id, has_side_effects=True, vmem_limit_bytes=60 * MIB
        ),
    )(*arrays)


def cut(which, way, width, pieces):
    if width % (pieces * 128):
        return [(which, way, None)]
    step = width // pieces
    return [(which, way, (at * step, step)) for at in range(pieces)]


def weave(first, second):
    out = []
    for at in range(max(len(first), len(second))):
        out += first[at : at + 1] + second[at : at + 1]
    return out


def small_pack(layout, vectors):
    flat = jnp.concatenate([v.astype(jnp.float32).reshape(v.shape[0], -1) for v in vectors], 1)
    width = -(-flat.shape[1] // 1024) * 1024
    flat = jnp.pad(flat, ((0, 0), (0, width - flat.shape[1])))
    return flat.reshape(flat.shape[0], width // 128, 128)


def dot_plain(first_mat, second_mat):
    return jnp.dot(first_mat, second_mat, preferred_element_type=jnp.float32)


def dot_left_t(first_mat, second_mat):
    return lax.dot_general(
        first_mat, second_mat, (((0,), (0,)), ((), ())), preferred_element_type=jnp.float32
    )


def dot_right_t(first_mat, second_mat):
    return lax.dot_general(
        first_mat, second_mat, (((1,), (1,)), ((), ())), preferred_element_type=jnp.float32
    )


def norm_forward(row_data, gain_vec, shift_vec):
    centred = row_data - jnp.mean(row_data, -1, keepdims=True)
    inverse = lax.rsqrt(jnp.mean(centred * centred, -1, keepdims=True) + LN_EPS)
    normed = centred * inverse
    return (normed * gain_vec + shift_vec, normed, inverse)


def norm_backward(upstream, normed, inverse, gain_vec):
    scaled = upstream * gain_vec
    back = inverse * (
        scaled
        - jnp.mean(scaled, -1, keepdims=True)
        - normed * jnp.mean(scaled * normed, -1, keepdims=True)
    )
    return (back, jnp.sum(upstream * normed, 0), jnp.sum(upstream, 0))


def gelu_slope(inner_act):
    return (
        0.5 * (1.0 + lax.erf(inner_act * 0.7071067811865476))
        + inner_act * jnp.exp(-0.5 * inner_act * inner_act) * 0.3989422804014327
    )


def attention_scores(queries, key_rows, sent_lengths):
    seq_len = queries.shape[1]
    scores = jnp.einsum("gqhe,gkhe->ghqk", queries, key_rows, preferred_element_type=jnp.float32)
    scores = scores * queries.shape[3] ** (-0.5)
    key_valid = jnp.arange(seq_len)[None, :] < sent_lengths[:, None]
    return jnp.where(key_valid[:, None, None, :], scores, MASKED)


def on_device(
    layout,
    hidden_in,
    lengths,
    partner,
    language,
    token_cotangent,
    query_weight,
    key_weight,
    value_weight,
    attn_out_weight,
    query_bias,
    value_bias,
    attn_out_bias,
    ln1_gain,
    ln1_shift,
    in_weight,
    in_bias,
    out_weight,
    out_bias,
    ln2_gain,
    ln2_shift,
    pool_weight,
    pool_bias,
):
    micro_count, sides, pair_dev, seq_len, model_width = hidden_in.shape
    inner_width = in_weight.shape[1]
    count = layout.count
    node_dev = sides * pair_dev
    sent_count = micro_count * node_dev
    row_count = sent_count * seq_len
    head_shape = (sent_count, seq_len, model_width // HEAD_DIM, HEAD_DIM)
    head_scale = HEAD_DIM ** (-0.5)
    pair_count = partner.shape[1]
    device = lax.axis_index("dp") * (count // layout.slow) + lax.axis_index("fsdp")

    vectors = (
        query_bias,
        value_bias,
        attn_out_bias,
        ln1_gain,
        ln1_shift,
        out_bias,
        ln2_gain,
        ln2_shift,
        pool_bias,
        in_bias,
    )
    small = small_pack(layout, [v[None] for v in vectors])[0]
    arrays = [
        query_weight,
        key_weight,
        value_weight,
        attn_out_weight,
        small,
        pool_weight,
        in_weight,
        out_weight,
    ]
    plan = [(4, 0, None), (0, 1, None), (1, 0, None), (2, 1, None), (3, 0, None), (5, 1, None)]
    plan += weave(cut(6, 0, inner_width, 4), cut(7, 1, model_width, 3))
    gathered = gather_all(layout, arrays, tuple(plan), 0)
    query_full, key_full, value_full, proj_full, small_full, pool_full, inner_full, outer_full = [
        full.reshape((count * array.shape[0],) + array.shape[1:])
        for full, array in zip(gathered, arrays)
    ]
    small_rows = small_full.reshape(count, -1)
    wide = []
    at = 0
    for v in vectors:
        wide.append(small_rows[:, at : at + v.shape[0]].reshape(-1))
        at += v.shape[0]
    (
        query_shift,
        value_shift,
        proj_shift,
        gain_first,
        shift_first,
        outer_shift,
        gain_second,
        shift_second,
        pool_shift,
        inner_shift,
    ) = wide

    tokens = hidden_in.reshape(row_count, model_width)
    sent_lengths = lengths.reshape(sent_count)
    queries = (dot_plain(tokens, query_full) + query_shift).astype(jnp.bfloat16)
    queries = queries.reshape(head_shape)
    key_rows = dot_plain(tokens, key_full).astype(jnp.bfloat16).reshape(head_shape)
    values = (dot_plain(tokens, value_full) + value_shift).astype(jnp.bfloat16)
    values = values.reshape(head_shape)
    scores = attention_scores(queries, key_rows, sent_lengths)
    peak = jnp.max(scores, -1, keepdims=True)
    log_totals = jnp.log(jnp.sum(jnp.exp(scores - peak), -1, keepdims=True)) + peak
    probs_b = jnp.exp(scores - log_totals).astype(jnp.bfloat16)
    mixture = jnp.einsum("ghqk,gkhe->gqhe", probs_b, values, preferred_element_type=jnp.float32)
    mixture = mixture.reshape(row_count, model_width).astype(jnp.bfloat16)
    first_sum = tokens.astype(jnp.float32) + dot_plain(mixture, proj_full) + proj_shift
    hidden, normed_one, inverse_one = norm_forward(first_sum, gain_first, shift_first)
    hidden_b = hidden.astype(jnp.bfloat16)
    inner_act = dot_plain(hidden_b, inner_full) + inner_shift
    active = jax.nn.gelu(inner_act, approximate=False).astype(jnp.bfloat16)
    second_sum = hidden + dot_plain(active, outer_full) + outer_shift
    output, normed_two, inverse_two = norm_forward(second_sum, gain_second, shift_second)
    block_out = output.astype(jnp.bfloat16).reshape(hidden_in.shape)

    cls_rows = output.reshape(sent_count, seq_len, model_width)[:, 0].astype(jnp.bfloat16)
    pooled = jnp.tanh(dot_plain(cls_rows, pool_full) + pool_shift)
    scale_inv = lax.rsqrt(jnp.sum(pooled * pooled, -1, keepdims=True) + UNIT_EPS)
    unit_vec = pooled * scale_inv
    unit_b = unit_vec.astype(jnp.bfloat16)
    (units,) = gather_all(layout, [unit_b], ((0, 0, None),), 1)
    units = units.reshape(count, micro_count, node_dev, model_width)
    units = jnp.moveaxis(units, 1, 0).reshape(micro_count, count * node_dev, model_width)
    pair_ids = jnp.arange(pair_count, dtype=jnp.int32)
    hit = partner[:, :, None] == pair_ids[None, None, :]
    target_language = jnp.sum(jnp.where(hit, language[:, :, None], 0), 1)

    def nodes(first, second):
        shape = (micro_count, count, 1, pair_dev)
        joined = jnp.concatenate([first.reshape(shape), second.reshape(shape)], 2)
        return joined.reshape(micro_count, count * node_dev)

    tongue = nodes(language, target_language)
    place = nodes(partner, jnp.broadcast_to(pair_ids, partner.shape))
    side = nodes(jnp.zeros_like(partner), jnp.ones_like(partner))
    across = side[:, :, None] != side[:, None, :]
    positive = across & (place[:, :, None] == place[:, None, :])
    include = across & (tongue[:, :, None] == tongue[:, None, :])
    similar = jnp.einsum("mid,mjd->mij", units, units, preferred_element_type=jnp.float32)
    scored = jnp.where(include, SIM_SCALE * similar - SIM_SCALE * MARGIN * positive, MASKED)
    totals = jax.nn.logsumexp(scored, axis=2)
    grad_sim = jnp.where(
        include,
        jnp.exp(scored - totals[:, :, None]) + jnp.exp(scored - totals[:, None, :]),
        0.0,
    )
    grad_sim = (grad_sim - 2.0 * positive).astype(jnp.bfloat16)
    grad_sim = lax.dynamic_slice_in_dim(grad_sim, device * node_dev, node_dev, 1)
    unit_grad = SIM_SCALE * jnp.einsum(
        "mij,mjd->mid", grad_sim, units, preferred_element_type=jnp.float32
    )
    unit_grad = unit_grad.reshape(sent_count, model_width)
    pooled_grad = scale_inv * (
        unit_grad - unit_vec * jnp.sum(unit_grad * unit_vec, -1, keepdims=True)
    )
    pre_grad = pooled_grad * (1.0 - pooled * pooled)
    pre_grad_b = pre_grad.astype(jnp.bfloat16)
    grad_pool = dot_left_t(cls_rows, pre_grad_b)
    grad_pool_shift = jnp.sum(pre_grad, 0)
    cls_grad = dot_right_t(pre_grad_b, pool_full)
    out_grad = token_cotangent.reshape(sent_count, seq_len, model_width).astype(jnp.float32)
    first = jnp.arange(seq_len)[None, :, None] == 0
    out_grad = out_grad + jnp.where(first, cls_grad[:, None, :], 0.0)
    out_grad = out_grad.reshape(row_count, model_width)
    second_grad, grad_gain_two, grad_shift_two = norm_backward(
        out_grad, normed_two, inverse_two, gain_second
    )
    second_b = second_grad.astype(jnp.bfloat16)
    grad_outer = dot_left_t(active, second_b)
    grad_outer_shift = jnp.sum(second_grad, 0)
    inner_grad = dot_right_t(second_b, outer_full) * gelu_slope(inner_act)
    grad_inner_shift = jnp.sum(inner_grad, 0)
    inner_b = inner_grad.astype(jnp.bfloat16)
    grad_inner = dot_left_t(hidden_b, inner_b)
    hidden_grad = second_grad + dot_right_t(inner_b, inner_full)
    first_grad, grad_gain_one, grad_shift_one = norm_backward(
        hidden_grad, normed_one, inverse_one, gain_first
    )
    grad_proj_shift = jnp.sum(first_grad, 0)
    first_b = first_grad.astype(jnp.bfloat16)
    grad_proj = dot_left_t(mixture, first_b)
    mixture_grad = dot_right_t(first_b, proj_full).astype(jnp.bfloat16).reshape(head_shape)
    probs_full = jnp.exp(scores - log_totals)
    prob_grad = jnp.einsum(
        "gqhe,gkhe->ghqk", mixture_grad, values, preferred_element_type=jnp.float32
    )
    value_grad = jnp.einsum(
        "ghqk,gqhe->gkhe", probs_b, mixture_grad, preferred_element_type=jnp.float32
    )
    value_grad = value_grad.astype(jnp.bfloat16).reshape(row_count, model_width)
    score_grad = probs_full * (prob_grad - jnp.sum(prob_grad * probs_full, -1, keepdims=True))
    score_grad = score_grad.astype(jnp.bfloat16)
    query_grad = jnp.einsum(
        "ghqk,gkhe->gqhe", score_grad, key_rows, preferred_element_type=jnp.float32
    )
    query_grad = (query_grad * head_scale).astype(jnp.bfloat16).reshape(row_count, model_width)
    key_grad = jnp.einsum(
        "ghqk,gqhe->gkhe", score_grad, queries, preferred_element_type=jnp.float32
    )
    key_grad = (key_grad * head_scale).astype(jnp.bfloat16).reshape(row_count, model_width)
    grad_query = dot_left_t(tokens, query_grad)
    grad_key = dot_left_t(tokens, key_grad)
    grad_value = dot_left_t(tokens, value_grad)
    grad_query_shift = jnp.sum(query_grad.astype(jnp.float32), 0)
    grad_value_shift = jnp.sum(value_grad.astype(jnp.float32), 0)
    token_grad = (
        first_grad
        + dot_right_t(query_grad, query_full)
        + dot_right_t(key_grad, key_full)
        + dot_right_t(value_grad, value_full)
    )
    input_grad = token_grad.reshape(hidden_in.shape)

    small_grad = small_pack(
        layout,
        [
            v.reshape(count, -1)
            for v in (
                grad_query_shift,
                grad_value_shift,
                grad_proj_shift,
                grad_gain_one,
                grad_shift_one,
                grad_outer_shift,
                grad_gain_two,
                grad_shift_two,
                grad_pool_shift,
                grad_inner_shift,
            )
        ],
    )
    partial_sums = [
        grad_query,
        grad_key,
        grad_value,
        grad_proj,
        grad_pool,
        grad_inner,
        grad_outer,
    ]
    parts = [
        part.astype(jnp.bfloat16).reshape(layout.dims + (-1, part.shape[1]))
        for part in partial_sums
    ]
    parts.append(small_grad.reshape(layout.dims + small_grad.shape[1:]))
    plan = weave(cut(5, 0, inner_width, 4), cut(6, 1, model_width, 3))
    plan += [(3, 1, None), (4, 0, None), (0, 1, None), (1, 0, None), (2, 1, None), (7, 0, None)]
    sums = scatter_all(layout, parts, tuple(plan), 2)
    small_sum = sums[7].reshape(-1)
    narrow = []
    at = 0
    for v in vectors:
        narrow.append(small_sum[at : at + v.shape[0]])
        at += v.shape[0]
    (
        sum_query_shift,
        sum_value_shift,
        sum_proj_shift,
        sum_gain_one,
        sum_shift_one,
        sum_outer_shift,
        sum_gain_two,
        sum_shift_two,
        sum_pool_shift,
        sum_inner_shift,
    ) = narrow
    return (
        block_out,
        input_grad,
        sums[0],
        sums[1],
        sums[2],
        sums[3],
        sum_query_shift,
        sum_value_shift,
        sum_proj_shift,
        sum_gain_one,
        sum_shift_one,
        sums[5],
        sum_inner_shift,
        sums[6],
        sum_outer_shift,
        sum_gain_two,
        sum_shift_two,
        sums[4],
        sum_pool_shift,
    )


def solution(mesh):
    rows = P(("dp", "fsdp"), None)
    vector = P(("dp", "fsdp"))
    sentences = P(None, None, ("dp", "fsdp"), None, None)
    placed = (
        (sentences, P(None, None, ("dp", "fsdp")), P(), P(), sentences)
        + (rows,) * 4
        + (vector,) * 5
        + (rows, vector, rows)
        + (vector,) * 3
        + (rows, vector)
    )
    return jax.shard_map(
        functools.partial(on_device, Layout(mesh.shape)),
        mesh=mesh,
        in_specs=placed,
        out_specs=(sentences, sentences)
        + (rows,) * 4
        + (vector,) * 5
        + (rows, vector, rows)
        + (vector,) * 3
        + (rows, vector),
        check_vma=False,
    )
```

```python
import functools

import jax
import jax.numpy as jnp
from jax import lax
from jax.experimental import pallas as pl
from jax.experimental.pallas import tpu as pltpu
from jax.sharding import PartitionSpec as P

HEAD_DIM = 64


LN_EPS = 1e-06
UNIT_EPS = 1e-06
SIM_SCALE = 10.0
MARGIN = 0.3
MASKED = -1e30
MIB = 1024 * 1024


MESH_ID = pl.DeviceIdType.MESH
AXES = ("dp", "fsdp")


class Layout:
    def __init__(self, mesh_shape):
        slow, fast = mesh_shape["dp"], mesh_shape["fsdp"]
        self.slow, self.count = slow, slow * fast
        if slow == 8:
            self.dims = (2, 2, 2, fast)
            self.orders = ((3, 1, 0, 2), (3, 0, 1, 2))
        else:
            self.dims = (slow, fast)
            self.orders = ((1, 0), (1, 0))
        self.sends = sum(size - 1 for size in self.dims)

    def own(self):
        digits = [lax.axis_index("fsdp")]
        rest = lax.axis_index("dp")
        for size in self.dims[-2::-1]:
            digits.insert(0, rest % size)
            rest = rest // size
        return digits

    def device(self, digits):
        slow = digits[0]
        for size, digit in zip(self.dims[1:-1], digits[1:-1]):
            slow = slow * size + digit
        return (slow, digits[-1])

    def shifted(self, own, dim, step):
        size = self.dims[dim]
        out = list(own)
        out[dim] = (own[dim] + step) % size
        return out

    def first_slot(self, order, stage):
        return sum(self.dims[dim] - 1 for dim in order[:stage])

    def greet(self, own):
        barrier = pltpu.get_barrier_semaphore()
        for dim, size in enumerate(self.dims):
            for step in range(1, size):
                pl.semaphore_signal(
                    barrier,
                    inc=1,
                    device_id=self.device(self.shifted(own, dim, step)),
                    device_id_type=MESH_ID,
                )
        pl.semaphore_wait(barrier, self.sends)


class GatherJob:
    def __init__(self, layout, own, order, shard, full, sems, columns=None):
        self.layout, self.own, self.order = layout, own, order
        self.shard, self.full, self.columns = shard, full, columns
        self.send_sems, self.recv_sems, self.local_sem = sems

    def block(self, digits, done):
        index = tuple(
            slice(None) if dim in done else digits[dim] for dim in range(len(self.layout.dims))
        )
        if self.columns is not None:
            index = index + (slice(None), pl.ds(*self.columns))
        return self.full.at[index]

    def piece(self):
        if self.columns is not None:
            return self.shard.at[:, pl.ds(*self.columns)]
        return self.shard

    def copies(self, stage, sending):
        dim, done = self.order[stage], self.order[:stage]
        base = self.layout.first_slot(self.order, stage)
        out = []
        for step in range(1, self.layout.dims[dim]):
            slot = base + step - 1
            other = self.layout.shifted(self.own, dim, step if sending else -step)
            target = self.block(self.own if sending else other, done)
            source = self.piece() if sending and stage == 0 else target
            out.append(
                pltpu.make_async_remote_copy(
                    src_ref=source,
                    dst_ref=target,
                    send_sem=self.send_sems.at[slot],
                    recv_sem=self.recv_sems.at[slot],
                    device_id=self.layout.device(other),
                    device_id_type=MESH_ID,
                )
            )
        return out

    def local(self):
        return pltpu.make_async_copy(self.piece(), self.block(self.own, ()), self.local_sem)

    def advance(self, stage):
        if stage == 0:
            self.local().start()
        else:
            for copy in self.copies(stage - 1, False):
                copy.wait_recv()
            if stage == 1:
                self.local().wait()
        if stage < len(self.order):
            for copy in self.copies(stage, True):
                copy.start()

    def finish(self):
        for stage in range(len(self.order)):
            for copy in self.copies(stage, True):
                copy.wait_send()


def run_rounds(jobs, stages, width=2):
    rounds = []
    last = stages + (len(jobs) - 1) // width
    for step in range(last + 1):
        todo = []
        for index, job in enumerate(jobs):
            stage = step - index // width
            if 0 <= stage <= stages:
                todo.append((job, stage))
        rounds.append(todo)
    return rounds


class ScatterJob:
    def __init__(self, layout, own, order, part, sums, lands, result, sems, columns=None):
        self.layout, self.own, self.order = layout, own, order
        self.part, self.sums, self.lands, self.result = part, sums, lands, result
        self.send_sems, self.recv_sems, self.local_sem = sems
        self.columns = columns

    def tail(self):
        if self.columns is not None:
            return (slice(None), pl.ds(*self.columns))
        return ()

    def local(self):
        dim = self.order[0]
        index = [slice(None)] * len(self.layout.dims)
        index[dim] = self.own[dim]
        return pltpu.make_async_copy(
            self.part.at[tuple(index) + self.tail()], self.sums[0], self.local_sem
        )

    def copies(self, stage):
        dim = self.order[stage]
        base = self.layout.first_slot(self.order, stage)
        left = [d for d in range(len(self.layout.dims)) if d not in self.order[:stage]]
        out = []
        for step in range(1, self.layout.dims[dim]):
            slot = base + step - 1
            there = self.layout.shifted(self.own, dim, step)
            index = tuple(there[dim] if d == dim else slice(None) for d in left)
            if stage == 0:
                source = self.part.at[index + self.tail()]
            else:
                source = self.sums[stage - 1].at[index]
            out.append(
                pltpu.make_async_remote_copy(
                    src_ref=source,
                    dst_ref=self.lands[stage].at[step - 1],
                    send_sem=self.send_sems.at[slot],
                    recv_sem=self.recv_sems.at[slot],
                    device_id=self.layout.device(there),
                    device_id_type=MESH_ID,
                )
            )
        return out

    def add(self, stage):
        dim = self.order[stage]
        left = [d for d in range(len(self.layout.dims)) if d not in self.order[:stage]]
        rest = [d for d in left if d != dim]
        sizes = [self.layout.dims[d] for d in rest]
        total = 1
        for size in sizes:
            total *= size

        def body(flat):
            digits = []
            for size in reversed(sizes):
                digits.insert(0, flat % size)
                flat = flat // size
            if stage == 0:
                own_index = tuple(digits)
                value = self.sums[0][own_index].astype(jnp.float32)
            else:
                where = dict(zip(rest, digits))
                where[dim] = self.own[dim]
                value = self.sums[stage - 1][tuple(where[d] for d in left)].astype(jnp.float32)
            for step in range(1, self.layout.dims[dim]):
                value = value + self.lands[stage][(step - 1,) + tuple(digits)].astype(jnp.float32)
            if rest:
                target = self.sums[stage]
                target[tuple(digits)] = value.astype(target.dtype)
            elif self.columns is not None:
                self.result[:, pl.ds(*self.columns)] = value
            else:
                self.result[...] = value

        if total == 1:
            body(0)
        else:
            pl.loop(0, total)(body)

    def advance(self, stage):
        if stage == 0:
            self.local().start()
        else:
            for copy in self.copies(stage - 1):
                copy.wait_recv()
            if stage == 1:
                self.local().wait()
            self.add(stage - 1)
        if stage < len(self.order):
            for copy in self.copies(stage):
                copy.start()

    def finish(self):
        for stage in range(len(self.order)):
            for copy in self.copies(stage):
                copy.wait_send()


def scatter_buffers(layout, order, rows, columns, dtype):
    sums, lands = [], []
    for stage, dim in enumerate(order):
        rest = tuple(
            size for d, size in enumerate(layout.dims) if d not in order[: stage + 1]
        )
        lands.append(pltpu.VMEM((layout.dims[dim] - 1,) + rest + (rows, columns), dtype))
        if stage < len(order) - 1:
            sums.append(pltpu.VMEM(rest + (rows, columns), dtype))
    return sums + lands


def gather_kernel(layout, plan, count, *refs):
    shards, fulls = refs[:count], refs[count : 2 * count]
    send_sems, recv_sems, local_sems = refs[2 * count :]
    own = layout.own()
    layout.greet(own)
    jobs = [
        GatherJob(
            layout,
            own,
            layout.orders[way],
            shards[which],
            fulls[which],
            (send_sems.at[at], recv_sems.at[at], local_sems.at[at]),
            columns,
        )
        for at, (which, way, columns) in enumerate(plan)
    ]
    for todo in run_rounds(jobs, len(layout.dims)):
        for job, stage in todo:
            job.advance(stage)
    for job in jobs:
        job.finish()


def gather_all(layout, arrays, plan, collective_id):
    anywhere = pl.BlockSpec(memory_space=pl.ANY)
    return pl.pallas_call(
        functools.partial(gather_kernel, layout, plan, len(arrays)),
        out_shape=[jax.ShapeDtypeStruct(layout.dims + a.shape, a.dtype) for a in arrays],
        in_specs=[anywhere] * len(arrays),
        out_specs=[anywhere] * len(arrays),
        scratch_shapes=[
            pltpu.SemaphoreType.DMA((len(plan), layout.sends)),
            pltpu.SemaphoreType.DMA((len(plan), layout.sends)),
            pltpu.SemaphoreType.DMA((len(plan),)),
        ],
        compiler_params=pltpu.CompilerParams(
            collective_id=collective_id, has_side_effects=True, vmem_limit_bytes=16 * MIB
        ),
    )(*arrays)


def scatter_kernel(layout, plan, count, buffers, *refs):
    parts, results = refs[:count], refs[count : 2 * count]
    scratch, (send_sems, recv_sems, local_sems) = refs[2 * count : -3], refs[-3:]
    own = layout.own()
    layout.greet(own)
    jobs = []
    stages = len(layout.dims)
    for at, (which, way, columns) in enumerate(plan):
        mine = scratch[at * buffers : (at + 1) * buffers]
        jobs.append(
            ScatterJob(
                layout,
                own,
                layout.orders[way][::-1],
                parts[which],
                mine[: stages - 1],
                mine[stages - 1 :],
                results[which],
                (send_sems.at[at], recv_sems.at[at], local_sems.at[at]),
                columns,
            )
        )
    for todo in run_rounds(jobs, stages):
        for job, stage in todo:
            job.advance(stage)
    for job in jobs:
        job.finish()


def scatter_all(layout, arrays, plan, collective_id):
    stages = len(layout.dims)
    scratch = []
    for which, way, columns in plan:
        rows, width = arrays[which].shape[-2:]
        width = width if columns is None else columns[1]
        scratch += scatter_buffers(
            layout, layout.orders[way][::-1], rows, width, arrays[which].dtype
        )
    return pl.pallas_call(
        functools.partial(scatter_kernel, layout, plan, len(arrays), 2 * stages - 1),
        out_shape=[jax.ShapeDtypeStruct(a.shape[-2:], jnp.float32) for a in arrays],
        in_specs=[pl.BlockSpec(memory_space=pl.ANY)] * len(arrays),
        out_specs=[pl.BlockSpec(memory_space=pltpu.VMEM)] * len(arrays),
        scratch_shapes=scratch
        + [
            pltpu.SemaphoreType.DMA((len(plan), layout.sends)),
            pltpu.SemaphoreType.DMA((len(plan), layout.sends)),
            pltpu.SemaphoreType.DMA((len(plan),)),
        ],
        compiler_params=pltpu.CompilerParams(
            collective_id=collective_id, has_side_effects=True, vmem_limit_bytes=60 * MIB
        ),
    )(*arrays)


def cut(which, way, width, pieces):
    if width % (pieces * 128):
        return [(which, way, None)]
    step = width // pieces
    return [(which, way, (at * step, step)) for at in range(pieces)]


def weave(first, second):
    out = []
    for at in range(max(len(first), len(second))):
        out += first[at : at + 1] + second[at : at + 1]
    return out


def small_pack(layout, vectors):
    flat = jnp.concatenate([v.astype(jnp.float32).reshape(v.shape[0], -1) for v in vectors], 1)
    width = -(-flat.shape[1] // 1024) * 1024
    flat = jnp.pad(flat, ((0, 0), (0, width - flat.shape[1])))
    return flat.reshape(flat.shape[0], width // 128, 128)


def dot_plain(first_mat, second_mat):
    return jnp.dot(first_mat, second_mat, preferred_element_type=jnp.float32)


def dot_left_t(first_mat, second_mat):
    return lax.dot_general(
        first_mat, second_mat, (((0,), (0,)), ((), ())), preferred_element_type=jnp.float32
    )


def dot_right_t(first_mat, second_mat):
    return lax.dot_general(
        first_mat, second_mat, (((1,), (1,)), ((), ())), preferred_element_type=jnp.float32
    )


def row_mean(value):
    return jnp.sum(value, -1, keepdims=True) * (1.0 / value.shape[-1])


def norm_parts(row_data):
    centred = row_data - row_mean(row_data)
    inverse = lax.rsqrt(row_mean(centred * centred) + LN_EPS)
    return centred * inverse, inverse


def norm_backward(upstream, normed, inverse, gain_vec):
    scaled = upstream * gain_vec
    return inverse * (scaled - row_mean(scaled) - normed * row_mean(scaled * normed))


def column_sum(value):
    return jnp.sum(value, 0, keepdims=True)


def gelu_and_slope(inner_act):
    below = 0.5 * (1.0 + lax.erf(inner_act * 0.7071067811865476))
    bell = jnp.exp(-0.5 * inner_act * inner_act) * 0.3989422804014327
    return inner_act * below, below + inner_act * bell


GROUP = 4
SPAN = GROUP * HEAD_DIM


def spread(rows, diag):
    return jnp.concatenate([rows] * GROUP, 0) * diag


def fold(square, seq_len):
    lane = lax.broadcasted_iota(jnp.int32, (seq_len, square.shape[1]), 1)
    out = square[:seq_len]
    for head in range(1, GROUP):
        block = square[head * seq_len : (head + 1) * seq_len]
        out = jnp.where(lane >= head * HEAD_DIM, block, out)
    return out


def probabilities(keys, wide_queries, length):
    scores = dot_right_t(keys, wide_queries) * HEAD_DIM ** (-0.5)
    at = lax.broadcasted_iota(jnp.int32, scores.shape, 0)
    scores = jnp.where(at < length, scores, MASKED)
    raised = jnp.exp(scores - jnp.max(scores, 0, keepdims=True))
    return raised * (1.0 / jnp.sum(raised, 0, keepdims=True))


def attend_kernel(
    seq_len,
    lengths_ref,
    x_ref,
    query_w,
    key_w,
    value_w,
    proj_w,
    vec_ref,
    diag_ref,
    q_ref,
    k_ref,
    v_ref,
    mix_ref,
    sum_ref,
    cls_ref,
):
    rows, width = x_ref.shape
    held = rows // seq_len
    first = pl.program_id(0) * held
    x = x_ref[...]
    q_ref[...] = (dot_plain(x, query_w[...]) + vec_ref[0:1, :]).astype(jnp.bfloat16)
    k_ref[...] = dot_plain(x, key_w[...]).astype(jnp.bfloat16)
    v_ref[...] = (dot_plain(x, value_w[...]) + vec_ref[1:2, :]).astype(jnp.bfloat16)
    diag = diag_ref[...]

    def sentence(at):
        length = lengths_ref[first + at]
        here = pl.ds(pl.multiple_of(at * seq_len, seq_len), seq_len)
        for low in range(0, width, SPAN):
            cols = pl.ds(low, SPAN)
            wide = spread(q_ref[here, cols], diag)
            probs = probabilities(k_ref[here, cols], wide, length).astype(jnp.bfloat16)
            mixed = fold(dot_left_t(probs, v_ref[here, cols]), seq_len)
            mix_ref[here, cols] = mixed.astype(jnp.bfloat16)

    pl.loop(0, held)(sentence)
    total = x.astype(jnp.float32) + dot_plain(mix_ref[...], proj_w[...]) + vec_ref[2:3, :]
    sum_ref[...] = total
    for at in range(held):
        cls_ref[0, at : at + 1, :] = total[at * seq_len : at * seq_len + 1]


def whole(shape):
    return pl.BlockSpec(shape, lambda *_: (0,) * len(shape), pipeline_mode=pl.Buffered(1))


def attend(x, lengths, weights, vec, diag, seq_len, rows):
    total, width = x.shape
    steps = total // rows
    held = rows // seq_len
    block = pl.BlockSpec((rows, width), lambda i: (i, 0))
    narrow = jax.ShapeDtypeStruct((total, width), jnp.bfloat16)
    return pl.pallas_call(
        functools.partial(attend_kernel, seq_len),
        grid=(steps,),
        out_shape=[
            narrow,
            narrow,
            narrow,
            narrow,
            jax.ShapeDtypeStruct((total, width), jnp.float32),
            jax.ShapeDtypeStruct((steps, held, width), jnp.float32),
        ],
        in_specs=[pl.BlockSpec(memory_space=pltpu.SMEM), block]
        + [whole(w.shape) for w in weights]
        + [whole(vec.shape), whole(diag.shape)],
        out_specs=[block] * 5 + [pl.BlockSpec((1, held, width), lambda i: (i, 0, 0))],
        compiler_params=pltpu.CompilerParams(vmem_limit_bytes=60 * MIB),
    )(lengths, x, *weights, vec, diag)


def feed_kernel(
    seq_len,
    blocks,
    pieces,
    sum_ref,
    tok_ref,
    cls_ref,
    inner_w,
    outer_w,
    vec_ref,
    bias_ref,
    out_ref,
    back_ref,
    inner_grad,
    outer_grad,
    vec_grad,
    bias_grad,
    slope,
    active,
    inner_b,
    hidden_b,
    second_b,
):
    step = pl.program_id(0)
    rows, width = sum_ref.shape
    piece = active.shape[2]

    @pl.when(step == 0)
    def _():
        vec_grad[...] = jnp.zeros_like(vec_grad)
        bias_grad[...] = jnp.zeros_like(bias_grad)

    @pl.when(step < blocks)
    def _():
        here = pl.ds(pl.multiple_of(step * rows, rows), rows)
        gain_one, shift_one = vec_ref[3:4, :], vec_ref[4:5, :]
        gain_two, shift_two = vec_ref[6:7, :], vec_ref[7:8, :]
        normed_one, inverse_one = norm_parts(sum_ref[...])
        hidden = normed_one * gain_one + shift_one
        narrow = hidden.astype(jnp.bfloat16)
        hidden_b[here, :] = narrow
        second_sum = hidden + vec_ref[5:6, :]
        for at in range(pieces):
            cols = slice(at * piece, (at + 1) * piece)
            value, steep = gelu_and_slope(dot_plain(narrow, inner_w[:, cols]) + bias_ref[:, cols])
            value = value.astype(jnp.bfloat16)
            slope[at] = steep
            active[at, here, :] = value
            second_sum = second_sum + dot_plain(value, outer_w[cols, :])
        normed_two, inverse_two = norm_parts(second_sum)
        out_ref[...] = (normed_two * gain_two + shift_two).astype(jnp.bfloat16)
        grad = tok_ref[...].astype(jnp.float32).reshape(rows // seq_len, seq_len, width)
        place = lax.broadcasted_iota(jnp.int32, grad.shape, 1)
        extra = cls_ref[...].reshape(rows // seq_len, 1, width)
        grad = (grad + jnp.where(place == 0, extra, 0.0)).reshape(rows, width)
        vec_grad[6:7, :] += column_sum(grad * normed_two)
        vec_grad[7:8, :] += column_sum(grad)
        second = norm_backward(grad, normed_two, inverse_two, gain_two)
        vec_grad[5:6, :] += column_sum(second)
        narrow_two = second.astype(jnp.bfloat16)
        second_b[here, :] = narrow_two
        hidden_grad = second
        for at in range(pieces):
            cols = slice(at * piece, (at + 1) * piece)
            inner = dot_right_t(narrow_two, outer_w[cols, :]) * slope[at]
            bias_grad[:, cols] += column_sum(inner)
            inner = inner.astype(jnp.bfloat16)
            inner_b[at, here, :] = inner
            hidden_grad = hidden_grad + dot_right_t(inner, inner_w[:, cols])
        vec_grad[3:4, :] += column_sum(hidden_grad * normed_one)
        vec_grad[4:5, :] += column_sum(hidden_grad)
        first = norm_backward(hidden_grad, normed_one, inverse_one, gain_one)
        vec_grad[2:3, :] += column_sum(first)
        back_ref[...] = first

    @pl.when(step >= blocks)
    def _():
        at = step - blocks
        outer_grad[...] = dot_left_t(active[at], second_b[...]).astype(jnp.bfloat16)
        inner_grad[...] = dot_left_t(hidden_b[...], inner_b[at]).astype(jnp.bfloat16)


def feed(first_sum, tokens_grad, cls_grad, inner_w, outer_w, vec, bias, seq_len, rows, piece):
    total, width = first_sum.shape
    wide = inner_w.shape[1]
    blocks, pieces = total // rows, wide // piece
    held = rows // seq_len
    cls_grad = cls_grad.reshape(blocks, held, width)
    block = pl.BlockSpec((rows, width), lambda i: (jnp.minimum(i, blocks - 1), 0))
    return pl.pallas_call(
        functools.partial(feed_kernel, seq_len, blocks, pieces),
        grid=(blocks + pieces,),
        out_shape=[
            jax.ShapeDtypeStruct((total, width), jnp.bfloat16),
            jax.ShapeDtypeStruct((total, width), jnp.float32),
            jax.ShapeDtypeStruct(inner_w.shape, jnp.bfloat16),
            jax.ShapeDtypeStruct(outer_w.shape, jnp.bfloat16),
            jax.ShapeDtypeStruct((8, width), jnp.float32),
            jax.ShapeDtypeStruct((1, wide), jnp.float32),
        ],
        in_specs=[
            block,
            block,
            pl.BlockSpec((1, held, width), lambda i: (jnp.minimum(i, blocks - 1), 0, 0)),
            whole(inner_w.shape),
            whole(outer_w.shape),
            whole(vec.shape),
            whole(bias.shape),
        ],
        out_specs=[
            block,
            block,
            pl.BlockSpec((width, piece), lambda i: (0, jnp.maximum(i - blocks, 0))),
            pl.BlockSpec((piece, width), lambda i: (jnp.maximum(i - blocks, 0), 0)),
            pl.BlockSpec((8, width), lambda i: (0, 0)),
            pl.BlockSpec((1, wide), lambda i: (0, 0)),
        ],
        scratch_shapes=[
            pltpu.VMEM((pieces, rows, piece), jnp.float32),
            pltpu.VMEM((pieces, total, piece), jnp.bfloat16),
            pltpu.VMEM((pieces, total, piece), jnp.bfloat16),
            pltpu.VMEM((total, width), jnp.bfloat16),
            pltpu.VMEM((total, width), jnp.bfloat16),
        ],
        compiler_params=pltpu.CompilerParams(vmem_limit_bytes=62 * MIB),
    )(first_sum, tokens_grad, cls_grad, inner_w, outer_w, vec, bias)


def back_kernel(
    seq_len,
    blocks,
    lengths_ref,
    x_ref,
    q_ref,
    k_ref,
    v_ref,
    mix_ref,
    first_ref,
    query_w,
    key_w,
    value_w,
    proj_w,
    diag_ref,
    in_ref,
    query_g,
    key_g,
    value_g,
    proj_g,
    vec_grad,
    x_all,
    mix_all,
    first_all,
    dq_all,
    dk_all,
    dv_all,
    dmix,
):
    step = pl.program_id(0)
    rows, width = x_ref.shape
    held = rows // seq_len
    scale = HEAD_DIM ** (-0.5)

    @pl.when(step == 0)
    def _():
        vec_grad[...] = jnp.zeros_like(vec_grad)

    @pl.when(step < blocks)
    def _():
        here = pl.ds(pl.multiple_of(step * rows, rows), rows)
        first = first_ref[...]
        narrow = first.astype(jnp.bfloat16)
        first_all[here, :] = narrow
        x_all[here, :] = x_ref[...]
        mix_all[here, :] = mix_ref[...]
        dmix[...] = dot_right_t(narrow, proj_w[...]).astype(jnp.bfloat16)
        diag = diag_ref[...]

        def sentence(at):
            length = lengths_ref[step * held + at]
            near = pl.ds(pl.multiple_of(at * seq_len, seq_len), seq_len)
            far = pl.ds(pl.multiple_of(step * rows + at * seq_len, seq_len), seq_len)
            for low in range(0, width, SPAN):
                cols = pl.ds(low, SPAN)
                keys = k_ref[near, cols]
                wide = spread(q_ref[near, cols], diag)
                wide_grad = spread(dmix[near, cols], diag)
                probs = probabilities(keys, wide, length)
                prob_grad = dot_right_t(v_ref[near, cols], wide_grad)
                dv_all[far, cols] = dot_plain(probs.astype(jnp.bfloat16), wide_grad).astype(
                    jnp.bfloat16
                )
                score_grad = probs * (prob_grad - column_sum(prob_grad * probs))
                score_grad = score_grad.astype(jnp.bfloat16)
                dk_all[far, cols] = (dot_plain(score_grad, wide) * scale).astype(jnp.bfloat16)
                dq_all[far, cols] = (fold(dot_left_t(score_grad, keys), seq_len) * scale).astype(
                    jnp.bfloat16
                )

        pl.loop(0, held)(sentence)
        dq, dk, dv = dq_all[here, :], dk_all[here, :], dv_all[here, :]
        vec_grad[0:1, :] += column_sum(dq.astype(jnp.float32))
        vec_grad[1:2, :] += column_sum(dv.astype(jnp.float32))
        in_ref[...] = (
            first
            + dot_right_t(dq, query_w[...])
            + dot_right_t(dk, key_w[...])
            + dot_right_t(dv, value_w[...])
        )

    for at, (left, right, target) in enumerate(
        (
            (mix_all, first_all, proj_g),
            (x_all, dq_all, query_g),
            (x_all, dk_all, key_g),
            (x_all, dv_all, value_g),
        )
    ):

        @pl.when(step == blocks + at)
        def _():
            target[...] = dot_left_t(left[...], right[...]).astype(jnp.bfloat16)


def back(x, lengths, saved, first_grad, weights, diag, seq_len, rows):
    total, width = x.shape
    blocks = total // rows
    block = pl.BlockSpec((rows, width), lambda i: (jnp.minimum(i, blocks - 1), 0))
    square = jax.ShapeDtypeStruct((width, width), jnp.bfloat16)
    return pl.pallas_call(
        functools.partial(back_kernel, seq_len, blocks),
        grid=(blocks + 4,),
        out_shape=[jax.ShapeDtypeStruct((total, width), jnp.float32)]
        + [square] * 4
        + [jax.ShapeDtypeStruct((8, width), jnp.float32)],
        in_specs=[pl.BlockSpec(memory_space=pltpu.SMEM)]
        + [block] * 6
        + [whole(w.shape) for w in weights]
        + [whole(diag.shape)],
        out_specs=[block]
        + [pl.BlockSpec((width, width), lambda i: (0, 0))] * 4
        + [pl.BlockSpec((8, width), lambda i: (0, 0))],
        scratch_shapes=[pltpu.VMEM((total, width), jnp.bfloat16)] * 6
        + [pltpu.VMEM((rows, width), jnp.bfloat16)],
        compiler_params=pltpu.CompilerParams(vmem_limit_bytes=60 * MIB),
    )(lengths, x, *saved, first_grad, *weights, diag)


def rank_kernel(
    layout,
    micros,
    node_dev,
    steps,
    sum_ref,
    inner_w,
    outer_w,
    pool_w,
    vec_ref,
    bias_ref,
    node_ref,
    cls_grad,
    pool_grad,
    shift_grad,
    hidden,
    total,
    mine,
    units,
    node_cols,
    totals,
    send_sems,
    recv_sems,
    local_sem,
):
    step = pl.program_id(0)
    sentences, width = sum_ref.shape
    own = layout.own()

    @pl.when(step == 0)
    def _():
        layout.greet(own)
        normed, _ = norm_parts(sum_ref[...])
        start = normed * vec_ref[3:4, :] + vec_ref[4:5, :]
        hidden[...] = start.astype(jnp.bfloat16)
        total[...] = start + vec_ref[5:6, :]
        node_cols[...] = node_ref[...].T

    value, _ = gelu_and_slope(dot_plain(hidden[...], inner_w[...]) + bias_ref[...])
    total[...] += dot_plain(value.astype(jnp.bfloat16), outer_w[...])

    @pl.when(step == steps - 1)
    def _():
        normed, _ = norm_parts(total[...])
        cls_rows = (normed * vec_ref[6:7, :] + vec_ref[7:8, :]).astype(jnp.bfloat16)
        pooled = jnp.tanh(dot_plain(cls_rows, pool_w[...]) + vec_ref[8:9, :])
        scale_inv = lax.rsqrt(jnp.sum(pooled * pooled, -1, keepdims=True) + UNIT_EPS)
        unit = pooled * scale_inv
        mine[...] = unit.astype(jnp.bfloat16)
        job = GatherJob(
            layout, own, layout.orders[0], mine, units, (send_sems, recv_sems, local_sem)
        )
        for stage in range(len(layout.dims) + 1):
            job.advance(stage)
        job.finish()

        device = own[0]
        for size, digit in zip(layout.dims[1:], own[1:]):
            device = device * size + digit
        at_home = pl.ds(pl.multiple_of(device * node_dev, node_dev), node_dev)
        count = layout.count * node_dev
        band = min(count, 512)
        every = units[...].reshape(layout.count, sentences, width)
        grads = []

        def scored(similar, tongue, place, side, tongue_row, place_row, side_row):
            across = side != side_row
            include = across & (tongue == tongue_row)
            positive = jnp.where(across & (place == place_row), 1.0, 0.0)
            return (
                jnp.where(include, SIM_SCALE * similar - SIM_SCALE * MARGIN * positive, MASKED),
                include,
                positive,
            )

        half = node_dev // 2

        def sides(shape, dim, offset):
            return (lax.broadcasted_iota(jnp.int32, shape, dim) + offset) // half % 2

        for micro in range(micros):
            here = slice(micro * node_dev, (micro + 1) * node_dev)
            nodes = every[:, here, :].reshape(count, width)
            tongue, place = node_cols[:, 2 * micro : 2 * micro + 1], node_cols[
                :, 2 * micro + 1 : 2 * micro + 2
            ]
            for low in range(0, count, band):
                cols = slice(low, low + band)
                similar = dot_right_t(nodes, nodes[cols])
                value, _, _ = scored(
                    similar,
                    tongue,
                    place,
                    sides((count, 1), 0, 0),
                    node_ref[2 * micro : 2 * micro + 1, cols],
                    node_ref[2 * micro + 1 : 2 * micro + 2, cols],
                    sides((1, band), 1, low),
                )
                peak = jnp.max(value, 0, keepdims=True)
                totals[:, cols] = jnp.log(column_sum(jnp.exp(value - peak))) + peak
            value, include, positive = scored(
                dot_right_t(mine[here, :], nodes),
                node_cols[at_home, 2 * micro : 2 * micro + 1],
                node_cols[at_home, 2 * micro + 1 : 2 * micro + 2],
                sides((node_dev, 1), 0, 0),
                node_ref[2 * micro : 2 * micro + 1, :],
                node_ref[2 * micro + 1 : 2 * micro + 2, :],
                sides((1, count), 1, 0),
            )
            peak = jnp.max(value, -1, keepdims=True)
            line = jnp.log(jnp.sum(jnp.exp(value - peak), -1, keepdims=True)) + peak
            grad_sim = jnp.where(
                include, jnp.exp(value - line) + jnp.exp(value - totals[...]), 0.0
            )
            grad_sim = (grad_sim - 2.0 * positive).astype(jnp.bfloat16)
            grads.append(SIM_SCALE * dot_plain(grad_sim, nodes))
        unit_grad = jnp.concatenate(grads, 0)
        pooled_grad = scale_inv * (
            unit_grad - unit * jnp.sum(unit_grad * unit, -1, keepdims=True)
        )
        pre_grad = pooled_grad * (1.0 - pooled * pooled)
        narrow = pre_grad.astype(jnp.bfloat16)
        pool_grad[...] = dot_left_t(cls_rows, narrow).astype(jnp.bfloat16)
        shift_grad[...] = column_sum(pre_grad)
        cls_grad[...] = dot_right_t(narrow, pool_w[...])


def rank(layout, cls_sum, inner_w, outer_w, pool_w, vec, bias, nodes, micros, piece, collective_id):
    sentences, width = cls_sum.shape
    wide = inner_w.shape[1]
    steps = wide // piece
    node_dev = sentences // micros
    return pl.pallas_call(
        functools.partial(rank_kernel, layout, micros, node_dev, steps),
        grid=(steps,),
        out_shape=[
            jax.ShapeDtypeStruct((sentences, width), jnp.float32),
            jax.ShapeDtypeStruct((width, width), jnp.bfloat16),
            jax.ShapeDtypeStruct((1, width), jnp.float32),
        ],
        in_specs=[
            whole(cls_sum.shape),
            pl.BlockSpec((width, piece), lambda i: (0, i)),
            pl.BlockSpec((piece, width), lambda i: (i, 0)),
            whole(pool_w.shape),
            whole(vec.shape),
            pl.BlockSpec((1, piece), lambda i: (0, i)),
            whole(nodes.shape),
        ],
        out_specs=[
            pl.BlockSpec((sentences, width), lambda i: (0, 0)),
            pl.BlockSpec((width, width), lambda i: (0, 0)),
            pl.BlockSpec((1, width), lambda i: (0, 0)),
        ],
        scratch_shapes=[
            pltpu.VMEM((sentences, width), jnp.bfloat16),
            pltpu.VMEM((sentences, width), jnp.float32),
            pltpu.VMEM((sentences, width), jnp.bfloat16),
            pltpu.VMEM(layout.dims + (sentences, width), jnp.bfloat16),
            pltpu.VMEM((nodes.shape[1], nodes.shape[0]), jnp.float32),
            pltpu.VMEM((1, nodes.shape[1]), jnp.float32),
            pltpu.SemaphoreType.DMA((layout.sends,)),
            pltpu.SemaphoreType.DMA((layout.sends,)),
            pltpu.SemaphoreType.DMA,
        ],
        compiler_params=pltpu.CompilerParams(
            collective_id=collective_id, has_side_effects=True, vmem_limit_bytes=60 * MIB
        ),
    )(cls_sum, inner_w, outer_w, pool_w, vec, bias, nodes)


def on_device(
    layout,
    hidden_in,
    lengths,
    partner,
    language,
    token_cotangent,
    query_weight,
    key_weight,
    value_weight,
    attn_out_weight,
    query_bias,
    value_bias,
    attn_out_bias,
    ln1_gain,
    ln1_shift,
    in_weight,
    in_bias,
    out_weight,
    out_bias,
    ln2_gain,
    ln2_shift,
    pool_weight,
    pool_bias,
):
    micro_count, sides, pair_dev, seq_len, model_width = hidden_in.shape
    inner_width = in_weight.shape[1]
    count = layout.count
    node_dev = sides * pair_dev
    sent_count = micro_count * node_dev
    row_count = sent_count * seq_len
    pair_count = partner.shape[1]

    vectors = (
        query_bias,
        value_bias,
        attn_out_bias,
        ln1_gain,
        ln1_shift,
        out_bias,
        ln2_gain,
        ln2_shift,
        pool_bias,
        in_bias,
    )
    small = small_pack(layout, [v[None] for v in vectors])[0]
    arrays = [
        query_weight,
        key_weight,
        value_weight,
        attn_out_weight,
        small,
        pool_weight,
        in_weight,
        out_weight,
    ]
    plan = [(4, 0, None), (0, 1, None), (1, 0, None), (2, 1, None), (3, 0, None), (5, 1, None)]
    plan += weave(cut(6, 0, inner_width, 4), cut(7, 1, model_width, 3))
    gathered = gather_all(layout, arrays, tuple(plan), 0)
    query_full, key_full, value_full, proj_full, small_full, pool_full, inner_full, outer_full = [
        full.reshape((count * array.shape[0],) + array.shape[1:])
        for full, array in zip(gathered, arrays)
    ]
    small_rows = small_full.reshape(count, -1)
    share = query_bias.shape[0]
    rows_of = len(vectors) - 1
    vec = small_rows[:, : rows_of * share].reshape(count, rows_of, share)
    vec = jnp.moveaxis(vec, 1, 0).reshape(rows_of, model_width)
    vec = jnp.pad(vec, ((0, 16 - rows_of), (0, 0)))
    bias = small_rows[:, rows_of * share : rows_of * share + in_bias.shape[0]]
    bias = bias.reshape(1, inner_width)

    pair_ids = jnp.arange(pair_count, dtype=jnp.int32)
    hit = partner[:, :, None] == pair_ids[None, None, :]
    target_language = jnp.sum(jnp.where(hit, language[:, :, None], 0), 1)

    def split(value):
        return value.reshape(micro_count, count, 1, pair_dev)

    node_rows = jnp.stack(
        [
            jnp.concatenate([split(language), split(target_language)], 2),
            jnp.concatenate(
                [split(partner), split(jnp.broadcast_to(pair_ids, partner.shape))], 2
            ),
        ],
        1,
    )
    node_rows = node_rows.reshape(2 * micro_count, count * node_dev).astype(jnp.float32)
    node_rows = jnp.pad(node_rows, ((0, -2 * micro_count % 8), (0, 0)))
    block_at = jnp.arange(SPAN) // HEAD_DIM
    diag = (block_at[:, None] == block_at[None, :]).astype(jnp.bfloat16)

    x = hidden_in.reshape(row_count, model_width)
    sent_lengths = lengths.reshape(sent_count)
    weights = (query_full, key_full, value_full, proj_full)
    *saved, first_sum, cls_sum = attend(x, sent_lengths, weights, vec, diag, seq_len, 512)
    cls_grad, grad_pool, grad_pool_shift = rank(
        layout,
        cls_sum.reshape(sent_count, model_width),
        inner_full,
        outer_full,
        pool_full,
        vec,
        bias,
        node_rows,
        micro_count,
        384,
        1,
    )
    block_out, first_grad, grad_inner, grad_outer, vec_grad, grad_bias = feed(
        first_sum,
        token_cotangent.reshape(row_count, model_width),
        cls_grad,
        inner_full,
        outer_full,
        vec,
        bias,
        seq_len,
        256,
        384,
    )
    input_grad, grad_query, grad_key, grad_value, grad_proj, vec_grad_two = back(
        x, sent_lengths, saved, first_grad, weights, diag, seq_len, 256
    )
    block_out = block_out.reshape(hidden_in.shape)
    input_grad = input_grad.reshape(hidden_in.shape)
    vec_grad = jnp.concatenate([vec_grad_two[:2], vec_grad[2:8], grad_pool_shift], 0)
    vec_grad = jnp.moveaxis(vec_grad.reshape(rows_of, count, share), 1, 0)
    small_grad = small_pack(
        layout, [vec_grad.reshape(count, -1), grad_bias.reshape(count, -1)]
    )
    partial_sums = [
        grad_query,
        grad_key,
        grad_value,
        grad_proj,
        grad_pool,
        grad_inner,
        grad_outer,
    ]
    parts = [
        part.astype(jnp.bfloat16).reshape(layout.dims + (-1, part.shape[1]))
        for part in partial_sums
    ]
    parts.append(small_grad.reshape(layout.dims + small_grad.shape[1:]))
    plan = weave(cut(5, 0, inner_width, 4), cut(6, 1, model_width, 3))
    plan += [(3, 1, None), (4, 0, None), (0, 1, None), (1, 0, None), (2, 1, None), (7, 0, None)]
    sums = scatter_all(layout, parts, tuple(plan), 2)
    small_sum = sums[7].reshape(-1)
    narrow = []
    at = 0
    for v in vectors:
        narrow.append(small_sum[at : at + v.shape[0]])
        at += v.shape[0]
    (
        sum_query_shift,
        sum_value_shift,
        sum_proj_shift,
        sum_gain_one,
        sum_shift_one,
        sum_outer_shift,
        sum_gain_two,
        sum_shift_two,
        sum_pool_shift,
        sum_inner_shift,
    ) = narrow
    return (
        block_out,
        input_grad,
        sums[0],
        sums[1],
        sums[2],
        sums[3],
        sum_query_shift,
        sum_value_shift,
        sum_proj_shift,
        sum_gain_one,
        sum_shift_one,
        sums[5],
        sum_inner_shift,
        sums[6],
        sum_outer_shift,
        sum_gain_two,
        sum_shift_two,
        sums[4],
        sum_pool_shift,
    )


def solution(mesh):
    rows = P(("dp", "fsdp"), None)
    vector = P(("dp", "fsdp"))
    sentences = P(None, None, ("dp", "fsdp"), None, None)
    placed = (
        (sentences, P(None, None, ("dp", "fsdp")), P(), P(), sentences)
        + (rows,) * 4
        + (vector,) * 5
        + (rows, vector, rows)
        + (vector,) * 3
        + (rows, vector)
    )
    return jax.shard_map(
        functools.partial(on_device, Layout(mesh.shape)),
        mesh=mesh,
        in_specs=placed,
        out_specs=(sentences, sentences)
        + (rows,) * 4
        + (vector,) * 5
        + (rows, vector, rows)
        + (vector,) * 3
        + (rows, vector),
        check_vma=False,
    )
```

```python
import functools

import jax
import jax.numpy as jnp
from jax import lax
from jax.experimental import pallas as pl
from jax.experimental.pallas import tpu as pltpu
from jax.sharding import PartitionSpec as P

HEAD_DIM = 64


LN_EPS = 1e-06
UNIT_EPS = 1e-06
SIM_SCALE = 10.0
MARGIN = 0.3
MASKED = -1e30
MIB = 1024 * 1024


MESH_ID = pl.DeviceIdType.MESH
AXES = ("dp", "fsdp")


class Layout:
    def __init__(self, mesh_shape):
        slow, fast = mesh_shape["dp"], mesh_shape["fsdp"]
        self.slow, self.count = slow, slow * fast
        if slow == 8:
            self.dims = (2, 2, 2, fast)
            self.orders = ((3, 1, 0, 2), (3, 0, 1, 2))
        else:
            self.dims = (slow, fast)
            self.orders = ((1, 0), (1, 0))
        self.sends = sum(size - 1 for size in self.dims)

    def own(self):
        digits = [lax.axis_index("fsdp")]
        rest = lax.axis_index("dp")
        for size in self.dims[-2::-1]:
            digits.insert(0, rest % size)
            rest = rest // size
        return digits

    def device(self, digits):
        slow = digits[0]
        for size, digit in zip(self.dims[1:-1], digits[1:-1]):
            slow = slow * size + digit
        return (slow, digits[-1])

    def shifted(self, own, dim, step):
        size = self.dims[dim]
        out = list(own)
        out[dim] = (own[dim] + step) % size
        return out

    def first_slot(self, order, stage):
        return sum(self.dims[dim] - 1 for dim in order[:stage])

    def greet(self, own):
        barrier = pltpu.get_barrier_semaphore()
        for dim, size in enumerate(self.dims):
            for step in range(1, size):
                pl.semaphore_signal(
                    barrier,
                    inc=1,
                    device_id=self.device(self.shifted(own, dim, step)),
                    device_id_type=MESH_ID,
                )
        pl.semaphore_wait(barrier, self.sends)


class GatherJob:
    def __init__(self, layout, own, order, shard, full, sems, columns=None):
        self.layout, self.own, self.order = layout, own, order
        self.shard, self.full, self.columns = shard, full, columns
        self.send_sems, self.recv_sems, self.local_sem = sems

    def block(self, digits, done):
        index = tuple(
            slice(None) if dim in done else digits[dim] for dim in range(len(self.layout.dims))
        )
        if self.columns is not None:
            index = index + (slice(None), pl.ds(*self.columns))
        return self.full.at[index]

    def piece(self):
        if self.columns is not None:
            return self.shard.at[:, pl.ds(*self.columns)]
        return self.shard

    def copies(self, stage, sending):
        dim, done = self.order[stage], self.order[:stage]
        base = self.layout.first_slot(self.order, stage)
        out = []
        for step in range(1, self.layout.dims[dim]):
            slot = base + step - 1
            other = self.layout.shifted(self.own, dim, step if sending else -step)
            target = self.block(self.own if sending else other, done)
            source = self.piece() if sending and stage == 0 else target
            out.append(
                pltpu.make_async_remote_copy(
                    src_ref=source,
                    dst_ref=target,
                    send_sem=self.send_sems.at[slot],
                    recv_sem=self.recv_sems.at[slot],
                    device_id=self.layout.device(other),
                    device_id_type=MESH_ID,
                )
            )
        return out

    def local(self):
        return pltpu.make_async_copy(self.piece(), self.block(self.own, ()), self.local_sem)

    def advance(self, stage):
        if stage == 0:
            self.local().start()
        else:
            for copy in self.copies(stage - 1, False):
                copy.wait_recv()
            if stage == 1:
                self.local().wait()
        if stage < len(self.order):
            for copy in self.copies(stage, True):
                copy.start()

    def finish(self):
        for stage in range(len(self.order)):
            for copy in self.copies(stage, True):
                copy.wait_send()


def run_rounds(jobs, stages, width=2):
    rounds = []
    last = stages + (len(jobs) - 1) // width
    for step in range(last + 1):
        todo = []
        for index, job in enumerate(jobs):
            stage = step - index // width
            if 0 <= stage <= stages:
                todo.append((job, stage))
        rounds.append(todo)
    return rounds


class Sidecar:
    def __init__(self, jobs, entries, stages, places):
        self.jobs = jobs
        self.rounds = []
        for step in range(max(entries) + stages + 1):
            todo = []
            for job, entry in zip(jobs, entries):
                if 0 <= step - entry <= stages:
                    todo.append((job, step - entry))
            self.rounds.append(todo)
        self.places = places(len(self.rounds))

    def visit(self, step, point):
        for todo, place in zip(self.rounds, self.places):
            if place[1] == point:

                @pl.when(step == place[0])
                def _():
                    for job, stage in todo:
                        job.advance(stage)

    def finish(self):
        for job in self.jobs:
            job.finish()


def evenly(places):
    return lambda count: [places[at * len(places) // count] for at in range(count)]


class SumJob:
    def __init__(self, layout, own, start, lands, results, sems):
        self.layout, self.own, self.start = layout, own, start
        self.lands, self.results = lands, results
        self.send_sems, self.recv_sems = sems
        self.order = tuple(range(len(layout.dims)))

    def copies(self, stage):
        base = self.layout.first_slot(self.order, stage)
        source = self.start if stage == 0 else self.results[stage - 1]
        out = []
        for step in range(1, self.layout.dims[stage]):
            slot = base + step - 1
            out.append(
                pltpu.make_async_remote_copy(
                    src_ref=source,
                    dst_ref=self.lands.at[slot],
                    send_sem=self.send_sems.at[slot],
                    recv_sem=self.recv_sems.at[slot],
                    device_id=self.layout.device(self.layout.shifted(self.own, stage, step)),
                    device_id_type=MESH_ID,
                )
            )
        return out

    def advance(self, stage):
        if stage > 0:
            before = stage - 1
            value = self.start[...] if before == 0 else self.results[before - 1][...]
            base = self.layout.first_slot(self.order, before)
            for at, copy in enumerate(self.copies(before)):
                copy.wait_recv()
                value = value + self.lands[base + at]
            self.results[before][...] = value
        if stage < len(self.order):
            for copy in self.copies(stage):
                copy.start()

    def finish(self):
        for stage in range(len(self.order)):
            for copy in self.copies(stage):
                copy.wait_send()


class ScatterJob:
    def __init__(self, layout, own, order, part, sums, lands, result, sems, columns=None):
        self.layout, self.own, self.order = layout, own, order
        self.part, self.sums, self.lands, self.result = part, sums, lands, result
        self.send_sems, self.recv_sems, self.local_sem = sems
        self.columns = columns

    def tail(self):
        if self.columns is not None:
            return (slice(None), pl.ds(*self.columns))
        return ()

    def local(self):
        dim = self.order[0]
        index = [slice(None)] * len(self.layout.dims)
        index[dim] = self.own[dim]
        return pltpu.make_async_copy(
            self.part.at[tuple(index) + self.tail()], self.sums[0], self.local_sem
        )

    def copies(self, stage):
        dim = self.order[stage]
        base = self.layout.first_slot(self.order, stage)
        left = [d for d in range(len(self.layout.dims)) if d not in self.order[:stage]]
        out = []
        for step in range(1, self.layout.dims[dim]):
            slot = base + step - 1
            there = self.layout.shifted(self.own, dim, step)
            index = tuple(there[dim] if d == dim else slice(None) for d in left)
            if stage == 0:
                source = self.part.at[index + self.tail()]
            else:
                source = self.sums[stage - 1].at[index]
            out.append(
                pltpu.make_async_remote_copy(
                    src_ref=source,
                    dst_ref=self.lands[stage].at[step - 1],
                    send_sem=self.send_sems.at[slot],
                    recv_sem=self.recv_sems.at[slot],
                    device_id=self.layout.device(there),
                    device_id_type=MESH_ID,
                )
            )
        return out

    def add(self, stage):
        dim = self.order[stage]
        left = [d for d in range(len(self.layout.dims)) if d not in self.order[:stage]]
        rest = [d for d in left if d != dim]
        sizes = [self.layout.dims[d] for d in rest]
        total = 1
        for size in sizes:
            total *= size

        def body(flat):
            digits = []
            for size in reversed(sizes):
                digits.insert(0, flat % size)
                flat = flat // size
            if stage == 0:
                own_index = tuple(digits)
                value = self.sums[0][own_index].astype(jnp.float32)
            else:
                where = dict(zip(rest, digits))
                where[dim] = self.own[dim]
                value = self.sums[stage - 1][tuple(where[d] for d in left)].astype(jnp.float32)
            for step in range(1, self.layout.dims[dim]):
                value = value + self.lands[stage][(step - 1,) + tuple(digits)].astype(jnp.float32)
            if rest:
                target = self.sums[stage]
                target[tuple(digits)] = value.astype(target.dtype)
            elif self.columns is not None:
                self.result[:, pl.ds(*self.columns)] = value
            else:
                self.result[...] = value

        if total == 1:
            body(0)
        else:
            pl.loop(0, total)(body)

    def advance(self, stage):
        if stage == 0:
            self.local().start()
        else:
            for copy in self.copies(stage - 1):
                copy.wait_recv()
            if stage == 1:
                self.local().wait()
            self.add(stage - 1)
        if stage < len(self.order):
            for copy in self.copies(stage):
                copy.start()

    def finish(self):
        for stage in range(len(self.order)):
            for copy in self.copies(stage):
                copy.wait_send()


def scatter_buffers(layout, order, rows, columns, dtype):
    sums, lands = [], []
    for stage, dim in enumerate(order):
        rest = tuple(
            size for d, size in enumerate(layout.dims) if d not in order[: stage + 1]
        )
        lands.append(pltpu.VMEM((layout.dims[dim] - 1,) + rest + (rows, columns), dtype))
        if stage < len(order) - 1:
            sums.append(pltpu.VMEM(rest + (rows, columns), dtype))
    return sums + lands


ANYWHERE = pl.BlockSpec(memory_space=pltpu.HBM)


def job_sems(layout, plan):
    return [
        pltpu.SemaphoreType.DMA((len(plan), layout.sends)),
        pltpu.SemaphoreType.DMA((len(plan), layout.sends)),
        pltpu.SemaphoreType.DMA((len(plan),)),
    ]


def gather_jobs(layout, own, plan, shards, fulls, send_sems, recv_sems, local_sems):
    return [
        GatherJob(
            layout,
            own,
            layout.orders[way],
            shards[which],
            fulls[which],
            (send_sems.at[at], recv_sems.at[at], local_sems.at[at]),
            columns,
        )
        for at, (which, way, columns) in enumerate(plan)
    ]


def gather_shapes(layout, arrays):
    return [jax.ShapeDtypeStruct(layout.dims + a.shape, a.dtype) for a in arrays]


def scatter_jobs(layout, own, plan, parts, results, scratch, send_sems, recv_sems, local_sems):
    stages = len(layout.dims)
    buffers = 2 * stages - 1
    jobs = []
    for at, (which, way, columns) in enumerate(plan):
        mine = scratch[at * buffers : (at + 1) * buffers]
        jobs.append(
            ScatterJob(
                layout,
                own,
                layout.orders[way][::-1],
                parts[which],
                mine[: stages - 1],
                mine[stages - 1 :],
                results[which],
                (send_sems.at[at], recv_sems.at[at], local_sems.at[at]),
                columns,
            )
        )
    return jobs


def scatter_scratch(layout, plan, shapes):
    scratch = []
    for which, way, columns in plan:
        rows, width = shapes[which]
        width = width if columns is None else columns[1]
        scratch += scatter_buffers(layout, layout.orders[way][::-1], rows, width, jnp.bfloat16)
    return scratch


def gather_kernel(layout, plan, count, *refs):
    shards, fulls = refs[:count], refs[count : 2 * count]
    send_sems, recv_sems, local_sems = refs[2 * count :]
    own = layout.own()
    layout.greet(own)
    jobs = gather_jobs(layout, own, plan, shards, fulls, send_sems, recv_sems, local_sems)
    for todo in run_rounds(jobs, len(layout.dims)):
        for job, stage in todo:
            job.advance(stage)
    for job in jobs:
        job.finish()


def gather_all(layout, arrays, plan, collective_id):
    return pl.pallas_call(
        functools.partial(gather_kernel, layout, plan, len(arrays)),
        out_shape=gather_shapes(layout, arrays),
        in_specs=[ANYWHERE] * len(arrays),
        out_specs=[ANYWHERE] * len(arrays),
        scratch_shapes=job_sems(layout, plan),
        compiler_params=pltpu.CompilerParams(
            collective_id=collective_id, has_side_effects=True, vmem_limit_bytes=16 * MIB
        ),
    )(*arrays)


def cut(which, way, width, pieces):
    if width % (pieces * 128):
        return [(which, way, None)]
    step = width // pieces
    return [(which, way, (at * step, step)) for at in range(pieces)]


def weave(first, second):
    out = []
    for at in range(max(len(first), len(second))):
        out += first[at : at + 1] + second[at : at + 1]
    return out


def copy_kernel(count, *refs):
    for source, target in zip(refs[:count], refs[count:]):
        target[...] = source[...]


def copy_all(arrays):
    return pl.pallas_call(
        functools.partial(copy_kernel, len(arrays)),
        out_shape=[jax.ShapeDtypeStruct(a.shape, a.dtype) for a in arrays],
    )(*arrays)


def small_pack(layout, vectors):
    flat = jnp.concatenate([v.astype(jnp.float32).reshape(v.shape[0], -1) for v in vectors], 1)
    width = -(-flat.shape[1] // 1024) * 1024
    flat = jnp.pad(flat, ((0, 0), (0, width - flat.shape[1])))
    return flat.reshape(flat.shape[0], width // 128, 128)


def dot_plain(first_mat, second_mat):
    return jnp.dot(first_mat, second_mat, preferred_element_type=jnp.float32)


def dot_left_t(first_mat, second_mat):
    return lax.dot_general(
        first_mat, second_mat, (((0,), (0,)), ((), ())), preferred_element_type=jnp.float32
    )


def dot_right_t(first_mat, second_mat):
    return lax.dot_general(
        first_mat, second_mat, (((1,), (1,)), ((), ())), preferred_element_type=jnp.float32
    )


def row_mean(value):
    return jnp.sum(value, -1, keepdims=True) * (1.0 / value.shape[-1])


def norm_parts(row_data):
    centred = row_data - row_mean(row_data)
    inverse = lax.rsqrt(row_mean(centred * centred) + LN_EPS)
    return centred * inverse, inverse


def norm_backward(upstream, normed, inverse, gain_vec):
    scaled = upstream * gain_vec
    return inverse * (scaled - row_mean(scaled) - normed * row_mean(scaled * normed))


def column_sum(value):
    return jnp.sum(value, 0, keepdims=True)


def gelu_and_slope(inner_act):
    below = 0.5 * (1.0 + lax.erf(inner_act * 0.7071067811865476))
    bell = jnp.exp(-0.5 * inner_act * inner_act) * 0.3989422804014327
    return inner_act * below, below + inner_act * bell


GROUP = 4
SPAN = GROUP * HEAD_DIM


def spread(rows, diag):
    return jnp.concatenate([rows] * GROUP, 0) * diag


def fold(square, seq_len):
    lane = lax.broadcasted_iota(jnp.int32, (seq_len, square.shape[1]), 1)
    out = square[:seq_len]
    for head in range(1, GROUP):
        block = square[head * seq_len : (head + 1) * seq_len]
        out = jnp.where(lane >= head * HEAD_DIM, block, out)
    return out


def probabilities(keys, wide_queries, length):
    scores = dot_right_t(keys, wide_queries) * HEAD_DIM ** (-0.5)
    at = lax.broadcasted_iota(jnp.int32, scores.shape, 0)
    scores = jnp.where(at < length, scores, MASKED)
    raised = jnp.exp(scores - jnp.max(scores, 0, keepdims=True))
    return raised * (1.0 / jnp.sum(raised, 0, keepdims=True))


def attend_kernel(
    layout,
    seq_len,
    plan,
    count,
    steps,
    lengths_ref,
    x_ref,
    query_w,
    key_w,
    value_w,
    proj_w,
    vec_ref,
    diag_ref,
    *refs,
):
    shards, (q_ref, k_ref, v_ref, mix_ref, sum_ref, cls_ref) = refs[:count], refs[count : count + 6]
    fulls, sems = refs[count + 6 : 2 * count + 6], refs[2 * count + 6 :]
    rows, width = x_ref.shape
    held = rows // seq_len
    step = pl.program_id(0)
    first = step * held
    own = layout.own()

    @pl.when(step == 0)
    def _():
        layout.greet(own)

    jobs = gather_jobs(layout, own, plan, shards, fulls, *sems)
    places = [(at, point) for at in range(steps) for point in range(4)]
    sidecar = Sidecar(jobs, [at // 2 for at in range(len(jobs))], len(layout.dims), evenly(places))
    sidecar.visit(step, 0)
    x = x_ref[...]
    q_ref[...] = (dot_plain(x, query_w[...]) + vec_ref[0:1, :]).astype(jnp.bfloat16)
    k_ref[...] = dot_plain(x, key_w[...]).astype(jnp.bfloat16)
    v_ref[...] = (dot_plain(x, value_w[...]) + vec_ref[1:2, :]).astype(jnp.bfloat16)
    diag = diag_ref[...]
    sidecar.visit(step, 1)

    def sentence(at):
        length = lengths_ref[first + at]
        here = pl.ds(at * seq_len, seq_len)
        for low in range(0, width, SPAN):
            cols = pl.ds(low, SPAN)
            wide = spread(q_ref[here, cols], diag)
            probs = probabilities(k_ref[here, cols], wide, length).astype(jnp.bfloat16)
            mixed = fold(dot_left_t(probs, v_ref[here, cols]), seq_len)
            mix_ref[here, cols] = mixed.astype(jnp.bfloat16)

    for at in range(held // 2):
        sentence(at)
    sidecar.visit(step, 2)
    for at in range(held // 2, held):
        sentence(at)
    sidecar.visit(step, 3)
    total = x.astype(jnp.float32) + dot_plain(mix_ref[...], proj_w[...]) + vec_ref[2:3, :]
    sum_ref[...] = total
    for at in range(held):
        cls_ref[0, at : at + 1, :] = total[at * seq_len : at * seq_len + 1]

    @pl.when(step == steps - 1)
    def _():
        sidecar.finish()


def whole(shape):
    return pl.BlockSpec(shape, lambda *_: (0,) * len(shape), pipeline_mode=pl.Buffered(1))


def attend(layout, x, lengths, weights, vec, diag, arrays, plan, seq_len, rows, collective_id):
    total, width = x.shape
    steps = total // rows
    held = rows // seq_len
    block = pl.BlockSpec((rows, width), lambda i: (i, 0))
    narrow = jax.ShapeDtypeStruct((total, width), jnp.bfloat16)
    return pl.pallas_call(
        functools.partial(attend_kernel, layout, seq_len, plan, len(arrays), steps),
        grid=(steps,),
        out_shape=[
            narrow,
            narrow,
            narrow,
            narrow,
            jax.ShapeDtypeStruct((total, width), jnp.float32),
            jax.ShapeDtypeStruct((steps, held, width), jnp.float32),
        ]
        + gather_shapes(layout, arrays),
        in_specs=[pl.BlockSpec(memory_space=pltpu.SMEM), block]
        + [whole(w.shape) for w in weights]
        + [whole(vec.shape), whole(diag.shape)]
        + [ANYWHERE] * len(arrays),
        out_specs=[block] * 5
        + [pl.BlockSpec((1, held, width), lambda i: (i, 0, 0))]
        + [ANYWHERE] * len(arrays),
        scratch_shapes=job_sems(layout, plan),
        compiler_params=pltpu.CompilerParams(
            collective_id=collective_id, has_side_effects=True, vmem_limit_bytes=60 * MIB
        ),
    )(lengths, x, *weights, vec, diag, *arrays)


def feed_kernel(
    seq_len,
    blocks,
    pieces,
    sum_ref,
    tok_ref,
    mix_ref,
    cls_ref,
    inner_w,
    outer_w,
    vec_ref,
    bias_ref,
    out_ref,
    back_ref,
    inner_grad,
    outer_grad,
    proj_grad,
    vec_grad,
    bias_grad,
    slope,
    active,
    inner_b,
    hidden_b,
    second_b,
    proj_sum,
):
    step = pl.program_id(0)
    rows, width = sum_ref.shape
    piece = active.shape[2]

    @pl.when(step == 0)
    def _():
        vec_grad[...] = jnp.zeros_like(vec_grad)
        bias_grad[...] = jnp.zeros_like(bias_grad)
        proj_sum[...] = jnp.zeros_like(proj_sum)

    @pl.when(step < blocks)
    def _():
        here = pl.ds(pl.multiple_of(step * rows, rows), rows)
        gain_one, shift_one = vec_ref[3:4, :], vec_ref[4:5, :]
        gain_two, shift_two = vec_ref[6:7, :], vec_ref[7:8, :]
        normed_one, inverse_one = norm_parts(sum_ref[...])
        hidden = normed_one * gain_one + shift_one
        narrow = hidden.astype(jnp.bfloat16)
        hidden_b[here, :] = narrow
        second_sum = hidden + vec_ref[5:6, :]
        for at in range(pieces):
            cols = slice(at * piece, (at + 1) * piece)
            value, steep = gelu_and_slope(dot_plain(narrow, inner_w[:, cols]) + bias_ref[:, cols])
            value = value.astype(jnp.bfloat16)
            slope[at] = steep
            active[at, here, :] = value
            second_sum = second_sum + dot_plain(value, outer_w[cols, :])
        normed_two, inverse_two = norm_parts(second_sum)
        out_ref[...] = (normed_two * gain_two + shift_two).astype(jnp.bfloat16)
        grad = tok_ref[...].astype(jnp.float32).reshape(rows // seq_len, seq_len, width)
        place = lax.broadcasted_iota(jnp.int32, grad.shape, 1)
        extra = cls_ref[...].reshape(rows // seq_len, 1, width)
        grad = (grad + jnp.where(place == 0, extra, 0.0)).reshape(rows, width)
        vec_grad[6:7, :] += column_sum(grad * normed_two)
        vec_grad[7:8, :] += column_sum(grad)
        second = norm_backward(grad, normed_two, inverse_two, gain_two)
        vec_grad[5:6, :] += column_sum(second)
        narrow_two = second.astype(jnp.bfloat16)
        second_b[here, :] = narrow_two
        hidden_grad = second
        for at in range(pieces):
            cols = slice(at * piece, (at + 1) * piece)
            inner = dot_right_t(narrow_two, outer_w[cols, :]) * slope[at]
            bias_grad[:, cols] += column_sum(inner)
            inner = inner.astype(jnp.bfloat16)
            inner_b[at, here, :] = inner
            hidden_grad = hidden_grad + dot_right_t(inner, inner_w[:, cols])
        vec_grad[3:4, :] += column_sum(hidden_grad * normed_one)
        vec_grad[4:5, :] += column_sum(hidden_grad)
        first = norm_backward(hidden_grad, normed_one, inverse_one, gain_one)
        vec_grad[2:3, :] += column_sum(first)
        back_ref[...] = first
        proj_sum[...] += dot_left_t(mix_ref[...], first.astype(jnp.bfloat16))

        @pl.when(step == blocks - 1)
        def _():
            proj_grad[...] = proj_sum[...].astype(jnp.bfloat16)

    @pl.when(step >= blocks)
    def _():
        at = step - blocks
        outer_grad[...] = dot_left_t(active[at], second_b[...]).astype(jnp.bfloat16)
        inner_grad[...] = dot_left_t(hidden_b[...], inner_b[at]).astype(jnp.bfloat16)


def feed(
    first_sum, tokens_grad, mixture, cls_grad, inner_w, outer_w, vec, bias, seq_len, rows, piece
):
    total, width = first_sum.shape
    wide = inner_w.shape[1]
    blocks, pieces = total // rows, wide // piece
    held = rows // seq_len
    cls_grad = cls_grad.reshape(blocks, held, width)
    block = pl.BlockSpec((rows, width), lambda i: (jnp.minimum(i, blocks - 1), 0))
    return pl.pallas_call(
        functools.partial(feed_kernel, seq_len, blocks, pieces),
        grid=(blocks + pieces,),
        out_shape=[
            jax.ShapeDtypeStruct((total, width), jnp.bfloat16),
            jax.ShapeDtypeStruct((total, width), jnp.float32),
            jax.ShapeDtypeStruct(inner_w.shape, jnp.bfloat16),
            jax.ShapeDtypeStruct(outer_w.shape, jnp.bfloat16),
            jax.ShapeDtypeStruct((width, width), jnp.bfloat16),
            jax.ShapeDtypeStruct((8, width), jnp.float32),
            jax.ShapeDtypeStruct((1, wide), jnp.float32),
        ],
        in_specs=[
            block,
            block,
            block,
            pl.BlockSpec((1, held, width), lambda i: (jnp.minimum(i, blocks - 1), 0, 0)),
            whole(inner_w.shape),
            whole(outer_w.shape),
            whole(vec.shape),
            whole(bias.shape),
        ],
        out_specs=[
            block,
            block,
            pl.BlockSpec((width, piece), lambda i: (0, jnp.maximum(i - blocks, 0))),
            pl.BlockSpec((piece, width), lambda i: (jnp.maximum(i - blocks, 0), 0)),
            whole((width, width)),
            pl.BlockSpec((8, width), lambda i: (0, 0)),
            pl.BlockSpec((1, wide), lambda i: (0, 0)),
        ],
        scratch_shapes=[
            pltpu.VMEM((pieces, rows, piece), jnp.float32),
            pltpu.VMEM((pieces, total, piece), jnp.bfloat16),
            pltpu.VMEM((pieces, total, piece), jnp.bfloat16),
            pltpu.VMEM((total, width), jnp.bfloat16),
            pltpu.VMEM((total, width), jnp.bfloat16),
            pltpu.VMEM((width, width), jnp.float32),
        ],
        compiler_params=pltpu.CompilerParams(vmem_limit_bytes=63 * MIB),
    )(first_sum, tokens_grad, mixture, cls_grad, inner_w, outer_w, vec, bias)


def unflat(flat, dims):
    digits = []
    for size in reversed(dims):
        digits.insert(0, flat % size)
        flat = flat // size
    return tuple(digits)


def back_kernel(
    layout,
    seq_len,
    blocks,
    plan,
    entries,
    count,
    lengths_ref,
    x_ref,
    q_ref,
    k_ref,
    v_ref,
    first_ref,
    query_w,
    key_w,
    value_w,
    proj_w,
    diag_ref,
    feed_vec,
    feed_bias,
    pool_vec,
    *refs,
):
    step = pl.program_id(0)
    rows, width = x_ref.shape
    held = rows // seq_len
    scale = HEAD_DIM ** (-0.5)
    stages = len(layout.dims)
    parts, refs = refs[:count], refs[count:]
    (in_ref, vec_sum), refs = refs[:2], refs[2:]
    sums, refs = refs[: count + 3], refs[count + 3 :]
    (x_all, dq_all, dk_all, dv_all, dmix), refs = refs[:5], refs[5:]
    own_parts, refs = refs[:3], refs[3:]
    (vec_grad, vec_lands), refs = refs[:2], refs[2:]
    vec_steps, refs = refs[: stages - 1], refs[stages - 1 :]
    own = layout.own()
    vec_job = SumJob(layout, own, vec_grad, vec_lands, tuple(vec_steps) + (vec_sum,), refs[-2:])
    jobs = scatter_jobs(layout, own, plan, parts + own_parts, sums, refs[:-5], *refs[-5:-2])

    def places(total):
        early = [(at // 2, at % 2) for at in range(2 * blocks)]
        first_own = min(entry for entry, job in zip(entries, plan) if job[0] >= count)
        out = [early[at * len(early) // first_own] for at in range(first_own)]
        out += [(blocks + at, 1) for at in range(3)]
        late = [(blocks + 3 + at, 0) for at in range(1, blocks)] + [(2 * blocks + 2, 1)]
        rest = total - len(out)
        stride = max(1, (len(late) - 1) // rest)
        return out + [late[min(at * stride, len(late) - 1)] for at in range(rest)]

    last_entry = max(entries)
    sidecar = Sidecar(jobs + [vec_job], list(entries) + [last_entry], stages, places)

    @pl.when(step == 0)
    def _():
        layout.greet(own)
        vec_grad[0:2, :] = jnp.zeros_like(vec_grad[0:2, :])
        vec_grad[2:8, :] = feed_vec[2:8, :]
        vec_grad[8:9, :] = pool_vec[...]
        pieces = feed_bias.shape[1] // width
        vec_grad[9:, :] = jnp.zeros_like(vec_grad[9:, :])
        for at in range(pieces):
            vec_grad[9 + at : 10 + at, :] = feed_bias[:, at * width : (at + 1) * width]

    @pl.when(step < blocks)
    def _():
        here = pl.ds(pl.multiple_of(step * rows, rows), rows)
        sidecar.visit(step, 0)
        x_all[here, :] = x_ref[...]
        narrow = first_ref[...].astype(jnp.bfloat16)
        dmix[...] = dot_right_t(narrow, proj_w[...]).astype(jnp.bfloat16)
        diag = diag_ref[...]

        def sentence(at):
            length = lengths_ref[step * held + at]
            near = pl.ds(at * seq_len, seq_len)
            far = pl.ds(pl.multiple_of(step * rows + at * seq_len, seq_len), seq_len)
            for low in range(0, width, SPAN):
                cols = pl.ds(low, SPAN)
                keys = k_ref[near, cols]
                wide = spread(q_ref[near, cols], diag)
                wide_grad = spread(dmix[near, cols], diag)
                probs = probabilities(keys, wide, length)
                prob_grad = dot_right_t(v_ref[near, cols], wide_grad)
                dv_all[far, cols] = dot_plain(probs.astype(jnp.bfloat16), wide_grad).astype(
                    jnp.bfloat16
                )
                score_grad = probs * (prob_grad - column_sum(prob_grad * probs))
                score_grad = score_grad.astype(jnp.bfloat16)
                dk_all[far, cols] = (dot_plain(score_grad, wide) * scale).astype(jnp.bfloat16)
                dq_all[far, cols] = (fold(dot_left_t(score_grad, keys), seq_len) * scale).astype(
                    jnp.bfloat16
                )

        for at in range(held // 2):
            sentence(at)
        sidecar.visit(step, 1)
        for at in range(held // 2, held):
            sentence(at)
        vec_grad[0:1, :] += column_sum(dq_all[here, :].astype(jnp.float32))
        vec_grad[1:2, :] += column_sum(dv_all[here, :].astype(jnp.float32))

    for at, (right, part) in enumerate(zip((dq_all, dk_all, dv_all), own_parts)):

        @pl.when(step == blocks + at)
        def _():
            value = dot_left_t(x_all[...], right[...])
            share = part.shape[-2]
            for device in range(layout.count):
                piece = value[device * share : (device + 1) * share]
                part[unflat(device, layout.dims)] = piece.astype(jnp.bfloat16)
            sidecar.visit(step, 1)

    @pl.when(step >= blocks + 3)
    def _():
        sidecar.visit(step, 0)
        here = pl.ds(pl.multiple_of((step - blocks - 3) * rows, rows), rows)
        in_ref[...] = (
            first_ref[...]
            + dot_right_t(dq_all[here, :], query_w[...])
            + dot_right_t(dk_all[here, :], key_w[...])
            + dot_right_t(dv_all[here, :], value_w[...])
        )
        sidecar.visit(step, 1)

    @pl.when(step == 2 * blocks + 2)
    def _():
        sidecar.finish()


def back(
    layout,
    x,
    lengths,
    saved,
    first_grad,
    weights,
    diag,
    vectors,
    arrays,
    plan,
    entries,
    seq_len,
    rows,
    collective_id,
):
    total, width = x.shape
    blocks = total // rows
    stages = len(layout.dims)
    share = width // layout.count
    shapes = [a.shape[-2:] for a in arrays] + [(share, width)] * 3
    block = pl.BlockSpec((rows, width), lambda i: (jnp.minimum(i, blocks - 1), 0))
    twice = pl.BlockSpec(
        (rows, width),
        lambda i: (jnp.where(i < blocks, i, jnp.maximum(i - blocks - 3, 0)), 0),
    )
    out_block = pl.BlockSpec((rows, width), lambda i: (jnp.maximum(i - blocks - 3, 0), 0))
    small = pltpu.VMEM((16, width), jnp.float32)
    return pl.pallas_call(
        functools.partial(back_kernel, layout, seq_len, blocks, plan, entries, len(arrays)),
        grid=(2 * blocks + 3,),
        out_shape=[
            jax.ShapeDtypeStruct((total, width), jnp.float32),
            jax.ShapeDtypeStruct((16, width), jnp.float32),
        ]
        + [jax.ShapeDtypeStruct(s, jnp.float32) for s in shapes],
        in_specs=[pl.BlockSpec(memory_space=pltpu.SMEM)]
        + [block] * 4
        + [twice]
        + [whole(w.shape) for w in weights]
        + [whole(diag.shape)]
        + [whole(v.shape) for v in vectors]
        + [ANYWHERE] * len(arrays),
        out_specs=[out_block, whole((16, width))] + [whole(s) for s in shapes],
        scratch_shapes=[pltpu.VMEM((total, width), jnp.bfloat16)] * 4
        + [pltpu.VMEM((rows, width), jnp.bfloat16)]
        + [pltpu.VMEM(layout.dims + (share, width), jnp.bfloat16)] * 3
        + [small, pltpu.VMEM((layout.sends, 16, width), jnp.float32)]
        + [small] * (stages - 1)
        + scatter_scratch(layout, plan, shapes)
        + job_sems(layout, plan)
        + [pltpu.SemaphoreType.DMA((layout.sends,))] * 2,
        compiler_params=pltpu.CompilerParams(
            collective_id=collective_id, has_side_effects=True, vmem_limit_bytes=63 * MIB
        ),
    )(lengths, x, *saved, first_grad, *weights, diag, *vectors, *arrays)


def rank_kernel(
    layout,
    micros,
    node_dev,
    steps,
    sum_ref,
    inner_w,
    outer_w,
    pool_w,
    vec_ref,
    bias_ref,
    node_ref,
    cls_grad,
    pool_grad,
    shift_grad,
    hidden,
    total,
    mine,
    units,
    node_cols,
    totals,
    send_sems,
    recv_sems,
    local_sem,
):
    step = pl.program_id(0)
    sentences, width = sum_ref.shape
    own = layout.own()

    @pl.when(step == 0)
    def _():
        layout.greet(own)
        normed, _ = norm_parts(sum_ref[...])
        start = normed * vec_ref[3:4, :] + vec_ref[4:5, :]
        hidden[...] = start.astype(jnp.bfloat16)
        total[...] = start + vec_ref[5:6, :]
        node_cols[...] = node_ref[...].T

    value, _ = gelu_and_slope(dot_plain(hidden[...], inner_w[...]) + bias_ref[...])
    total[...] += dot_plain(value.astype(jnp.bfloat16), outer_w[...])

    @pl.when(step == steps - 1)
    def _():
        normed, _ = norm_parts(total[...])
        cls_rows = (normed * vec_ref[6:7, :] + vec_ref[7:8, :]).astype(jnp.bfloat16)
        pooled = jnp.tanh(dot_plain(cls_rows, pool_w[...]) + vec_ref[8:9, :])
        scale_inv = lax.rsqrt(jnp.sum(pooled * pooled, -1, keepdims=True) + UNIT_EPS)
        unit = pooled * scale_inv
        mine[...] = unit.astype(jnp.bfloat16)
        job = GatherJob(
            layout, own, layout.orders[0], mine, units, (send_sems, recv_sems, local_sem)
        )
        for stage in range(len(layout.dims) + 1):
            job.advance(stage)
        job.finish()

        device = own[0]
        for size, digit in zip(layout.dims[1:], own[1:]):
            device = device * size + digit
        at_home = pl.ds(pl.multiple_of(device * node_dev, node_dev), node_dev)
        count = layout.count * node_dev
        band = min(count, 512)
        every = units[...].reshape(layout.count, sentences, width)
        grads = []

        def scored(similar, tongue, place, side, tongue_row, place_row, side_row):
            across = side != side_row
            include = across & (tongue == tongue_row)
            positive = jnp.where(across & (place == place_row), 1.0, 0.0)
            return (
                jnp.where(include, SIM_SCALE * similar - SIM_SCALE * MARGIN * positive, MASKED),
                include,
                positive,
            )

        half = node_dev // 2

        def sides(shape, dim, offset):
            return (lax.broadcasted_iota(jnp.int32, shape, dim) + offset) // half % 2

        for micro in range(micros):
            here = slice(micro * node_dev, (micro + 1) * node_dev)
            nodes = every[:, here, :].reshape(count, width)
            tongue, place = node_cols[:, 2 * micro : 2 * micro + 1], node_cols[
                :, 2 * micro + 1 : 2 * micro + 2
            ]
            for low in range(0, count, band):
                cols = slice(low, low + band)
                similar = dot_right_t(nodes, nodes[cols])
                value, _, _ = scored(
                    similar,
                    tongue,
                    place,
                    sides((count, 1), 0, 0),
                    node_ref[2 * micro : 2 * micro + 1, cols],
                    node_ref[2 * micro + 1 : 2 * micro + 2, cols],
                    sides((1, band), 1, low),
                )
                peak = jnp.max(value, 0, keepdims=True)
                totals[:, cols] = jnp.log(column_sum(jnp.exp(value - peak))) + peak
            value, include, positive = scored(
                dot_right_t(mine[here, :], nodes),
                node_cols[at_home, 2 * micro : 2 * micro + 1],
                node_cols[at_home, 2 * micro + 1 : 2 * micro + 2],
                sides((node_dev, 1), 0, 0),
                node_ref[2 * micro : 2 * micro + 1, :],
                node_ref[2 * micro + 1 : 2 * micro + 2, :],
                sides((1, count), 1, 0),
            )
            peak = jnp.max(value, -1, keepdims=True)
            line = jnp.log(jnp.sum(jnp.exp(value - peak), -1, keepdims=True)) + peak
            grad_sim = jnp.where(
                include, jnp.exp(value - line) + jnp.exp(value - totals[...]), 0.0
            )
            grad_sim = (grad_sim - 2.0 * positive).astype(jnp.bfloat16)
            grads.append(SIM_SCALE * dot_plain(grad_sim, nodes))
        unit_grad = jnp.concatenate(grads, 0)
        pooled_grad = scale_inv * (
            unit_grad - unit * jnp.sum(unit_grad * unit, -1, keepdims=True)
        )
        pre_grad = pooled_grad * (1.0 - pooled * pooled)
        narrow = pre_grad.astype(jnp.bfloat16)
        pool_grad[...] = dot_left_t(cls_rows, narrow).astype(jnp.bfloat16)
        shift_grad[...] = column_sum(pre_grad)
        cls_grad[...] = dot_right_t(narrow, pool_w[...])


def rank(layout, cls_sum, inner_w, outer_w, pool_w, vec, bias, nodes, micros, piece, collective_id):
    sentences, width = cls_sum.shape
    wide = inner_w.shape[1]
    steps = wide // piece
    node_dev = sentences // micros
    return pl.pallas_call(
        functools.partial(rank_kernel, layout, micros, node_dev, steps),
        grid=(steps,),
        out_shape=[
            jax.ShapeDtypeStruct((sentences, width), jnp.float32),
            jax.ShapeDtypeStruct((width, width), jnp.bfloat16),
            jax.ShapeDtypeStruct((1, width), jnp.float32),
        ],
        in_specs=[
            whole(cls_sum.shape),
            pl.BlockSpec((width, piece), lambda i: (0, i)),
            pl.BlockSpec((piece, width), lambda i: (i, 0)),
            whole(pool_w.shape),
            whole(vec.shape),
            pl.BlockSpec((1, piece), lambda i: (0, i)),
            whole(nodes.shape),
        ],
        out_specs=[
            pl.BlockSpec((sentences, width), lambda i: (0, 0)),
            pl.BlockSpec((width, width), lambda i: (0, 0)),
            pl.BlockSpec((1, width), lambda i: (0, 0)),
        ],
        scratch_shapes=[
            pltpu.VMEM((sentences, width), jnp.bfloat16),
            pltpu.VMEM((sentences, width), jnp.float32),
            pltpu.VMEM((sentences, width), jnp.bfloat16),
            pltpu.VMEM(layout.dims + (sentences, width), jnp.bfloat16),
            pltpu.VMEM((nodes.shape[1], nodes.shape[0]), jnp.float32),
            pltpu.VMEM((1, nodes.shape[1]), jnp.float32),
            pltpu.SemaphoreType.DMA((layout.sends,)),
            pltpu.SemaphoreType.DMA((layout.sends,)),
            pltpu.SemaphoreType.DMA,
        ],
        compiler_params=pltpu.CompilerParams(
            collective_id=collective_id, has_side_effects=True, vmem_limit_bytes=60 * MIB
        ),
    )(cls_sum, inner_w, outer_w, pool_w, vec, bias, nodes)


def on_device(
    layout,
    hidden_in,
    lengths,
    partner,
    language,
    token_cotangent,
    query_weight,
    key_weight,
    value_weight,
    attn_out_weight,
    query_bias,
    value_bias,
    attn_out_bias,
    ln1_gain,
    ln1_shift,
    in_weight,
    in_bias,
    out_weight,
    out_bias,
    ln2_gain,
    ln2_shift,
    pool_weight,
    pool_bias,
):
    micro_count, sides, pair_dev, seq_len, model_width = hidden_in.shape
    inner_width = in_weight.shape[1]
    count = layout.count
    node_dev = sides * pair_dev
    sent_count = micro_count * node_dev
    row_count = sent_count * seq_len
    pair_count = partner.shape[1]
    device = lax.axis_index("dp") * (count // layout.slow) + lax.axis_index("fsdp")

    vectors = (
        query_bias,
        value_bias,
        attn_out_bias,
        ln1_gain,
        ln1_shift,
        out_bias,
        ln2_gain,
        ln2_shift,
        pool_bias,
        in_bias,
    )
    small = small_pack(layout, [v[None] for v in vectors])[0]
    arrays = [query_weight, key_weight, value_weight, attn_out_weight, small]
    plan = [(4, 0, None)]
    plan += weave(cut(0, 0, model_width, 2), cut(1, 1, model_width, 2))
    plan += weave(cut(2, 0, model_width, 2), cut(3, 1, model_width, 2))
    gathered = gather_all(layout, arrays, tuple(plan), 0)

    def joined(full, array):
        return full.reshape((count * array.shape[0],) + array.shape[1:])

    *weights, small_full = map(joined, gathered, arrays)
    small_rows = small_full.reshape(count, -1)
    share = query_bias.shape[0]
    rows_of = len(vectors) - 1
    vec = small_rows[:, : rows_of * share].reshape(count, rows_of, share)
    vec = jnp.moveaxis(vec, 1, 0).reshape(rows_of, model_width)
    vec = jnp.pad(vec, ((0, 16 - rows_of), (0, 0)))
    bias = small_rows[:, rows_of * share : rows_of * share + in_bias.shape[0]]
    bias = bias.reshape(1, inner_width)

    pair_ids = jnp.arange(pair_count, dtype=jnp.int32)
    hit = partner[:, :, None] == pair_ids[None, None, :]
    target_language = jnp.sum(jnp.where(hit, language[:, :, None], 0), 1)

    def split(value):
        return value.reshape(micro_count, count, 1, pair_dev)

    node_rows = jnp.stack(
        [
            jnp.concatenate([split(language), split(target_language)], 2),
            jnp.concatenate(
                [split(partner), split(jnp.broadcast_to(pair_ids, partner.shape))], 2
            ),
        ],
        1,
    )
    node_rows = node_rows.reshape(2 * micro_count, count * node_dev).astype(jnp.float32)
    node_rows = jnp.pad(node_rows, ((0, -2 * micro_count % 8), (0, 0)))
    block_at = jnp.arange(SPAN) // HEAD_DIM
    diag = (block_at[:, None] == block_at[None, :]).astype(jnp.bfloat16)

    x = hidden_in.reshape(row_count, model_width)
    sent_lengths = lengths.reshape(sent_count)
    arrays = [in_weight, out_weight, pool_weight]
    plan = weave(cut(0, 0, inner_width, 4), cut(1, 1, model_width, 3)) + [(2, 1, None)]
    queries, keys, values, mixture, first_sum, cls_sum, *gathered = attend(
        layout, x, sent_lengths, weights, vec, diag, arrays, tuple(plan), seq_len, 512, 1
    )
    inner_full, outer_full, pool_full = map(joined, gathered, arrays)
    cls_grad, grad_pool, grad_pool_shift = rank(
        layout,
        cls_sum.reshape(sent_count, model_width),
        inner_full,
        outer_full,
        pool_full,
        vec,
        bias,
        node_rows,
        micro_count,
        384,
        2,
    )
    block_out, first_grad, grad_inner, grad_outer, grad_proj, vec_grad, grad_bias = feed(
        first_sum,
        token_cotangent.reshape(row_count, model_width),
        mixture,
        cls_grad,
        inner_full,
        outer_full,
        vec,
        bias,
        seq_len,
        256,
        768,
    )

    def apart(part):
        return part.reshape(layout.dims + (-1, part.shape[1]))

    parts = list(map(apart, (grad_inner, grad_outer, grad_pool, grad_proj)))
    plan = weave(cut(0, 0, inner_width, 4), cut(1, 1, model_width, 3))
    plan += [(2, 1, None), (3, 0, None)]
    entries = [at // 2 for at in range(len(plan))]
    for which in (4, 5, 6):
        halves = cut(which, 0, model_width, 2)[:1] + cut(which, 1, model_width, 2)[1:]
        entries += [entries[-1] + 1] * len(halves)
        plan += halves
    input_grad, vec_sum, *sums = back(
        layout,
        x,
        sent_lengths,
        (queries, keys, values),
        first_grad,
        weights,
        diag,
        (vec_grad, grad_bias, grad_pool_shift),
        parts,
        tuple(plan),
        tuple(entries),
        seq_len,
        256,
        3,
    )
    block_out = block_out.reshape(hidden_in.shape)
    input_grad = input_grad.reshape(hidden_in.shape)
    sums = copy_all(sums)
    vec_own = lax.dynamic_slice_in_dim(vec_sum[:rows_of], device * share, share, 1)
    bias_sum = vec_sum[rows_of : rows_of + inner_width // model_width].reshape(-1)
    bias_own = lax.dynamic_slice_in_dim(bias_sum, device * in_bias.shape[0], in_bias.shape[0])
    (
        sum_query_shift,
        sum_value_shift,
        sum_proj_shift,
        sum_gain_one,
        sum_shift_one,
        sum_outer_shift,
        sum_gain_two,
        sum_shift_two,
        sum_pool_shift,
    ) = vec_own
    return (
        block_out,
        input_grad,
        sums[4],
        sums[5],
        sums[6],
        sums[3],
        sum_query_shift,
        sum_value_shift,
        sum_proj_shift,
        sum_gain_one,
        sum_shift_one,
        sums[0],
        bias_own,
        sums[1],
        sum_outer_shift,
        sum_gain_two,
        sum_shift_two,
        sums[2],
        sum_pool_shift,
    )


def solution(mesh):
    rows = P(("dp", "fsdp"), None)
    vector = P(("dp", "fsdp"))
    sentences = P(None, None, ("dp", "fsdp"), None, None)
    placed = (
        (sentences, P(None, None, ("dp", "fsdp")), P(), P(), sentences)
        + (rows,) * 4
        + (vector,) * 5
        + (rows, vector, rows)
        + (vector,) * 3
        + (rows, vector)
    )
    return jax.shard_map(
        functools.partial(on_device, Layout(mesh.shape)),
        mesh=mesh,
        in_specs=placed,
        out_specs=(sentences, sentences)
        + (rows,) * 4
        + (vector,) * 5
        + (rows, vector, rows)
        + (vector,) * 3
        + (rows, vector),
        check_vma=False,
    )
```

```python
import functools

import jax
import jax.numpy as jnp
from jax import lax
from jax.experimental import pallas as pl
from jax.experimental.pallas import tpu as pltpu
from jax.sharding import PartitionSpec as P

HEAD_DIM = 64


LN_EPS = 1e-06
UNIT_EPS = 1e-06
SIM_SCALE = 10.0
MARGIN = 0.3
MASKED = -1e30
MIB = 1024 * 1024


MESH_ID = pl.DeviceIdType.MESH
AXES = ("dp", "fsdp")


class Layout:
    def __init__(self, mesh_shape):
        slow, fast = mesh_shape["dp"], mesh_shape["fsdp"]
        self.slow, self.count = slow, slow * fast
        if slow == 8:
            self.dims = (2, 2, 2, fast)
            self.orders = ((3, 1, 0, 2), (3, 0, 1, 2))
        else:
            self.dims = (slow, fast)
            self.orders = ((1, 0), (1, 0))
        self.sends = sum(size - 1 for size in self.dims)

    def own(self):
        digits = [lax.axis_index("fsdp")]
        rest = lax.axis_index("dp")
        for size in self.dims[-2::-1]:
            digits.insert(0, rest % size)
            rest = rest // size
        return digits

    def device(self, digits):
        slow = digits[0]
        for size, digit in zip(self.dims[1:-1], digits[1:-1]):
            slow = slow * size + digit
        return (slow, digits[-1])

    def shifted(self, own, dim, step):
        size = self.dims[dim]
        out = list(own)
        out[dim] = (own[dim] + step) % size
        return out

    def first_slot(self, order, stage):
        return sum(self.dims[dim] - 1 for dim in order[:stage])

    def greet(self, own):
        barrier = pltpu.get_barrier_semaphore()
        for dim, size in enumerate(self.dims):
            for step in range(1, size):
                pl.semaphore_signal(
                    barrier,
                    inc=1,
                    device_id=self.device(self.shifted(own, dim, step)),
                    device_id_type=MESH_ID,
                )
        pl.semaphore_wait(barrier, self.sends)


class GatherJob:
    def __init__(self, layout, own, order, shard, full, sems, columns=None):
        self.layout, self.own, self.order = layout, own, order
        self.shard, self.full, self.columns = shard, full, columns
        self.send_sems, self.recv_sems, self.local_sem = sems

    def block(self, digits, done):
        index = tuple(
            slice(None) if dim in done else digits[dim] for dim in range(len(self.layout.dims))
        )
        if self.columns is not None:
            index = index + (slice(None), pl.ds(*self.columns))
        return self.full.at[index]

    def piece(self):
        if self.columns is not None:
            return self.shard.at[:, pl.ds(*self.columns)]
        return self.shard

    def copies(self, stage, sending):
        dim, done = self.order[stage], self.order[:stage]
        base = self.layout.first_slot(self.order, stage)
        out = []
        for step in range(1, self.layout.dims[dim]):
            slot = base + step - 1
            other = self.layout.shifted(self.own, dim, step if sending else -step)
            target = self.block(self.own if sending else other, done)
            source = self.piece() if sending and stage == 0 else target
            out.append(
                pltpu.make_async_remote_copy(
                    src_ref=source,
                    dst_ref=target,
                    send_sem=self.send_sems.at[slot],
                    recv_sem=self.recv_sems.at[slot],
                    device_id=self.layout.device(other),
                    device_id_type=MESH_ID,
                )
            )
        return out

    def local(self):
        return pltpu.make_async_copy(self.piece(), self.block(self.own, ()), self.local_sem)

    def advance(self, stage):
        if stage == 0:
            self.local().start()
        else:
            for copy in self.copies(stage - 1, False):
                copy.wait_recv()
            if stage == 1:
                self.local().wait()
        if stage < len(self.order):
            for copy in self.copies(stage, True):
                copy.start()

    def finish(self):
        for stage in range(len(self.order)):
            for copy in self.copies(stage, True):
                copy.wait_send()


def run_rounds(jobs, stages, width=2):
    rounds = []
    last = stages + (len(jobs) - 1) // width
    for step in range(last + 1):
        todo = []
        for index, job in enumerate(jobs):
            stage = step - index // width
            if 0 <= stage <= stages:
                todo.append((job, stage))
        rounds.append(todo)
    return rounds


class Sidecar:
    def __init__(self, jobs, entries, stages, lag, place):
        self.jobs = jobs
        events = []
        for at, (job, entry) in enumerate(zip(jobs, entries)):
            for stage in range(stages + 1):
                events.append((entry + lag * stage, at, job, stage))
        events.sort(key=lambda event: event[:2])
        self.rounds = []
        for when, _, job, stage in events:
            here = place(when, events[-1][0])
            if not self.rounds or self.rounds[-1][0] != here:
                self.rounds.append((here, []))
            self.rounds[-1][1].append((job, stage))

    def visit(self, step, point):
        for place, todo in self.rounds:
            if place[1] == point:

                @pl.when(step == place[0])
                def _():
                    for job, stage in todo:
                        job.advance(stage)

    def finish(self):
        for job in self.jobs:
            job.finish()


def evenly(places):
    return lambda when, last: places[min(int(when * len(places) / last), len(places) - 1)]


class SumJob:
    def __init__(self, layout, own, start, lands, results, sems):
        self.layout, self.own, self.start = layout, own, start
        self.lands, self.results = lands, results
        self.send_sems, self.recv_sems = sems
        self.order = tuple(range(len(layout.dims)))

    def copies(self, stage):
        base = self.layout.first_slot(self.order, stage)
        source = self.start if stage == 0 else self.results[stage - 1]
        out = []
        for step in range(1, self.layout.dims[stage]):
            slot = base + step - 1
            out.append(
                pltpu.make_async_remote_copy(
                    src_ref=source,
                    dst_ref=self.lands.at[slot],
                    send_sem=self.send_sems.at[slot],
                    recv_sem=self.recv_sems.at[slot],
                    device_id=self.layout.device(self.layout.shifted(self.own, stage, step)),
                    device_id_type=MESH_ID,
                )
            )
        return out

    def advance(self, stage):
        if stage > 0:
            before = stage - 1
            value = self.start[...] if before == 0 else self.results[before - 1][...]
            base = self.layout.first_slot(self.order, before)
            for at, copy in enumerate(self.copies(before)):
                copy.wait_recv()
                value = value + self.lands[base + at]
            self.results[before][...] = value
        if stage < len(self.order):
            for copy in self.copies(stage):
                copy.start()

    def finish(self):
        for stage in range(len(self.order)):
            for copy in self.copies(stage):
                copy.wait_send()


class ScatterJob:
    def __init__(self, layout, own, order, part, sums, lands, result, sems, columns=None):
        self.layout, self.own, self.order = layout, own, order
        self.part, self.sums, self.lands, self.result = part, sums, lands, result
        self.send_sems, self.recv_sems, self.local_sem = sems
        self.columns = columns

    def tail(self):
        if self.columns is not None:
            return (slice(None), pl.ds(*self.columns))
        return ()

    def local(self):
        dim = self.order[0]
        index = [slice(None)] * len(self.layout.dims)
        index[dim] = self.own[dim]
        return pltpu.make_async_copy(
            self.part.at[tuple(index) + self.tail()], self.sums[0], self.local_sem
        )

    def copies(self, stage):
        dim = self.order[stage]
        base = self.layout.first_slot(self.order, stage)
        left = [d for d in range(len(self.layout.dims)) if d not in self.order[:stage]]
        out = []
        for step in range(1, self.layout.dims[dim]):
            slot = base + step - 1
            there = self.layout.shifted(self.own, dim, step)
            index = tuple(there[dim] if d == dim else slice(None) for d in left)
            if stage == 0:
                source = self.part.at[index + self.tail()]
            else:
                source = self.sums[stage - 1].at[index]
            out.append(
                pltpu.make_async_remote_copy(
                    src_ref=source,
                    dst_ref=self.lands[stage].at[step - 1],
                    send_sem=self.send_sems.at[slot],
                    recv_sem=self.recv_sems.at[slot],
                    device_id=self.layout.device(there),
                    device_id_type=MESH_ID,
                )
            )
        return out

    def add(self, stage):
        dim = self.order[stage]
        left = [d for d in range(len(self.layout.dims)) if d not in self.order[:stage]]
        rest = [d for d in left if d != dim]
        sizes = [self.layout.dims[d] for d in rest]
        total = 1
        for size in sizes:
            total *= size

        def body(flat):
            digits = []
            for size in reversed(sizes):
                digits.insert(0, flat % size)
                flat = flat // size
            if stage == 0:
                own_index = tuple(digits)
                value = self.sums[0][own_index].astype(jnp.float32)
            else:
                where = dict(zip(rest, digits))
                where[dim] = self.own[dim]
                value = self.sums[stage - 1][tuple(where[d] for d in left)].astype(jnp.float32)
            for step in range(1, self.layout.dims[dim]):
                value = value + self.lands[stage][(step - 1,) + tuple(digits)].astype(jnp.float32)
            if rest:
                target = self.sums[stage]
                target[tuple(digits)] = value.astype(target.dtype)
            elif self.columns is not None:
                self.result[:, pl.ds(*self.columns)] = value
            else:
                self.result[...] = value

        if total == 1:
            body(0)
        else:
            pl.loop(0, total)(body)

    def advance(self, stage):
        if stage == 0:
            self.local().start()
        else:
            for copy in self.copies(stage - 1):
                copy.wait_recv()
            if stage == 1:
                self.local().wait()
            self.add(stage - 1)
        if stage < len(self.order):
            for copy in self.copies(stage):
                copy.start()

    def finish(self):
        for stage in range(len(self.order)):
            for copy in self.copies(stage):
                copy.wait_send()


def scatter_buffers(layout, order, rows, columns, dtype):
    sums, lands = [], []
    for stage, dim in enumerate(order):
        rest = tuple(
            size for d, size in enumerate(layout.dims) if d not in order[: stage + 1]
        )
        lands.append(pltpu.VMEM((layout.dims[dim] - 1,) + rest + (rows, columns), dtype))
        if stage < len(order) - 1:
            sums.append(pltpu.VMEM(rest + (rows, columns), dtype))
    return sums + lands


ANYWHERE = pl.BlockSpec(memory_space=pltpu.HBM)


def job_sems(layout, plan):
    return [
        pltpu.SemaphoreType.DMA((len(plan), layout.sends)),
        pltpu.SemaphoreType.DMA((len(plan), layout.sends)),
        pltpu.SemaphoreType.DMA((len(plan),)),
    ]


def gather_jobs(layout, own, plan, shards, fulls, send_sems, recv_sems, local_sems):
    return [
        GatherJob(
            layout,
            own,
            layout.orders[way],
            shards[which],
            fulls[which],
            (send_sems.at[at], recv_sems.at[at], local_sems.at[at]),
            columns,
        )
        for at, (which, way, columns) in enumerate(plan)
    ]


def gather_shapes(layout, arrays):
    return [jax.ShapeDtypeStruct(layout.dims + a.shape, a.dtype) for a in arrays]


def scatter_jobs(layout, own, plan, parts, results, scratch, send_sems, recv_sems, local_sems):
    stages = len(layout.dims)
    buffers = 2 * stages - 1
    jobs = []
    for at, (which, way, columns) in enumerate(plan):
        mine = scratch[at * buffers : (at + 1) * buffers]
        jobs.append(
            ScatterJob(
                layout,
                own,
                layout.orders[way][::-1],
                parts[which],
                mine[: stages - 1],
                mine[stages - 1 :],
                results[which],
                (send_sems.at[at], recv_sems.at[at], local_sems.at[at]),
                columns,
            )
        )
    return jobs


def scatter_scratch(layout, plan, shapes):
    scratch = []
    for which, way, columns in plan:
        rows, width = shapes[which]
        width = width if columns is None else columns[1]
        scratch += scatter_buffers(layout, layout.orders[way][::-1], rows, width, jnp.bfloat16)
    return scratch


def gather_kernel(layout, plan, count, *refs):
    shards, fulls = refs[:count], refs[count : 2 * count]
    send_sems, recv_sems, local_sems = refs[2 * count :]
    own = layout.own()
    layout.greet(own)
    jobs = gather_jobs(layout, own, plan, shards, fulls, send_sems, recv_sems, local_sems)
    for todo in run_rounds(jobs, len(layout.dims), 4):
        for job, stage in todo:
            job.advance(stage)
    for job in jobs:
        job.finish()


def gather_all(layout, arrays, plan, collective_id):
    return pl.pallas_call(
        functools.partial(gather_kernel, layout, plan, len(arrays)),
        out_shape=gather_shapes(layout, arrays),
        in_specs=[ANYWHERE] * len(arrays),
        out_specs=[ANYWHERE] * len(arrays),
        scratch_shapes=job_sems(layout, plan),
        compiler_params=pltpu.CompilerParams(
            collective_id=collective_id, has_side_effects=True, vmem_limit_bytes=63 * MIB
        ),
    )(*arrays)


def cut(which, way, width, pieces):
    if width % (pieces * 128):
        return [(which, way, None)]
    step = width // pieces
    return [(which, way, (at * step, step)) for at in range(pieces)]


def weave(first, second):
    out = []
    for at in range(max(len(first), len(second))):
        out += first[at : at + 1] + second[at : at + 1]
    return out


def copy_kernel(count, *refs):
    for source, target in zip(refs[:count], refs[count:]):
        target[...] = source[...]


def copy_all(arrays):
    return pl.pallas_call(
        functools.partial(copy_kernel, len(arrays)),
        out_shape=[jax.ShapeDtypeStruct(a.shape, a.dtype) for a in arrays],
    )(*arrays)


def small_pack(layout, vectors):
    flat = jnp.concatenate([v.astype(jnp.float32).reshape(v.shape[0], -1) for v in vectors], 1)
    width = -(-flat.shape[1] // 1024) * 1024
    flat = jnp.pad(flat, ((0, 0), (0, width - flat.shape[1])))
    return flat.reshape(flat.shape[0], width // 128, 128)


def dot_plain(first_mat, second_mat):
    return jnp.dot(first_mat, second_mat, preferred_element_type=jnp.float32)


def dot_left_t(first_mat, second_mat):
    return lax.dot_general(
        first_mat, second_mat, (((0,), (0,)), ((), ())), preferred_element_type=jnp.float32
    )


def dot_right_t(first_mat, second_mat):
    return lax.dot_general(
        first_mat, second_mat, (((1,), (1,)), ((), ())), preferred_element_type=jnp.float32
    )


def row_mean(value):
    return jnp.sum(value, -1, keepdims=True) * (1.0 / value.shape[-1])


def norm_parts(row_data):
    centred = row_data - row_mean(row_data)
    inverse = lax.rsqrt(row_mean(centred * centred) + LN_EPS)
    return centred * inverse, inverse


def norm_backward(upstream, normed, inverse, gain_vec):
    scaled = upstream * gain_vec
    return inverse * (scaled - row_mean(scaled) - normed * row_mean(scaled * normed))


def column_sum(value):
    return jnp.sum(value, 0, keepdims=True)


def gelu_and_slope(inner_act):
    below = 0.5 * (1.0 + lax.erf(inner_act * 0.7071067811865476))
    bell = jnp.exp(-0.5 * inner_act * inner_act) * 0.3989422804014327
    return inner_act * below, below + inner_act * bell


LAG_OUT, LAG_IN = 1.5, 1.5
GROUP = 4
SPAN = GROUP * HEAD_DIM


def spread(rows, diag):
    return jnp.concatenate([rows] * GROUP, 0) * diag


def fold(square, seq_len):
    lane = lax.broadcasted_iota(jnp.int32, (seq_len, square.shape[1]), 1)
    out = square[:seq_len]
    for head in range(1, GROUP):
        block = square[head * seq_len : (head + 1) * seq_len]
        out = jnp.where(lane >= head * HEAD_DIM, block, out)
    return out


def probabilities(keys, wide_queries, length):
    scores = dot_right_t(keys, wide_queries) * HEAD_DIM ** (-0.5)
    at = lax.broadcasted_iota(jnp.int32, scores.shape, 0)
    scores = jnp.where(at < length, scores, MASKED)
    raised = jnp.exp(scores - jnp.max(scores, 0, keepdims=True))
    return raised * (1.0 / jnp.sum(raised, 0, keepdims=True))


def attend_kernel(
    layout,
    seq_len,
    plan,
    entries,
    count,
    steps,
    lengths_ref,
    x_ref,
    query_w,
    key_w,
    value_w,
    proj_w,
    vec_ref,
    diag_ref,
    *refs,
):
    shards, (q_ref, k_ref, v_ref, mix_ref, sum_ref, cls_ref) = refs[:count], refs[count : count + 6]
    fulls, sems = refs[count + 6 : 2 * count + 6], refs[2 * count + 6 :]
    rows, width = x_ref.shape
    held = rows // seq_len
    step = pl.program_id(0)
    first = step * held
    own = layout.own()

    @pl.when(step == 0)
    def _():
        layout.greet(own)

    jobs = gather_jobs(layout, own, plan, shards, fulls, *sems)
    places = [(at, point) for at in range(steps) for point in range(4)]
    sidecar = Sidecar(jobs, entries, len(layout.dims), LAG_OUT, evenly(places))
    sidecar.visit(step, 0)
    x = x_ref[...]
    q_ref[...] = (dot_plain(x, query_w[...]) + vec_ref[0:1, :]).astype(jnp.bfloat16)
    k_ref[...] = dot_plain(x, key_w[...]).astype(jnp.bfloat16)
    v_ref[...] = (dot_plain(x, value_w[...]) + vec_ref[1:2, :]).astype(jnp.bfloat16)
    diag = diag_ref[...]
    sidecar.visit(step, 1)

    def sentence(at):
        length = lengths_ref[first + at]
        here = pl.ds(at * seq_len, seq_len)
        for low in range(0, width, SPAN):
            cols = pl.ds(low, SPAN)
            wide = spread(q_ref[here, cols], diag)
            probs = probabilities(k_ref[here, cols], wide, length).astype(jnp.bfloat16)
            mixed = fold(dot_left_t(probs, v_ref[here, cols]), seq_len)
            mix_ref[here, cols] = mixed.astype(jnp.bfloat16)

    for at in range(held // 2):
        sentence(at)
    sidecar.visit(step, 2)
    for at in range(held // 2, held):
        sentence(at)
    sidecar.visit(step, 3)
    total = x.astype(jnp.float32) + dot_plain(mix_ref[...], proj_w[...]) + vec_ref[2:3, :]
    sum_ref[...] = total
    for at in range(held):
        cls_ref[0, at : at + 1, :] = total[at * seq_len : at * seq_len + 1]

    @pl.when(step == steps - 1)
    def _():
        sidecar.finish()


def whole(shape):
    return pl.BlockSpec(shape, lambda *_: (0,) * len(shape), pipeline_mode=pl.Buffered(1))


def attend(
    layout, x, lengths, weights, vec, diag, arrays, plan, entries, seq_len, rows, collective_id
):
    total, width = x.shape
    steps = total // rows
    held = rows // seq_len
    block = pl.BlockSpec((rows, width), lambda i: (i, 0))
    narrow = jax.ShapeDtypeStruct((total, width), jnp.bfloat16)
    return pl.pallas_call(
        functools.partial(attend_kernel, layout, seq_len, plan, entries, len(arrays), steps),
        grid=(steps,),
        out_shape=[
            narrow,
            narrow,
            narrow,
            narrow,
            jax.ShapeDtypeStruct((total, width), jnp.float32),
            jax.ShapeDtypeStruct((steps, held, width), jnp.float32),
        ]
        + gather_shapes(layout, arrays),
        in_specs=[pl.BlockSpec(memory_space=pltpu.SMEM), block]
        + [whole(w.shape) for w in weights]
        + [whole(vec.shape), whole(diag.shape)]
        + [ANYWHERE] * len(arrays),
        out_specs=[block] * 5
        + [pl.BlockSpec((1, held, width), lambda i: (i, 0, 0))]
        + [ANYWHERE] * len(arrays),
        scratch_shapes=job_sems(layout, plan),
        compiler_params=pltpu.CompilerParams(
            collective_id=collective_id, has_side_effects=True, vmem_limit_bytes=63 * MIB
        ),
    )(lengths, x, *weights, vec, diag, *arrays)


def feed_kernel(
    seq_len,
    blocks,
    pieces,
    sum_ref,
    tok_ref,
    mix_ref,
    cls_ref,
    inner_w,
    outer_w,
    vec_ref,
    bias_ref,
    out_ref,
    back_ref,
    inner_grad,
    outer_grad,
    proj_grad,
    vec_grad,
    bias_grad,
    slope,
    active,
    inner_b,
    hidden_b,
    second_b,
    proj_sum,
):
    step = pl.program_id(0)
    rows, width = sum_ref.shape
    piece = active.shape[2]

    @pl.when(step == 0)
    def _():
        vec_grad[...] = jnp.zeros_like(vec_grad)
        bias_grad[...] = jnp.zeros_like(bias_grad)
        proj_sum[...] = jnp.zeros_like(proj_sum)

    @pl.when(step < blocks)
    def _():
        here = pl.ds(pl.multiple_of(step * rows, rows), rows)
        gain_one, shift_one = vec_ref[3:4, :], vec_ref[4:5, :]
        gain_two, shift_two = vec_ref[6:7, :], vec_ref[7:8, :]
        normed_one, inverse_one = norm_parts(sum_ref[...])
        hidden = normed_one * gain_one + shift_one
        narrow = hidden.astype(jnp.bfloat16)
        hidden_b[here, :] = narrow
        second_sum = hidden + vec_ref[5:6, :]
        for at in range(pieces):
            cols = slice(at * piece, (at + 1) * piece)
            value, steep = gelu_and_slope(dot_plain(narrow, inner_w[:, cols]) + bias_ref[:, cols])
            value = value.astype(jnp.bfloat16)
            slope[at] = steep
            active[at, here, :] = value
            second_sum = second_sum + dot_plain(value, outer_w[cols, :])
        normed_two, inverse_two = norm_parts(second_sum)
        out_ref[...] = (normed_two * gain_two + shift_two).astype(jnp.bfloat16)
        grad = tok_ref[...].astype(jnp.float32).reshape(rows // seq_len, seq_len, width)
        place = lax.broadcasted_iota(jnp.int32, grad.shape, 1)
        extra = cls_ref[...].reshape(rows // seq_len, 1, width)
        grad = (grad + jnp.where(place == 0, extra, 0.0)).reshape(rows, width)
        vec_grad[6:7, :] += column_sum(grad * normed_two)
        vec_grad[7:8, :] += column_sum(grad)
        second = norm_backward(grad, normed_two, inverse_two, gain_two)
        vec_grad[5:6, :] += column_sum(second)
        narrow_two = second.astype(jnp.bfloat16)
        second_b[here, :] = narrow_two
        hidden_grad = second
        for at in range(pieces):
            cols = slice(at * piece, (at + 1) * piece)
            inner = dot_right_t(narrow_two, outer_w[cols, :]) * slope[at]
            bias_grad[:, cols] += column_sum(inner)
            inner = inner.astype(jnp.bfloat16)
            inner_b[at, here, :] = inner
            hidden_grad = hidden_grad + dot_right_t(inner, inner_w[:, cols])
        vec_grad[3:4, :] += column_sum(hidden_grad * normed_one)
        vec_grad[4:5, :] += column_sum(hidden_grad)
        first = norm_backward(hidden_grad, normed_one, inverse_one, gain_one)
        vec_grad[2:3, :] += column_sum(first)
        back_ref[...] = first
        proj_sum[...] += dot_left_t(mix_ref[...], first.astype(jnp.bfloat16))

        @pl.when(step == blocks - 1)
        def _():
            proj_grad[...] = proj_sum[...].astype(jnp.bfloat16)

    @pl.when(step >= blocks)
    def _():
        at = step - blocks
        outer_grad[...] = dot_left_t(active[at], second_b[...]).astype(jnp.bfloat16)
        inner_grad[...] = dot_left_t(hidden_b[...], inner_b[at]).astype(jnp.bfloat16)


def feed(
    first_sum, tokens_grad, mixture, cls_grad, inner_w, outer_w, vec, bias, seq_len, rows, piece
):
    total, width = first_sum.shape
    wide = inner_w.shape[1]
    blocks, pieces = total // rows, wide // piece
    held = rows // seq_len
    cls_grad = cls_grad.reshape(blocks, held, width)
    block = pl.BlockSpec((rows, width), lambda i: (jnp.minimum(i, blocks - 1), 0))
    return pl.pallas_call(
        functools.partial(feed_kernel, seq_len, blocks, pieces),
        grid=(blocks + pieces,),
        out_shape=[
            jax.ShapeDtypeStruct((total, width), jnp.bfloat16),
            jax.ShapeDtypeStruct((total, width), jnp.float32),
            jax.ShapeDtypeStruct(inner_w.shape, jnp.bfloat16),
            jax.ShapeDtypeStruct(outer_w.shape, jnp.bfloat16),
            jax.ShapeDtypeStruct((width, width), jnp.bfloat16),
            jax.ShapeDtypeStruct((8, width), jnp.float32),
            jax.ShapeDtypeStruct((1, wide), jnp.float32),
        ],
        in_specs=[
            block,
            block,
            block,
            pl.BlockSpec((1, held, width), lambda i: (jnp.minimum(i, blocks - 1), 0, 0)),
            whole(inner_w.shape),
            whole(outer_w.shape),
            whole(vec.shape),
            whole(bias.shape),
        ],
        out_specs=[
            block,
            block,
            pl.BlockSpec((width, piece), lambda i: (0, jnp.maximum(i - blocks, 0))),
            pl.BlockSpec((piece, width), lambda i: (jnp.maximum(i - blocks, 0), 0)),
            whole((width, width)),
            pl.BlockSpec((8, width), lambda i: (0, 0)),
            pl.BlockSpec((1, wide), lambda i: (0, 0)),
        ],
        scratch_shapes=[
            pltpu.VMEM((pieces, rows, piece), jnp.float32),
            pltpu.VMEM((pieces, total, piece), jnp.bfloat16),
            pltpu.VMEM((pieces, total, piece), jnp.bfloat16),
            pltpu.VMEM((total, width), jnp.bfloat16),
            pltpu.VMEM((total, width), jnp.bfloat16),
            pltpu.VMEM((width, width), jnp.float32),
        ],
        compiler_params=pltpu.CompilerParams(vmem_limit_bytes=63 * MIB),
    )(first_sum, tokens_grad, mixture, cls_grad, inner_w, outer_w, vec, bias)


def unflat(flat, dims):
    digits = []
    for size in reversed(dims):
        digits.insert(0, flat % size)
        flat = flat // size
    return tuple(digits)


def back_kernel(
    layout,
    seq_len,
    blocks,
    plan,
    entries,
    count,
    lengths_ref,
    x_ref,
    q_ref,
    k_ref,
    v_ref,
    first_ref,
    query_w,
    key_w,
    value_w,
    proj_w,
    diag_ref,
    feed_vec,
    feed_bias,
    pool_vec,
    *refs,
):
    step = pl.program_id(0)
    rows, width = x_ref.shape
    held = rows // seq_len
    scale = HEAD_DIM ** (-0.5)
    stages = len(layout.dims)
    parts, refs = refs[:count], refs[count:]
    (in_ref, vec_sum), refs = refs[:2], refs[2:]
    sums, refs = refs[: count + 3], refs[count + 3 :]
    (x_all, dq_all, dk_all, dv_all, dmix), refs = refs[:5], refs[5:]
    own_parts, refs = refs[:3], refs[3:]
    (vec_grad, vec_lands), refs = refs[:2], refs[2:]
    vec_steps, refs = refs[: stages - 1], refs[stages - 1 :]
    own = layout.own()
    vec_job = SumJob(layout, own, vec_grad, vec_lands, tuple(vec_steps) + (vec_sum,), refs[-2:])
    jobs = scatter_jobs(layout, own, plan, parts + own_parts, sums, refs[:-5], *refs[-5:-2])

    own_at = sorted({entry for entry, job in zip(entries, plan) if job[0] >= count})

    def place(when, last):
        if when < own_at[0]:
            half = int(when * 2 * blocks / own_at[0])
            return (half // 2, half % 2)
        for at, entry in enumerate(own_at):
            if when <= entry:
                return (blocks + at, 1)
        half = int((when - own_at[-1]) * blocks / (last - own_at[-1]))
        return (blocks + 3 + half, 0) if half < blocks else (2 * blocks + 2, 1)

    last_entry = max(entries)
    sidecar = Sidecar(jobs + [vec_job], list(entries) + [last_entry], stages, LAG_IN, place)

    @pl.when(step == 0)
    def _():
        layout.greet(own)
        vec_grad[0:2, :] = jnp.zeros_like(vec_grad[0:2, :])
        vec_grad[2:8, :] = feed_vec[2:8, :]
        vec_grad[8:9, :] = pool_vec[...]
        pieces = feed_bias.shape[1] // width
        vec_grad[9:, :] = jnp.zeros_like(vec_grad[9:, :])
        for at in range(pieces):
            vec_grad[9 + at : 10 + at, :] = feed_bias[:, at * width : (at + 1) * width]

    @pl.when(step < blocks)
    def _():
        here = pl.ds(pl.multiple_of(step * rows, rows), rows)
        sidecar.visit(step, 0)
        x_all[here, :] = x_ref[...]
        narrow = first_ref[...].astype(jnp.bfloat16)
        dmix[...] = dot_right_t(narrow, proj_w[...]).astype(jnp.bfloat16)
        diag = diag_ref[...]

        def sentence(at):
            length = lengths_ref[step * held + at]
            near = pl.ds(at * seq_len, seq_len)
            far = pl.ds(pl.multiple_of(step * rows + at * seq_len, seq_len), seq_len)
            for low in range(0, width, SPAN):
                cols = pl.ds(low, SPAN)
                keys = k_ref[near, cols]
                wide = spread(q_ref[near, cols], diag)
                wide_grad = spread(dmix[near, cols], diag)
                probs = probabilities(keys, wide, length)
                prob_grad = dot_right_t(v_ref[near, cols], wide_grad)
                dv_all[far, cols] = dot_plain(probs.astype(jnp.bfloat16), wide_grad).astype(
                    jnp.bfloat16
                )
                score_grad = probs * (prob_grad - column_sum(prob_grad * probs))
                score_grad = score_grad.astype(jnp.bfloat16)
                dk_all[far, cols] = (dot_plain(score_grad, wide) * scale).astype(jnp.bfloat16)
                dq_all[far, cols] = (fold(dot_left_t(score_grad, keys), seq_len) * scale).astype(
                    jnp.bfloat16
                )

        for at in range(held // 2):
            sentence(at)
        sidecar.visit(step, 1)
        for at in range(held // 2, held):
            sentence(at)
        vec_grad[0:1, :] += column_sum(dq_all[here, :].astype(jnp.float32))
        vec_grad[1:2, :] += column_sum(dv_all[here, :].astype(jnp.float32))

    for at, (right, part) in enumerate(zip((dq_all, dk_all, dv_all), own_parts)):

        @pl.when(step == blocks + at)
        def _():
            value = dot_left_t(x_all[...], right[...])
            share = part.shape[-2]
            for device in range(layout.count):
                piece = value[device * share : (device + 1) * share]
                part[unflat(device, layout.dims)] = piece.astype(jnp.bfloat16)
            sidecar.visit(step, 1)

    @pl.when(step >= blocks + 3)
    def _():
        sidecar.visit(step, 0)
        here = pl.ds(pl.multiple_of((step - blocks - 3) * rows, rows), rows)
        in_ref[...] = (
            first_ref[...]
            + dot_right_t(dq_all[here, :], query_w[...])
            + dot_right_t(dk_all[here, :], key_w[...])
            + dot_right_t(dv_all[here, :], value_w[...])
        )
        sidecar.visit(step, 1)

    @pl.when(step == 2 * blocks + 2)
    def _():
        sidecar.finish()


def back(
    layout,
    x,
    lengths,
    saved,
    first_grad,
    weights,
    diag,
    vectors,
    arrays,
    plan,
    entries,
    seq_len,
    rows,
    collective_id,
):
    total, width = x.shape
    blocks = total // rows
    stages = len(layout.dims)
    share = width // layout.count
    shapes = [a.shape[-2:] for a in arrays] + [(share, width)] * 3
    block = pl.BlockSpec((rows, width), lambda i: (jnp.minimum(i, blocks - 1), 0))
    twice = pl.BlockSpec(
        (rows, width),
        lambda i: (jnp.where(i < blocks, i, jnp.maximum(i - blocks - 3, 0)), 0),
    )
    out_block = pl.BlockSpec((rows, width), lambda i: (jnp.maximum(i - blocks - 3, 0), 0))
    small = pltpu.VMEM((16, width), jnp.float32)
    return pl.pallas_call(
        functools.partial(back_kernel, layout, seq_len, blocks, plan, entries, len(arrays)),
        grid=(2 * blocks + 3,),
        out_shape=[
            jax.ShapeDtypeStruct((total, width), jnp.float32),
            jax.ShapeDtypeStruct((16, width), jnp.float32),
        ]
        + [jax.ShapeDtypeStruct(s, jnp.float32) for s in shapes],
        in_specs=[pl.BlockSpec(memory_space=pltpu.SMEM)]
        + [block] * 4
        + [twice]
        + [whole(w.shape) for w in weights]
        + [whole(diag.shape)]
        + [whole(v.shape) for v in vectors]
        + [ANYWHERE] * len(arrays),
        out_specs=[out_block, whole((16, width))] + [whole(s) for s in shapes],
        scratch_shapes=[pltpu.VMEM((total, width), jnp.bfloat16)] * 4
        + [pltpu.VMEM((rows, width), jnp.bfloat16)]
        + [pltpu.VMEM(layout.dims + (share, width), jnp.bfloat16)] * 3
        + [small, pltpu.VMEM((layout.sends, 16, width), jnp.float32)]
        + [small] * (stages - 1)
        + scatter_scratch(layout, plan, shapes)
        + job_sems(layout, plan)
        + [pltpu.SemaphoreType.DMA((layout.sends,))] * 2,
        compiler_params=pltpu.CompilerParams(
            collective_id=collective_id, has_side_effects=True, vmem_limit_bytes=63 * MIB
        ),
    )(lengths, x, *saved, first_grad, *weights, diag, *vectors, *arrays)


def rank_kernel(
    layout,
    micros,
    node_dev,
    steps,
    sum_ref,
    inner_w,
    outer_w,
    pool_w,
    vec_ref,
    bias_ref,
    node_ref,
    cls_grad,
    pool_grad,
    shift_grad,
    hidden,
    total,
    mine,
    units,
    node_cols,
    totals,
    send_sems,
    recv_sems,
    local_sems,
):
    step = pl.program_id(0)
    sentences, width = sum_ref.shape
    own = layout.own()

    @pl.when(step == 0)
    def _():
        layout.greet(own)
        normed, _ = norm_parts(sum_ref[...])
        start = normed * vec_ref[3:4, :] + vec_ref[4:5, :]
        hidden[...] = start.astype(jnp.bfloat16)
        total[...] = start + vec_ref[5:6, :]
        node_cols[...] = node_ref[...].T

    value, _ = gelu_and_slope(dot_plain(hidden[...], inner_w[...]) + bias_ref[...])
    total[...] += dot_plain(value.astype(jnp.bfloat16), outer_w[...])

    @pl.when(step == steps - 1)
    def _():
        normed, _ = norm_parts(total[...])
        cls_rows = (normed * vec_ref[6:7, :] + vec_ref[7:8, :]).astype(jnp.bfloat16)
        pooled = jnp.tanh(dot_plain(cls_rows, pool_w[...]) + vec_ref[8:9, :])
        scale_inv = lax.rsqrt(jnp.sum(pooled * pooled, -1, keepdims=True) + UNIT_EPS)
        unit = pooled * scale_inv
        mine[...] = unit.astype(jnp.bfloat16)
        step_cols = width // len(layout.orders)
        plan = [(0, way, (way * step_cols, step_cols)) for way in range(len(layout.orders))]
        jobs = gather_jobs(layout, own, plan, [mine], [units], send_sems, recv_sems, local_sems)
        for stage in range(len(layout.dims) + 1):
            for job in jobs:
                job.advance(stage)
        for job in jobs:
            job.finish()

        device = own[0]
        for size, digit in zip(layout.dims[1:], own[1:]):
            device = device * size + digit
        at_home = pl.ds(pl.multiple_of(device * node_dev, node_dev), node_dev)
        count = layout.count * node_dev
        band = min(count, 512)
        every = units[...].reshape(layout.count, sentences, width)
        grads = []

        def scored(similar, tongue, place, side, tongue_row, place_row, side_row):
            across = side != side_row
            include = across & (tongue == tongue_row)
            positive = jnp.where(across & (place == place_row), 1.0, 0.0)
            return (
                jnp.where(include, SIM_SCALE * similar - SIM_SCALE * MARGIN * positive, MASKED),
                include,
                positive,
            )

        half = node_dev // 2

        def sides(shape, dim, offset):
            return (lax.broadcasted_iota(jnp.int32, shape, dim) + offset) // half % 2

        for micro in range(micros):
            here = slice(micro * node_dev, (micro + 1) * node_dev)
            nodes = every[:, here, :].reshape(count, width)
            tongue, place = node_cols[:, 2 * micro : 2 * micro + 1], node_cols[
                :, 2 * micro + 1 : 2 * micro + 2
            ]
            for low in range(0, count, band):
                cols = slice(low, low + band)
                similar = dot_right_t(nodes, nodes[cols])
                value, _, _ = scored(
                    similar,
                    tongue,
                    place,
                    sides((count, 1), 0, 0),
                    node_ref[2 * micro : 2 * micro + 1, cols],
                    node_ref[2 * micro + 1 : 2 * micro + 2, cols],
                    sides((1, band), 1, low),
                )
                peak = jnp.max(value, 0, keepdims=True)
                totals[:, cols] = jnp.log(column_sum(jnp.exp(value - peak))) + peak
            value, include, positive = scored(
                dot_right_t(mine[here, :], nodes),
                node_cols[at_home, 2 * micro : 2 * micro + 1],
                node_cols[at_home, 2 * micro + 1 : 2 * micro + 2],
                sides((node_dev, 1), 0, 0),
                node_ref[2 * micro : 2 * micro + 1, :],
                node_ref[2 * micro + 1 : 2 * micro + 2, :],
                sides((1, count), 1, 0),
            )
            peak = jnp.max(value, -1, keepdims=True)
            line = jnp.log(jnp.sum(jnp.exp(value - peak), -1, keepdims=True)) + peak
            grad_sim = jnp.where(
                include, jnp.exp(value - line) + jnp.exp(value - totals[...]), 0.0
            )
            grad_sim = (grad_sim - 2.0 * positive).astype(jnp.bfloat16)
            grads.append(SIM_SCALE * dot_plain(grad_sim, nodes))
        unit_grad = jnp.concatenate(grads, 0)
        pooled_grad = scale_inv * (
            unit_grad - unit * jnp.sum(unit_grad * unit, -1, keepdims=True)
        )
        pre_grad = pooled_grad * (1.0 - pooled * pooled)
        narrow = pre_grad.astype(jnp.bfloat16)
        pool_grad[...] = dot_left_t(cls_rows, narrow).astype(jnp.bfloat16)
        shift_grad[...] = column_sum(pre_grad)
        cls_grad[...] = dot_right_t(narrow, pool_w[...])


def rank(layout, cls_sum, inner_w, outer_w, pool_w, vec, bias, nodes, micros, piece, collective_id):
    sentences, width = cls_sum.shape
    wide = inner_w.shape[1]
    steps = wide // piece
    node_dev = sentences // micros
    return pl.pallas_call(
        functools.partial(rank_kernel, layout, micros, node_dev, steps),
        grid=(steps,),
        out_shape=[
            jax.ShapeDtypeStruct((sentences, width), jnp.float32),
            jax.ShapeDtypeStruct((width, width), jnp.bfloat16),
            jax.ShapeDtypeStruct((1, width), jnp.float32),
        ],
        in_specs=[
            whole(cls_sum.shape),
            pl.BlockSpec((width, piece), lambda i: (0, i)),
            pl.BlockSpec((piece, width), lambda i: (i, 0)),
            whole(pool_w.shape),
            whole(vec.shape),
            pl.BlockSpec((1, piece), lambda i: (0, i)),
            whole(nodes.shape),
        ],
        out_specs=[
            pl.BlockSpec((sentences, width), lambda i: (0, 0)),
            pl.BlockSpec((width, width), lambda i: (0, 0)),
            pl.BlockSpec((1, width), lambda i: (0, 0)),
        ],
        scratch_shapes=[
            pltpu.VMEM((sentences, width), jnp.bfloat16),
            pltpu.VMEM((sentences, width), jnp.float32),
            pltpu.VMEM((sentences, width), jnp.bfloat16),
            pltpu.VMEM(layout.dims + (sentences, width), jnp.bfloat16),
            pltpu.VMEM((nodes.shape[1], nodes.shape[0]), jnp.float32),
            pltpu.VMEM((1, nodes.shape[1]), jnp.float32),
        ]
        + job_sems(layout, layout.orders),
        compiler_params=pltpu.CompilerParams(
            collective_id=collective_id, has_side_effects=True, vmem_limit_bytes=63 * MIB
        ),
    )(cls_sum, inner_w, outer_w, pool_w, vec, bias, nodes)


def on_device(
    layout,
    hidden_in,
    lengths,
    partner,
    language,
    token_cotangent,
    query_weight,
    key_weight,
    value_weight,
    attn_out_weight,
    query_bias,
    value_bias,
    attn_out_bias,
    ln1_gain,
    ln1_shift,
    in_weight,
    in_bias,
    out_weight,
    out_bias,
    ln2_gain,
    ln2_shift,
    pool_weight,
    pool_bias,
):
    micro_count, sides, pair_dev, seq_len, model_width = hidden_in.shape
    inner_width = in_weight.shape[1]
    count = layout.count
    node_dev = sides * pair_dev
    sent_count = micro_count * node_dev
    row_count = sent_count * seq_len
    pair_count = partner.shape[1]
    device = lax.axis_index("dp") * (count // layout.slow) + lax.axis_index("fsdp")

    vectors = (
        query_bias,
        value_bias,
        attn_out_bias,
        ln1_gain,
        ln1_shift,
        out_bias,
        ln2_gain,
        ln2_shift,
        pool_bias,
        in_bias,
    )
    small = small_pack(layout, [v[None] for v in vectors])[0]
    arrays = [query_weight, key_weight, value_weight, attn_out_weight, small]
    plan = [(4, 0, None)]
    plan += weave(cut(0, 0, model_width, 2), cut(1, 1, model_width, 2))
    plan += weave(cut(2, 0, model_width, 2), cut(3, 1, model_width, 2))
    gathered = gather_all(layout, arrays, tuple(plan), 0)

    def joined(full, array):
        return full.reshape((count * array.shape[0],) + array.shape[1:])

    *weights, small_full = map(joined, gathered, arrays)
    small_rows = small_full.reshape(count, -1)
    share = query_bias.shape[0]
    rows_of = len(vectors) - 1
    vec = small_rows[:, : rows_of * share].reshape(count, rows_of, share)
    vec = jnp.moveaxis(vec, 1, 0).reshape(rows_of, model_width)
    vec = jnp.pad(vec, ((0, 16 - rows_of), (0, 0)))
    bias = small_rows[:, rows_of * share : rows_of * share + in_bias.shape[0]]
    bias = bias.reshape(1, inner_width)

    pair_ids = jnp.arange(pair_count, dtype=jnp.int32)
    hit = partner[:, :, None] == pair_ids[None, None, :]
    target_language = jnp.sum(jnp.where(hit, language[:, :, None], 0), 1)

    def split(value):
        return value.reshape(micro_count, count, 1, pair_dev)

    node_rows = jnp.stack(
        [
            jnp.concatenate([split(language), split(target_language)], 2),
            jnp.concatenate(
                [split(partner), split(jnp.broadcast_to(pair_ids, partner.shape))], 2
            ),
        ],
        1,
    )
    node_rows = node_rows.reshape(2 * micro_count, count * node_dev).astype(jnp.float32)
    node_rows = jnp.pad(node_rows, ((0, -2 * micro_count % 8), (0, 0)))
    block_at = jnp.arange(SPAN) // HEAD_DIM
    diag = (block_at[:, None] == block_at[None, :]).astype(jnp.bfloat16)

    x = hidden_in.reshape(row_count, model_width)
    sent_lengths = lengths.reshape(sent_count)
    arrays = [in_weight, out_weight, pool_weight]

    def halves(which):
        return cut(which, 0, model_width, 2)[:1] + cut(which, 1, model_width, 2)[1:]

    first_cuts, second_cuts = cut(0, 0, inner_width, 8), cut(1, 1, model_width, 6)
    plan = weave(first_cuts[:6], second_cuts)
    plan += weave(first_cuts[6:], halves(2))
    entries = tuple(at // 2 for at in range(len(plan)))
    queries, keys, values, mixture, first_sum, cls_sum, *gathered = attend(
        layout, x, sent_lengths, weights, vec, diag, arrays, tuple(plan), entries, seq_len, 512, 1
    )
    inner_full, outer_full, pool_full = map(joined, gathered, arrays)
    cls_grad, grad_pool, grad_pool_shift = rank(
        layout,
        cls_sum.reshape(sent_count, model_width),
        inner_full,
        outer_full,
        pool_full,
        vec,
        bias,
        node_rows,
        micro_count,
        384,
        2,
    )
    block_out, first_grad, grad_inner, grad_outer, grad_proj, vec_grad, grad_bias = feed(
        first_sum,
        token_cotangent.reshape(row_count, model_width),
        mixture,
        cls_grad,
        inner_full,
        outer_full,
        vec,
        bias,
        seq_len,
        256,
        768,
    )

    def apart(part):
        return part.reshape(layout.dims + (-1, part.shape[1]))

    parts = list(map(apart, (grad_inner, grad_outer, grad_pool, grad_proj)))
    plan = weave(first_cuts[:6], second_cuts)
    plan += weave(first_cuts[6:], halves(2)[::-1]) + halves(3)
    entries = [at // 2 for at in range(len(plan))]
    for which in (4, 5, 6):
        entries += [entries[-1] + 1] * 2
        plan += halves(which)
    input_grad, vec_sum, *sums = back(
        layout,
        x,
        sent_lengths,
        (queries, keys, values),
        first_grad,
        weights,
        diag,
        (vec_grad, grad_bias, grad_pool_shift),
        parts,
        tuple(plan),
        tuple(entries),
        seq_len,
        256,
        3,
    )
    block_out = block_out.reshape(hidden_in.shape)
    input_grad = input_grad.reshape(hidden_in.shape)
    sums = copy_all(sums)
    vec_own = lax.dynamic_slice_in_dim(vec_sum[:rows_of], device * share, share, 1)
    bias_sum = vec_sum[rows_of : rows_of + inner_width // model_width].reshape(-1)
    bias_own = lax.dynamic_slice_in_dim(bias_sum, device * in_bias.shape[0], in_bias.shape[0])
    (
        sum_query_shift,
        sum_value_shift,
        sum_proj_shift,
        sum_gain_one,
        sum_shift_one,
        sum_outer_shift,
        sum_gain_two,
        sum_shift_two,
        sum_pool_shift,
    ) = vec_own
    return (
        block_out,
        input_grad,
        sums[4],
        sums[5],
        sums[6],
        sums[3],
        sum_query_shift,
        sum_value_shift,
        sum_proj_shift,
        sum_gain_one,
        sum_shift_one,
        sums[0],
        bias_own,
        sums[1],
        sum_outer_shift,
        sum_gain_two,
        sum_shift_two,
        sums[2],
        sum_pool_shift,
    )


def solution(mesh):
    rows = P(("dp", "fsdp"), None)
    vector = P(("dp", "fsdp"))
    sentences = P(None, None, ("dp", "fsdp"), None, None)
    placed = (
        (sentences, P(None, None, ("dp", "fsdp")), P(), P(), sentences)
        + (rows,) * 4
        + (vector,) * 5
        + (rows, vector, rows)
        + (vector,) * 3
        + (rows, vector)
    )
    return jax.shard_map(
        functools.partial(on_device, Layout(mesh.shape)),
        mesh=mesh,
        in_specs=placed,
        out_specs=(sentences, sentences)
        + (rows,) * 4
        + (vector,) * 5
        + (rows, vector, rows)
        + (vector,) * 3
        + (rows, vector),
        check_vma=False,
    )
```

```python
import functools

import jax
import jax.numpy as jnp
from jax import lax
from jax.experimental import pallas as pl
from jax.experimental.pallas import tpu as pltpu
from jax.sharding import PartitionSpec as P

HEAD_DIM = 64


LN_EPS = 1e-06
UNIT_EPS = 1e-06
SIM_SCALE = 10.0
MARGIN = 0.3
MASKED = -1e30
MIB = 1024 * 1024


MESH_ID = pl.DeviceIdType.MESH
AXES = ("dp", "fsdp")


class Layout:
    def __init__(self, mesh_shape):
        slow, fast = mesh_shape["dp"], mesh_shape["fsdp"]
        self.slow, self.count = slow, slow * fast
        if slow == 8:
            self.dims = (2, 2, 2, fast)
            self.orders = ((3, 1, 0, 2), (3, 0, 1, 2))
        else:
            self.dims = (slow, fast)
            self.orders = ((1, 0), (1, 0))
        self.sends = sum(size - 1 for size in self.dims)

    def own(self):
        digits = [lax.axis_index("fsdp")]
        rest = lax.axis_index("dp")
        for size in self.dims[-2::-1]:
            digits.insert(0, rest % size)
            rest = rest // size
        return digits

    def device(self, digits):
        slow = digits[0]
        for size, digit in zip(self.dims[1:-1], digits[1:-1]):
            slow = slow * size + digit
        return (slow, digits[-1])

    def shifted(self, own, dim, step):
        size = self.dims[dim]
        out = list(own)
        out[dim] = (own[dim] + step) % size
        return out

    def first_slot(self, order, stage):
        return sum(self.dims[dim] - 1 for dim in order[:stage])

    def greet(self, own):
        barrier = pltpu.get_barrier_semaphore()
        for dim, size in enumerate(self.dims):
            for step in range(1, size):
                pl.semaphore_signal(
                    barrier,
                    inc=1,
                    device_id=self.device(self.shifted(own, dim, step)),
                    device_id_type=MESH_ID,
                )
        pl.semaphore_wait(barrier, self.sends)


class GatherJob:
    def __init__(self, layout, own, order, shard, full, sems, columns=None):
        self.layout, self.own, self.order = layout, own, order
        self.shard, self.full, self.columns = shard, full, columns
        self.send_sems, self.recv_sems, self.local_sem = sems

    def block(self, digits, done):
        index = tuple(
            slice(None) if dim in done else digits[dim] for dim in range(len(self.layout.dims))
        )
        if self.columns is not None:
            index = index + (slice(None), pl.ds(*self.columns))
        return self.full.at[index]

    def piece(self):
        if self.columns is not None:
            return self.shard.at[:, pl.ds(*self.columns)]
        return self.shard

    def copies(self, stage, sending):
        dim, done = self.order[stage], self.order[:stage]
        base = self.layout.first_slot(self.order, stage)
        out = []
        for step in range(1, self.layout.dims[dim]):
            slot = base + step - 1
            other = self.layout.shifted(self.own, dim, step if sending else -step)
            target = self.block(self.own if sending else other, done)
            source = self.piece() if sending and stage == 0 else target
            out.append(
                pltpu.make_async_remote_copy(
                    src_ref=source,
                    dst_ref=target,
                    send_sem=self.send_sems.at[slot],
                    recv_sem=self.recv_sems.at[slot],
                    device_id=self.layout.device(other),
                    device_id_type=MESH_ID,
                )
            )
        return out

    def local(self):
        return pltpu.make_async_copy(self.piece(), self.block(self.own, ()), self.local_sem)

    def advance(self, stage):
        if stage == 0:
            self.local().start()
        else:
            for copy in self.copies(stage - 1, False):
                copy.wait_recv()
            if stage == 1:
                self.local().wait()
        if stage < len(self.order):
            for copy in self.copies(stage, True):
                copy.start()

    def finish(self):
        for stage in range(len(self.order)):
            for copy in self.copies(stage, True):
                copy.wait_send()


def run_rounds(jobs, stages, width=2):
    rounds = []
    last = stages + (len(jobs) - 1) // width
    for step in range(last + 1):
        todo = []
        for index, job in enumerate(jobs):
            stage = step - index // width
            if 0 <= stage <= stages:
                todo.append((job, stage))
        rounds.append(todo)
    return rounds


class Sidecar:
    def __init__(self, jobs, entries, stages, offsets, place):
        self.jobs = jobs
        events = []
        for at, (job, entry) in enumerate(zip(jobs, entries)):
            for stage in range(stages + 1):
                after = offsets[stage] if len(offsets) == stages + 1 else 1.5 * stage
                events.append((entry + after, at, job, stage))
        events.sort(key=lambda event: event[:2])
        self.rounds = []
        for when, _, job, stage in events:
            here = place(when, events[-1][0])
            if not self.rounds or self.rounds[-1][0] != here:
                self.rounds.append((here, []))
            self.rounds[-1][1].append((job, stage))

    def visit(self, step, point):
        for place, todo in self.rounds:
            if place[1] == point:

                @pl.when(step == place[0])
                def _():
                    for job, stage in todo:
                        job.advance(stage)

    def finish(self):
        for job in self.jobs:
            job.finish()


def evenly(places):
    return lambda when, last: places[min(int(when * len(places) / last), len(places) - 1)]


class SumJob:
    def __init__(self, layout, own, start, lands, results, sems):
        self.layout, self.own, self.start = layout, own, start
        self.lands, self.results = lands, results
        self.send_sems, self.recv_sems = sems
        self.order = tuple(range(len(layout.dims)))

    def copies(self, stage):
        base = self.layout.first_slot(self.order, stage)
        source = self.start if stage == 0 else self.results[stage - 1]
        out = []
        for step in range(1, self.layout.dims[stage]):
            slot = base + step - 1
            out.append(
                pltpu.make_async_remote_copy(
                    src_ref=source,
                    dst_ref=self.lands.at[slot],
                    send_sem=self.send_sems.at[slot],
                    recv_sem=self.recv_sems.at[slot],
                    device_id=self.layout.device(self.layout.shifted(self.own, stage, step)),
                    device_id_type=MESH_ID,
                )
            )
        return out

    def advance(self, stage):
        if stage > 0:
            before = stage - 1
            value = self.start[...] if before == 0 else self.results[before - 1][...]
            base = self.layout.first_slot(self.order, before)
            for at, copy in enumerate(self.copies(before)):
                copy.wait_recv()
                value = value + self.lands[base + at]
            self.results[before][...] = value
        if stage < len(self.order):
            for copy in self.copies(stage):
                copy.start()

    def finish(self):
        for stage in range(len(self.order)):
            for copy in self.copies(stage):
                copy.wait_send()


class ScatterJob:
    def __init__(self, layout, own, order, part, sums, lands, result, sems, columns=None):
        self.layout, self.own, self.order = layout, own, order
        self.part, self.sums, self.lands, self.result = part, sums, lands, result
        self.send_sems, self.recv_sems, self.local_sem = sems
        self.columns = columns

    def tail(self):
        if self.columns is not None:
            return (slice(None), pl.ds(*self.columns))
        return ()

    def local(self):
        dim = self.order[0]
        index = [slice(None)] * len(self.layout.dims)
        index[dim] = self.own[dim]
        return pltpu.make_async_copy(
            self.part.at[tuple(index) + self.tail()], self.sums[0], self.local_sem
        )

    def copies(self, stage):
        dim = self.order[stage]
        base = self.layout.first_slot(self.order, stage)
        left = [d for d in range(len(self.layout.dims)) if d not in self.order[:stage]]
        out = []
        for step in range(1, self.layout.dims[dim]):
            slot = base + step - 1
            there = self.layout.shifted(self.own, dim, step)
            index = tuple(there[dim] if d == dim else slice(None) for d in left)
            if stage == 0:
                source = self.part.at[index + self.tail()]
            else:
                source = self.sums[stage - 1].at[index]
            out.append(
                pltpu.make_async_remote_copy(
                    src_ref=source,
                    dst_ref=self.lands[stage].at[step - 1],
                    send_sem=self.send_sems.at[slot],
                    recv_sem=self.recv_sems.at[slot],
                    device_id=self.layout.device(there),
                    device_id_type=MESH_ID,
                )
            )
        return out

    def add(self, stage):
        dim = self.order[stage]
        left = [d for d in range(len(self.layout.dims)) if d not in self.order[:stage]]
        rest = [d for d in left if d != dim]
        sizes = [self.layout.dims[d] for d in rest]
        total = 1
        for size in sizes:
            total *= size

        def body(flat):
            digits = []
            for size in reversed(sizes):
                digits.insert(0, flat % size)
                flat = flat // size
            if stage == 0:
                own_index = tuple(digits)
                value = self.sums[0][own_index].astype(jnp.float32)
            else:
                where = dict(zip(rest, digits))
                where[dim] = self.own[dim]
                value = self.sums[stage - 1][tuple(where[d] for d in left)].astype(jnp.float32)
            for step in range(1, self.layout.dims[dim]):
                value = value + self.lands[stage][(step - 1,) + tuple(digits)].astype(jnp.float32)
            if rest:
                target = self.sums[stage]
                target[tuple(digits)] = value.astype(target.dtype)
            elif self.columns is not None:
                self.result[:, pl.ds(*self.columns)] = value
            else:
                self.result[...] = value

        if total == 1:
            body(0)
        else:
            pl.loop(0, total)(body)

    def advance(self, stage):
        if stage == 0:
            self.local().start()
        else:
            for copy in self.copies(stage - 1):
                copy.wait_recv()
            if stage == 1:
                self.local().wait()
            self.add(stage - 1)
        if stage < len(self.order):
            for copy in self.copies(stage):
                copy.start()

    def finish(self):
        for stage in range(len(self.order)):
            for copy in self.copies(stage):
                copy.wait_send()


def scatter_buffers(layout, order, rows, columns, dtype):
    sums, lands = [], []
    for stage, dim in enumerate(order):
        rest = tuple(
            size for d, size in enumerate(layout.dims) if d not in order[: stage + 1]
        )
        lands.append(pltpu.VMEM((layout.dims[dim] - 1,) + rest + (rows, columns), dtype))
        if stage < len(order) - 1:
            sums.append(pltpu.VMEM(rest + (rows, columns), dtype))
    return sums + lands


ANYWHERE = pl.BlockSpec(memory_space=pltpu.HBM)


def job_sems(layout, plan):
    return [
        pltpu.SemaphoreType.DMA((len(plan), layout.sends)),
        pltpu.SemaphoreType.DMA((len(plan), layout.sends)),
        pltpu.SemaphoreType.DMA((len(plan),)),
    ]


def gather_jobs(layout, own, plan, shards, fulls, send_sems, recv_sems, local_sems):
    return [
        GatherJob(
            layout,
            own,
            layout.orders[way],
            shards[which],
            fulls[which],
            (send_sems.at[at], recv_sems.at[at], local_sems.at[at]),
            columns,
        )
        for at, (which, way, columns) in enumerate(plan)
    ]


def gather_shapes(layout, arrays):
    return [jax.ShapeDtypeStruct(layout.dims + a.shape, a.dtype) for a in arrays]


def scatter_jobs(layout, own, plan, parts, results, scratch, send_sems, recv_sems, local_sems):
    stages = len(layout.dims)
    buffers = 2 * stages - 1
    jobs = []
    for at, (which, way, columns) in enumerate(plan):
        mine = scratch[at * buffers : (at + 1) * buffers]
        jobs.append(
            ScatterJob(
                layout,
                own,
                layout.orders[way][::-1],
                parts[which],
                mine[: stages - 1],
                mine[stages - 1 :],
                results[which],
                (send_sems.at[at], recv_sems.at[at], local_sems.at[at]),
                columns,
            )
        )
    return jobs


def scatter_scratch(layout, plan, shapes):
    scratch = []
    for which, way, columns in plan:
        rows, width = shapes[which]
        width = width if columns is None else columns[1]
        scratch += scatter_buffers(layout, layout.orders[way][::-1], rows, width, jnp.bfloat16)
    return scratch


def gather_kernel(layout, plan, count, *refs):
    shards, fulls = refs[:count], refs[count : 2 * count]
    send_sems, recv_sems, local_sems = refs[2 * count :]
    own = layout.own()
    layout.greet(own)
    jobs = gather_jobs(layout, own, plan, shards, fulls, send_sems, recv_sems, local_sems)
    for todo in run_rounds(jobs, len(layout.dims), 4):
        for job, stage in todo:
            job.advance(stage)
    for job in jobs:
        job.finish()


def gather_all(layout, arrays, plan, collective_id):
    return pl.pallas_call(
        functools.partial(gather_kernel, layout, plan, len(arrays)),
        out_shape=gather_shapes(layout, arrays),
        in_specs=[ANYWHERE] * len(arrays),
        out_specs=[ANYWHERE] * len(arrays),
        scratch_shapes=job_sems(layout, plan),
        compiler_params=pltpu.CompilerParams(
            collective_id=collective_id, has_side_effects=True, vmem_limit_bytes=63 * MIB
        ),
    )(*arrays)


def cut(which, way, width, pieces):
    if width % (pieces * 128):
        return [(which, way, None)]
    step = width // pieces
    return [(which, way, (at * step, step)) for at in range(pieces)]


def weave(first, second):
    out = []
    for at in range(max(len(first), len(second))):
        out += first[at : at + 1] + second[at : at + 1]
    return out


def copy_kernel(count, *refs):
    for source, target in zip(refs[:count], refs[count:]):
        target[...] = source[...]


def copy_all(arrays):
    return pl.pallas_call(
        functools.partial(copy_kernel, len(arrays)),
        out_shape=[jax.ShapeDtypeStruct(a.shape, a.dtype) for a in arrays],
    )(*arrays)


def small_pack(layout, vectors):
    flat = jnp.concatenate([v.astype(jnp.float32).reshape(v.shape[0], -1) for v in vectors], 1)
    width = -(-flat.shape[1] // 1024) * 1024
    flat = jnp.pad(flat, ((0, 0), (0, width - flat.shape[1])))
    return flat.reshape(flat.shape[0], width // 128, 128)


def dot_plain(first_mat, second_mat):
    return jnp.dot(first_mat, second_mat, preferred_element_type=jnp.float32)


def dot_left_t(first_mat, second_mat):
    return lax.dot_general(
        first_mat, second_mat, (((0,), (0,)), ((), ())), preferred_element_type=jnp.float32
    )


def dot_right_t(first_mat, second_mat):
    return lax.dot_general(
        first_mat, second_mat, (((1,), (1,)), ((), ())), preferred_element_type=jnp.float32
    )


def row_mean(value):
    return jnp.sum(value, -1, keepdims=True) * (1.0 / value.shape[-1])


def norm_parts(row_data):
    centred = row_data - row_mean(row_data)
    inverse = lax.rsqrt(row_mean(centred * centred) + LN_EPS)
    return centred * inverse, inverse


def norm_backward(upstream, normed, inverse, gain_vec):
    scaled = upstream * gain_vec
    return inverse * (scaled - row_mean(scaled) - normed * row_mean(scaled * normed))


def column_sum(value):
    return jnp.sum(value, 0, keepdims=True)


def gelu_and_slope(inner_act):
    below = 0.5 * (1.0 + lax.erf(inner_act * 0.7071067811865476))
    bell = jnp.exp(-0.5 * inner_act * inner_act) * 0.3989422804014327
    return inner_act * below, below + inner_act * bell


GATHER_TIMES = (0, 1, 2, 3.5, 4.25)
SCATTER_TIMES = (0, 0.75, 2.75, 3.75, 6.75)
GROUP = 4
SPAN = GROUP * HEAD_DIM


def spread(rows, diag):
    return jnp.concatenate([rows] * GROUP, 0) * diag


def fold(square, seq_len):
    lane = lax.broadcasted_iota(jnp.int32, (seq_len, square.shape[1]), 1)
    out = square[:seq_len]
    for head in range(1, GROUP):
        block = square[head * seq_len : (head + 1) * seq_len]
        out = jnp.where(lane >= head * HEAD_DIM, block, out)
    return out


def probabilities(keys, wide_queries, length):
    scores = dot_right_t(keys, wide_queries) * HEAD_DIM ** (-0.5)
    at = lax.broadcasted_iota(jnp.int32, scores.shape, 0)
    scores = jnp.where(at < length, scores, MASKED)
    raised = jnp.exp(scores - jnp.max(scores, 0, keepdims=True))
    return raised * (1.0 / jnp.sum(raised, 0, keepdims=True))


def attend_kernel(
    layout,
    seq_len,
    plan,
    entries,
    count,
    steps,
    lengths_ref,
    x_ref,
    query_w,
    key_w,
    value_w,
    proj_w,
    vec_ref,
    diag_ref,
    *refs,
):
    shards, (q_ref, k_ref, v_ref, mix_ref, sum_ref, cls_ref) = refs[:count], refs[count : count + 6]
    fulls, sems = refs[count + 6 : 2 * count + 6], refs[2 * count + 6 :]
    rows, width = x_ref.shape
    held = rows // seq_len
    step = pl.program_id(0)
    first = step * held
    own = layout.own()

    @pl.when(step == 0)
    def _():
        layout.greet(own)

    jobs = gather_jobs(layout, own, plan, shards, fulls, *sems)
    places = [(at, point) for at in range(steps) for point in range(4)]
    sidecar = Sidecar(jobs, entries, len(layout.dims), GATHER_TIMES, evenly(places))
    sidecar.visit(step, 0)
    x = x_ref[...]
    q_ref[...] = (dot_plain(x, query_w[...]) + vec_ref[0:1, :]).astype(jnp.bfloat16)
    k_ref[...] = dot_plain(x, key_w[...]).astype(jnp.bfloat16)
    v_ref[...] = (dot_plain(x, value_w[...]) + vec_ref[1:2, :]).astype(jnp.bfloat16)
    diag = diag_ref[...]
    sidecar.visit(step, 1)

    def sentence(at):
        length = lengths_ref[first + at]
        here = pl.ds(at * seq_len, seq_len)
        for low in range(0, width, SPAN):
            cols = pl.ds(low, SPAN)
            wide = spread(q_ref[here, cols], diag)
            probs = probabilities(k_ref[here, cols], wide, length).astype(jnp.bfloat16)
            mixed = fold(dot_left_t(probs, v_ref[here, cols]), seq_len)
            mix_ref[here, cols] = mixed.astype(jnp.bfloat16)

    for at in range(held // 2):
        sentence(at)
    sidecar.visit(step, 2)
    for at in range(held // 2, held):
        sentence(at)
    sidecar.visit(step, 3)
    total = x.astype(jnp.float32) + dot_plain(mix_ref[...], proj_w[...]) + vec_ref[2:3, :]
    sum_ref[...] = total
    for at in range(held):
        cls_ref[0, at : at + 1, :] = total[at * seq_len : at * seq_len + 1]

    @pl.when(step == steps - 1)
    def _():
        sidecar.finish()


def whole(shape):
    return pl.BlockSpec(shape, lambda *_: (0,) * len(shape), pipeline_mode=pl.Buffered(1))


def attend(
    layout, x, lengths, weights, vec, diag, arrays, plan, entries, seq_len, rows, collective_id
):
    total, width = x.shape
    steps = total // rows
    held = rows // seq_len
    block = pl.BlockSpec((rows, width), lambda i: (i, 0))
    narrow = jax.ShapeDtypeStruct((total, width), jnp.bfloat16)
    return pl.pallas_call(
        functools.partial(attend_kernel, layout, seq_len, plan, entries, len(arrays), steps),
        grid=(steps,),
        out_shape=[
            narrow,
            narrow,
            narrow,
            narrow,
            jax.ShapeDtypeStruct((total, width), jnp.float32),
            jax.ShapeDtypeStruct((steps, held, width), jnp.float32),
        ]
        + gather_shapes(layout, arrays),
        in_specs=[pl.BlockSpec(memory_space=pltpu.SMEM), block]
        + [whole(w.shape) for w in weights]
        + [whole(vec.shape), whole(diag.shape)]
        + [ANYWHERE] * len(arrays),
        out_specs=[block] * 5
        + [pl.BlockSpec((1, held, width), lambda i: (i, 0, 0))]
        + [ANYWHERE] * len(arrays),
        scratch_shapes=job_sems(layout, plan),
        compiler_params=pltpu.CompilerParams(
            collective_id=collective_id, has_side_effects=True, vmem_limit_bytes=63 * MIB
        ),
    )(lengths, x, *weights, vec, diag, *arrays)


def feed_kernel(
    seq_len,
    blocks,
    pieces,
    sum_ref,
    tok_ref,
    mix_ref,
    cls_ref,
    inner_w,
    outer_w,
    vec_ref,
    bias_ref,
    out_ref,
    back_ref,
    inner_grad,
    outer_grad,
    proj_grad,
    vec_grad,
    bias_grad,
    slope,
    active,
    inner_b,
    hidden_b,
    second_b,
    proj_sum,
):
    step = pl.program_id(0)
    rows, width = sum_ref.shape
    piece = active.shape[2]

    @pl.when(step == 0)
    def _():
        vec_grad[...] = jnp.zeros_like(vec_grad)
        bias_grad[...] = jnp.zeros_like(bias_grad)
        proj_sum[...] = jnp.zeros_like(proj_sum)

    @pl.when(step < blocks)
    def _():
        here = pl.ds(pl.multiple_of(step * rows, rows), rows)
        gain_one, shift_one = vec_ref[3:4, :], vec_ref[4:5, :]
        gain_two, shift_two = vec_ref[6:7, :], vec_ref[7:8, :]
        normed_one, inverse_one = norm_parts(sum_ref[...])
        hidden = normed_one * gain_one + shift_one
        narrow = hidden.astype(jnp.bfloat16)
        hidden_b[here, :] = narrow
        second_sum = hidden + vec_ref[5:6, :]
        for at in range(pieces):
            cols = slice(at * piece, (at + 1) * piece)
            value, steep = gelu_and_slope(dot_plain(narrow, inner_w[:, cols]) + bias_ref[:, cols])
            value = value.astype(jnp.bfloat16)
            slope[at] = steep
            active[at, here, :] = value
            second_sum = second_sum + dot_plain(value, outer_w[cols, :])
        normed_two, inverse_two = norm_parts(second_sum)
        out_ref[...] = (normed_two * gain_two + shift_two).astype(jnp.bfloat16)
        grad = tok_ref[...].astype(jnp.float32).reshape(rows // seq_len, seq_len, width)
        place = lax.broadcasted_iota(jnp.int32, grad.shape, 1)
        extra = cls_ref[...].reshape(rows // seq_len, 1, width)
        grad = (grad + jnp.where(place == 0, extra, 0.0)).reshape(rows, width)
        vec_grad[6:7, :] += column_sum(grad * normed_two)
        vec_grad[7:8, :] += column_sum(grad)
        second = norm_backward(grad, normed_two, inverse_two, gain_two)
        vec_grad[5:6, :] += column_sum(second)
        narrow_two = second.astype(jnp.bfloat16)
        second_b[here, :] = narrow_two
        hidden_grad = second
        for at in range(pieces):
            cols = slice(at * piece, (at + 1) * piece)
            inner = dot_right_t(narrow_two, outer_w[cols, :]) * slope[at]
            bias_grad[:, cols] += column_sum(inner)
            inner = inner.astype(jnp.bfloat16)
            inner_b[at, here, :] = inner
            hidden_grad = hidden_grad + dot_right_t(inner, inner_w[:, cols])
        vec_grad[3:4, :] += column_sum(hidden_grad * normed_one)
        vec_grad[4:5, :] += column_sum(hidden_grad)
        first = norm_backward(hidden_grad, normed_one, inverse_one, gain_one)
        vec_grad[2:3, :] += column_sum(first)
        back_ref[...] = first
        proj_sum[...] += dot_left_t(mix_ref[...], first.astype(jnp.bfloat16))

        @pl.when(step == blocks - 1)
        def _():
            proj_grad[...] = proj_sum[...].astype(jnp.bfloat16)

    @pl.when(step >= blocks)
    def _():
        at = step - blocks
        outer_grad[...] = dot_left_t(active[at], second_b[...]).astype(jnp.bfloat16)
        inner_grad[...] = dot_left_t(hidden_b[...], inner_b[at]).astype(jnp.bfloat16)


def feed(
    first_sum, tokens_grad, mixture, cls_grad, inner_w, outer_w, vec, bias, seq_len, rows, piece
):
    total, width = first_sum.shape
    wide = inner_w.shape[1]
    blocks, pieces = total // rows, wide // piece
    held = rows // seq_len
    cls_grad = cls_grad.reshape(blocks, held, width)
    block = pl.BlockSpec((rows, width), lambda i: (jnp.minimum(i, blocks - 1), 0))
    return pl.pallas_call(
        functools.partial(feed_kernel, seq_len, blocks, pieces),
        grid=(blocks + pieces,),
        out_shape=[
            jax.ShapeDtypeStruct((total, width), jnp.bfloat16),
            jax.ShapeDtypeStruct((total, width), jnp.float32),
            jax.ShapeDtypeStruct(inner_w.shape, jnp.bfloat16),
            jax.ShapeDtypeStruct(outer_w.shape, jnp.bfloat16),
            jax.ShapeDtypeStruct((width, width), jnp.bfloat16),
            jax.ShapeDtypeStruct((8, width), jnp.float32),
            jax.ShapeDtypeStruct((1, wide), jnp.float32),
        ],
        in_specs=[
            block,
            block,
            block,
            pl.BlockSpec((1, held, width), lambda i: (jnp.minimum(i, blocks - 1), 0, 0)),
            whole(inner_w.shape),
            whole(outer_w.shape),
            whole(vec.shape),
            whole(bias.shape),
        ],
        out_specs=[
            block,
            block,
            pl.BlockSpec((width, piece), lambda i: (0, jnp.maximum(i - blocks, 0))),
            pl.BlockSpec((piece, width), lambda i: (jnp.maximum(i - blocks, 0), 0)),
            whole((width, width)),
            pl.BlockSpec((8, width), lambda i: (0, 0)),
            pl.BlockSpec((1, wide), lambda i: (0, 0)),
        ],
        scratch_shapes=[
            pltpu.VMEM((pieces, rows, piece), jnp.float32),
            pltpu.VMEM((pieces, total, piece), jnp.bfloat16),
            pltpu.VMEM((pieces, total, piece), jnp.bfloat16),
            pltpu.VMEM((total, width), jnp.bfloat16),
            pltpu.VMEM((total, width), jnp.bfloat16),
            pltpu.VMEM((width, width), jnp.float32),
        ],
        compiler_params=pltpu.CompilerParams(vmem_limit_bytes=63 * MIB),
    )(first_sum, tokens_grad, mixture, cls_grad, inner_w, outer_w, vec, bias)


def unflat(flat, dims):
    digits = []
    for size in reversed(dims):
        digits.insert(0, flat % size)
        flat = flat // size
    return tuple(digits)


def back_kernel(
    layout,
    seq_len,
    blocks,
    plan,
    entries,
    count,
    lengths_ref,
    x_ref,
    q_ref,
    k_ref,
    v_ref,
    first_ref,
    query_w,
    key_w,
    value_w,
    proj_w,
    diag_ref,
    feed_vec,
    feed_bias,
    pool_vec,
    *refs,
):
    step = pl.program_id(0)
    rows, width = x_ref.shape
    held = rows // seq_len
    scale = HEAD_DIM ** (-0.5)
    stages = len(layout.dims)
    parts, refs = refs[:count], refs[count:]
    (in_ref, vec_sum), refs = refs[:2], refs[2:]
    sums, refs = refs[: count + 3], refs[count + 3 :]
    (x_all, dq_all, dk_all, dv_all, dmix), refs = refs[:5], refs[5:]
    own_parts, refs = refs[:3], refs[3:]
    (vec_grad, vec_lands), refs = refs[:2], refs[2:]
    vec_steps, refs = refs[: stages - 1], refs[stages - 1 :]
    own = layout.own()
    vec_job = SumJob(layout, own, vec_grad, vec_lands, tuple(vec_steps) + (vec_sum,), refs[-2:])
    jobs = scatter_jobs(layout, own, plan, parts + own_parts, sums, refs[:-5], *refs[-5:-2])

    own_at = sorted({entry for entry, job in zip(entries, plan) if job[0] >= count})

    def place(when, last):
        if when < own_at[0]:
            half = int(when * 2 * blocks / own_at[0])
            return (half // 2, half % 2)
        for at, entry in enumerate(own_at):
            if when <= entry:
                return (blocks + at, 1)
        half = int((when - own_at[-1]) * blocks / (last - own_at[-1]))
        return (blocks + 3 + half, 0) if half < blocks else (2 * blocks + 2, 1)

    last_entry = max(entries)
    sidecar = Sidecar(jobs + [vec_job], list(entries) + [last_entry], stages, SCATTER_TIMES, place)

    @pl.when(step == 0)
    def _():
        layout.greet(own)
        vec_grad[0:2, :] = jnp.zeros_like(vec_grad[0:2, :])
        vec_grad[2:8, :] = feed_vec[2:8, :]
        vec_grad[8:9, :] = pool_vec[...]
        pieces = feed_bias.shape[1] // width
        vec_grad[9:, :] = jnp.zeros_like(vec_grad[9:, :])
        for at in range(pieces):
            vec_grad[9 + at : 10 + at, :] = feed_bias[:, at * width : (at + 1) * width]

    @pl.when(step < blocks)
    def _():
        here = pl.ds(pl.multiple_of(step * rows, rows), rows)
        sidecar.visit(step, 0)
        x_all[here, :] = x_ref[...]
        narrow = first_ref[...].astype(jnp.bfloat16)
        dmix[...] = dot_right_t(narrow, proj_w[...]).astype(jnp.bfloat16)
        diag = diag_ref[...]

        def sentence(at):
            length = lengths_ref[step * held + at]
            near = pl.ds(at * seq_len, seq_len)
            far = pl.ds(pl.multiple_of(step * rows + at * seq_len, seq_len), seq_len)
            for low in range(0, width, SPAN):
                cols = pl.ds(low, SPAN)
                keys = k_ref[near, cols]
                wide = spread(q_ref[near, cols], diag)
                wide_grad = spread(dmix[near, cols], diag)
                probs = probabilities(keys, wide, length)
                prob_grad = dot_right_t(v_ref[near, cols], wide_grad)
                dv_all[far, cols] = dot_plain(probs.astype(jnp.bfloat16), wide_grad).astype(
                    jnp.bfloat16
                )
                score_grad = probs * (prob_grad - column_sum(prob_grad * probs))
                score_grad = score_grad.astype(jnp.bfloat16)
                dk_all[far, cols] = (dot_plain(score_grad, wide) * scale).astype(jnp.bfloat16)
                dq_all[far, cols] = (fold(dot_left_t(score_grad, keys), seq_len) * scale).astype(
                    jnp.bfloat16
                )

        for at in range(held // 2):
            sentence(at)
        sidecar.visit(step, 1)
        for at in range(held // 2, held):
            sentence(at)
        vec_grad[0:1, :] += column_sum(dq_all[here, :].astype(jnp.float32))
        vec_grad[1:2, :] += column_sum(dv_all[here, :].astype(jnp.float32))

    for at, (right, part) in enumerate(zip((dq_all, dk_all, dv_all), own_parts)):

        @pl.when(step == blocks + at)
        def _():
            value = dot_left_t(x_all[...], right[...])
            share = part.shape[-2]
            for device in range(layout.count):
                piece = value[device * share : (device + 1) * share]
                part[unflat(device, layout.dims)] = piece.astype(jnp.bfloat16)
            sidecar.visit(step, 1)

    @pl.when(step >= blocks + 3)
    def _():
        sidecar.visit(step, 0)
        here = pl.ds(pl.multiple_of((step - blocks - 3) * rows, rows), rows)
        in_ref[...] = (
            first_ref[...]
            + dot_right_t(dq_all[here, :], query_w[...])
            + dot_right_t(dk_all[here, :], key_w[...])
            + dot_right_t(dv_all[here, :], value_w[...])
        )
        sidecar.visit(step, 1)

    @pl.when(step == 2 * blocks + 2)
    def _():
        sidecar.finish()


def back(
    layout,
    x,
    lengths,
    saved,
    first_grad,
    weights,
    diag,
    vectors,
    arrays,
    plan,
    entries,
    seq_len,
    rows,
    collective_id,
):
    total, width = x.shape
    blocks = total // rows
    stages = len(layout.dims)
    share = width // layout.count
    shapes = [a.shape[-2:] for a in arrays] + [(share, width)] * 3
    block = pl.BlockSpec((rows, width), lambda i: (jnp.minimum(i, blocks - 1), 0))
    twice = pl.BlockSpec(
        (rows, width),
        lambda i: (jnp.where(i < blocks, i, jnp.maximum(i - blocks - 3, 0)), 0),
    )
    out_block = pl.BlockSpec((rows, width), lambda i: (jnp.maximum(i - blocks - 3, 0), 0))
    small = pltpu.VMEM((16, width), jnp.float32)
    return pl.pallas_call(
        functools.partial(back_kernel, layout, seq_len, blocks, plan, entries, len(arrays)),
        grid=(2 * blocks + 3,),
        out_shape=[
            jax.ShapeDtypeStruct((total, width), jnp.float32),
            jax.ShapeDtypeStruct((16, width), jnp.float32),
        ]
        + [jax.ShapeDtypeStruct(s, jnp.float32) for s in shapes],
        in_specs=[pl.BlockSpec(memory_space=pltpu.SMEM)]
        + [block] * 4
        + [twice]
        + [whole(w.shape) for w in weights]
        + [whole(diag.shape)]
        + [whole(v.shape) for v in vectors]
        + [ANYWHERE] * len(arrays),
        out_specs=[out_block, whole((16, width))] + [whole(s) for s in shapes],
        scratch_shapes=[pltpu.VMEM((total, width), jnp.bfloat16)] * 4
        + [pltpu.VMEM((rows, width), jnp.bfloat16)]
        + [pltpu.VMEM(layout.dims + (share, width), jnp.bfloat16)] * 3
        + [small, pltpu.VMEM((layout.sends, 16, width), jnp.float32)]
        + [small] * (stages - 1)
        + scatter_scratch(layout, plan, shapes)
        + job_sems(layout, plan)
        + [pltpu.SemaphoreType.DMA((layout.sends,))] * 2,
        compiler_params=pltpu.CompilerParams(
            collective_id=collective_id, has_side_effects=True, vmem_limit_bytes=63 * MIB
        ),
    )(lengths, x, *saved, first_grad, *weights, diag, *vectors, *arrays)


def rank_kernel(
    layout,
    micros,
    node_dev,
    steps,
    sum_ref,
    inner_w,
    outer_w,
    pool_w,
    vec_ref,
    bias_ref,
    node_ref,
    cls_grad,
    pool_grad,
    shift_grad,
    hidden,
    total,
    mine,
    units,
    node_cols,
    totals,
    send_sems,
    recv_sems,
    local_sems,
):
    step = pl.program_id(0)
    sentences, width = sum_ref.shape
    own = layout.own()

    @pl.when(step == 0)
    def _():
        layout.greet(own)
        normed, _ = norm_parts(sum_ref[...])
        start = normed * vec_ref[3:4, :] + vec_ref[4:5, :]
        hidden[...] = start.astype(jnp.bfloat16)
        total[...] = start + vec_ref[5:6, :]
        node_cols[...] = node_ref[...].T

    value, _ = gelu_and_slope(dot_plain(hidden[...], inner_w[...]) + bias_ref[...])
    total[...] += dot_plain(value.astype(jnp.bfloat16), outer_w[...])

    @pl.when(step == steps - 1)
    def _():
        normed, _ = norm_parts(total[...])
        cls_rows = (normed * vec_ref[6:7, :] + vec_ref[7:8, :]).astype(jnp.bfloat16)
        pooled = jnp.tanh(dot_plain(cls_rows, pool_w[...]) + vec_ref[8:9, :])
        scale_inv = lax.rsqrt(jnp.sum(pooled * pooled, -1, keepdims=True) + UNIT_EPS)
        unit = pooled * scale_inv
        mine[...] = unit.astype(jnp.bfloat16)
        step_cols = width // len(layout.orders)
        plan = [(0, way, (way * step_cols, step_cols)) for way in range(len(layout.orders))]
        jobs = gather_jobs(layout, own, plan, [mine], [units], send_sems, recv_sems, local_sems)
        for stage in range(len(layout.dims) + 1):
            for job in jobs:
                job.advance(stage)
        for job in jobs:
            job.finish()

        device = own[0]
        for size, digit in zip(layout.dims[1:], own[1:]):
            device = device * size + digit
        at_home = pl.ds(pl.multiple_of(device * node_dev, node_dev), node_dev)
        count = layout.count * node_dev
        band = min(count, 512)
        every = units[...].reshape(layout.count, sentences, width)
        grads = []

        def scored(similar, tongue, place, side, tongue_row, place_row, side_row):
            across = side != side_row
            include = across & (tongue == tongue_row)
            positive = jnp.where(across & (place == place_row), 1.0, 0.0)
            return (
                jnp.where(include, SIM_SCALE * similar - SIM_SCALE * MARGIN * positive, MASKED),
                include,
                positive,
            )

        half = node_dev // 2

        def sides(shape, dim, offset):
            return (lax.broadcasted_iota(jnp.int32, shape, dim) + offset) // half % 2

        for micro in range(micros):
            here = slice(micro * node_dev, (micro + 1) * node_dev)
            nodes = every[:, here, :].reshape(count, width)
            tongue, place = node_cols[:, 2 * micro : 2 * micro + 1], node_cols[
                :, 2 * micro + 1 : 2 * micro + 2
            ]
            for low in range(0, count, band):
                cols = slice(low, low + band)
                similar = dot_right_t(nodes, nodes[cols])
                value, _, _ = scored(
                    similar,
                    tongue,
                    place,
                    sides((count, 1), 0, 0),
                    node_ref[2 * micro : 2 * micro + 1, cols],
                    node_ref[2 * micro + 1 : 2 * micro + 2, cols],
                    sides((1, band), 1, low),
                )
                peak = jnp.max(value, 0, keepdims=True)
                totals[:, cols] = jnp.log(column_sum(jnp.exp(value - peak))) + peak
            value, include, positive = scored(
                dot_right_t(mine[here, :], nodes),
                node_cols[at_home, 2 * micro : 2 * micro + 1],
                node_cols[at_home, 2 * micro + 1 : 2 * micro + 2],
                sides((node_dev, 1), 0, 0),
                node_ref[2 * micro : 2 * micro + 1, :],
                node_ref[2 * micro + 1 : 2 * micro + 2, :],
                sides((1, count), 1, 0),
            )
            peak = jnp.max(value, -1, keepdims=True)
            line = jnp.log(jnp.sum(jnp.exp(value - peak), -1, keepdims=True)) + peak
            grad_sim = jnp.where(
                include, jnp.exp(value - line) + jnp.exp(value - totals[...]), 0.0
            )
            grad_sim = (grad_sim - 2.0 * positive).astype(jnp.bfloat16)
            grads.append(SIM_SCALE * dot_plain(grad_sim, nodes))
        unit_grad = jnp.concatenate(grads, 0)
        pooled_grad = scale_inv * (
            unit_grad - unit * jnp.sum(unit_grad * unit, -1, keepdims=True)
        )
        pre_grad = pooled_grad * (1.0 - pooled * pooled)
        narrow = pre_grad.astype(jnp.bfloat16)
        pool_grad[...] = dot_left_t(cls_rows, narrow).astype(jnp.bfloat16)
        shift_grad[...] = column_sum(pre_grad)
        cls_grad[...] = dot_right_t(narrow, pool_w[...])


def rank(layout, cls_sum, inner_w, outer_w, pool_w, vec, bias, nodes, micros, piece, collective_id):
    sentences, width = cls_sum.shape
    wide = inner_w.shape[1]
    steps = wide // piece
    node_dev = sentences // micros
    return pl.pallas_call(
        functools.partial(rank_kernel, layout, micros, node_dev, steps),
        grid=(steps,),
        out_shape=[
            jax.ShapeDtypeStruct((sentences, width), jnp.float32),
            jax.ShapeDtypeStruct((width, width), jnp.bfloat16),
            jax.ShapeDtypeStruct((1, width), jnp.float32),
        ],
        in_specs=[
            whole(cls_sum.shape),
            pl.BlockSpec((width, piece), lambda i: (0, i)),
            pl.BlockSpec((piece, width), lambda i: (i, 0)),
            whole(pool_w.shape),
            whole(vec.shape),
            pl.BlockSpec((1, piece), lambda i: (0, i)),
            whole(nodes.shape),
        ],
        out_specs=[
            pl.BlockSpec((sentences, width), lambda i: (0, 0)),
            pl.BlockSpec((width, width), lambda i: (0, 0)),
            pl.BlockSpec((1, width), lambda i: (0, 0)),
        ],
        scratch_shapes=[
            pltpu.VMEM((sentences, width), jnp.bfloat16),
            pltpu.VMEM((sentences, width), jnp.float32),
            pltpu.VMEM((sentences, width), jnp.bfloat16),
            pltpu.VMEM(layout.dims + (sentences, width), jnp.bfloat16),
            pltpu.VMEM((nodes.shape[1], nodes.shape[0]), jnp.float32),
            pltpu.VMEM((1, nodes.shape[1]), jnp.float32),
        ]
        + job_sems(layout, layout.orders),
        compiler_params=pltpu.CompilerParams(
            collective_id=collective_id, has_side_effects=True, vmem_limit_bytes=63 * MIB
        ),
    )(cls_sum, inner_w, outer_w, pool_w, vec, bias, nodes)


def on_device(
    layout,
    hidden_in,
    lengths,
    partner,
    language,
    token_cotangent,
    query_weight,
    key_weight,
    value_weight,
    attn_out_weight,
    query_bias,
    value_bias,
    attn_out_bias,
    ln1_gain,
    ln1_shift,
    in_weight,
    in_bias,
    out_weight,
    out_bias,
    ln2_gain,
    ln2_shift,
    pool_weight,
    pool_bias,
):
    micro_count, sides, pair_dev, seq_len, model_width = hidden_in.shape
    inner_width = in_weight.shape[1]
    count = layout.count
    node_dev = sides * pair_dev
    sent_count = micro_count * node_dev
    row_count = sent_count * seq_len
    pair_count = partner.shape[1]
    device = lax.axis_index("dp") * (count // layout.slow) + lax.axis_index("fsdp")

    vectors = (
        query_bias,
        value_bias,
        attn_out_bias,
        ln1_gain,
        ln1_shift,
        out_bias,
        ln2_gain,
        ln2_shift,
        pool_bias,
        in_bias,
    )
    small = small_pack(layout, [v[None] for v in vectors])[0]
    arrays = [query_weight, key_weight, value_weight, attn_out_weight, small]
    plan = [(4, 0, None)]
    plan += weave(cut(0, 0, model_width, 2), cut(1, 1, model_width, 2))
    plan += weave(cut(2, 0, model_width, 2), cut(3, 1, model_width, 2))
    gathered = gather_all(layout, arrays, tuple(plan), 0)

    def joined(full, array):
        return full.reshape((count * array.shape[0],) + array.shape[1:])

    *weights, small_full = map(joined, gathered, arrays)
    small_rows = small_full.reshape(count, -1)
    share = query_bias.shape[0]
    rows_of = len(vectors) - 1
    vec = small_rows[:, : rows_of * share].reshape(count, rows_of, share)
    vec = jnp.moveaxis(vec, 1, 0).reshape(rows_of, model_width)
    vec = jnp.pad(vec, ((0, 16 - rows_of), (0, 0)))
    bias = small_rows[:, rows_of * share : rows_of * share + in_bias.shape[0]]
    bias = bias.reshape(1, inner_width)

    pair_ids = jnp.arange(pair_count, dtype=jnp.int32)
    hit = partner[:, :, None] == pair_ids[None, None, :]
    target_language = jnp.sum(jnp.where(hit, language[:, :, None], 0), 1)

    def split(value):
        return value.reshape(micro_count, count, 1, pair_dev)

    node_rows = jnp.stack(
        [
            jnp.concatenate([split(language), split(target_language)], 2),
            jnp.concatenate(
                [split(partner), split(jnp.broadcast_to(pair_ids, partner.shape))], 2
            ),
        ],
        1,
    )
    node_rows = node_rows.reshape(2 * micro_count, count * node_dev).astype(jnp.float32)
    node_rows = jnp.pad(node_rows, ((0, -2 * micro_count % 8), (0, 0)))
    block_at = jnp.arange(SPAN) // HEAD_DIM
    diag = (block_at[:, None] == block_at[None, :]).astype(jnp.bfloat16)

    x = hidden_in.reshape(row_count, model_width)
    sent_lengths = lengths.reshape(sent_count)
    arrays = [in_weight, out_weight, pool_weight]

    def halves(which):
        return cut(which, 0, model_width, 2)[:1] + cut(which, 1, model_width, 2)[1:]

    first_cuts, second_cuts = cut(0, 0, inner_width, 8), cut(1, 1, model_width, 6)
    plan = weave(first_cuts[:6], second_cuts)
    plan += halves(2) + first_cuts[6:]
    entries = tuple(0.4 * at for at in range(len(plan)))
    queries, keys, values, mixture, first_sum, cls_sum, *gathered = attend(
        layout, x, sent_lengths, weights, vec, diag, arrays, tuple(plan), entries, seq_len, 512, 1
    )
    inner_full, outer_full, pool_full = map(joined, gathered, arrays)
    cls_grad, grad_pool, grad_pool_shift = rank(
        layout,
        cls_sum.reshape(sent_count, model_width),
        inner_full,
        outer_full,
        pool_full,
        vec,
        bias,
        node_rows,
        micro_count,
        768,
        2,
    )
    block_out, first_grad, grad_inner, grad_outer, grad_proj, vec_grad, grad_bias = feed(
        first_sum,
        token_cotangent.reshape(row_count, model_width),
        mixture,
        cls_grad,
        inner_full,
        outer_full,
        vec,
        bias,
        seq_len,
        256,
        768,
    )

    def apart(part):
        return part.reshape(layout.dims + (-1, part.shape[1]))

    parts = list(map(apart, (grad_inner, grad_outer, grad_pool, grad_proj)))
    first_cuts, second_cuts = cut(0, 0, inner_width, 4), cut(1, 1, model_width, 3)
    plan = weave(first_cuts[:3], second_cuts) + first_cuts[3:]
    plan += weave(halves(2)[::-1], halves(3)[::-1])
    entries = [0.75 * (at // 2) for at in range(len(plan))]
    for which in (4, 5, 6):
        entries += [entries[-1] + 0.75] * 2
        plan += halves(which)
    input_grad, vec_sum, *sums = back(
        layout,
        x,
        sent_lengths,
        (queries, keys, values),
        first_grad,
        weights,
        diag,
        (vec_grad, grad_bias, grad_pool_shift),
        parts,
        tuple(plan),
        tuple(entries),
        seq_len,
        256,
        3,
    )
    block_out = block_out.reshape(hidden_in.shape)
    input_grad = input_grad.reshape(hidden_in.shape)
    sums = copy_all(sums)
    vec_own = lax.dynamic_slice_in_dim(vec_sum[:rows_of], device * share, share, 1)
    bias_sum = vec_sum[rows_of : rows_of + inner_width // model_width].reshape(-1)
    bias_own = lax.dynamic_slice_in_dim(bias_sum, device * in_bias.shape[0], in_bias.shape[0])
    (
        sum_query_shift,
        sum_value_shift,
        sum_proj_shift,
        sum_gain_one,
        sum_shift_one,
        sum_outer_shift,
        sum_gain_two,
        sum_shift_two,
        sum_pool_shift,
    ) = vec_own
    return (
        block_out,
        input_grad,
        sums[4],
        sums[5],
        sums[6],
        sums[3],
        sum_query_shift,
        sum_value_shift,
        sum_proj_shift,
        sum_gain_one,
        sum_shift_one,
        sums[0],
        bias_own,
        sums[1],
        sum_outer_shift,
        sum_gain_two,
        sum_shift_two,
        sums[2],
        sum_pool_shift,
    )


def solution(mesh):
    rows = P(("dp", "fsdp"), None)
    vector = P(("dp", "fsdp"))
    sentences = P(None, None, ("dp", "fsdp"), None, None)
    placed = (
        (sentences, P(None, None, ("dp", "fsdp")), P(), P(), sentences)
        + (rows,) * 4
        + (vector,) * 5
        + (rows, vector, rows)
        + (vector,) * 3
        + (rows, vector)
    )
    return jax.shard_map(
        functools.partial(on_device, Layout(mesh.shape)),
        mesh=mesh,
        in_specs=placed,
        out_specs=(sentences, sentences)
        + (rows,) * 4
        + (vector,) * 5
        + (rows, vector, rows)
        + (vector,) * 3
        + (rows, vector),
        check_vma=False,
    )
```

```python
import functools

import jax
import jax.numpy as jnp
from jax import lax
from jax.experimental import pallas as pl
from jax.experimental.pallas import tpu as pltpu
from jax.sharding import PartitionSpec as P

HEAD_DIM = 64


LN_EPS = 1e-06
UNIT_EPS = 1e-06
SIM_SCALE = 10.0
MARGIN = 0.3
MASKED = -1e30
MIB = 1024 * 1024


MESH_ID = pl.DeviceIdType.MESH
AXES = ("dp", "fsdp")


class Layout:
    def __init__(self, mesh_shape):
        slow, fast = mesh_shape["dp"], mesh_shape["fsdp"]
        self.slow, self.count = slow, slow * fast
        if slow == 8:
            self.dims = (2, 2, 2, fast)
            self.orders = ((3, 1, 0, 2), (3, 0, 1, 2))
        else:
            self.dims = (slow, fast)
            self.orders = ((1, 0), (1, 0))
        self.sends = sum(size - 1 for size in self.dims)

    def own(self):
        digits = [lax.axis_index("fsdp")]
        rest = lax.axis_index("dp")
        for size in self.dims[-2::-1]:
            digits.insert(0, rest % size)
            rest = rest // size
        return digits

    def device(self, digits):
        slow = digits[0]
        for size, digit in zip(self.dims[1:-1], digits[1:-1]):
            slow = slow * size + digit
        return (slow, digits[-1])

    def shifted(self, own, dim, step):
        size = self.dims[dim]
        out = list(own)
        out[dim] = (own[dim] + step) % size
        return out

    def first_slot(self, order, stage):
        return sum(self.dims[dim] - 1 for dim in order[:stage])

    def greet(self, own):
        barrier = pltpu.get_barrier_semaphore()
        for dim, size in enumerate(self.dims):
            for step in range(1, size):
                pl.semaphore_signal(
                    barrier,
                    inc=1,
                    device_id=self.device(self.shifted(own, dim, step)),
                    device_id_type=MESH_ID,
                )
        pl.semaphore_wait(barrier, self.sends)


class GatherJob:
    def __init__(self, layout, own, order, shard, full, sems, columns=None):
        self.layout, self.own, self.order = layout, own, order
        self.shard, self.full, self.columns = shard, full, columns
        self.send_sems, self.recv_sems, self.local_sem = sems

    def block(self, digits, done):
        index = tuple(
            slice(None) if dim in done else digits[dim] for dim in range(len(self.layout.dims))
        )
        if self.columns is not None:
            index = index + (slice(None), pl.ds(*self.columns))
        return self.full.at[index]

    def piece(self):
        if self.columns is not None:
            return self.shard.at[:, pl.ds(*self.columns)]
        return self.shard

    def copies(self, stage, sending):
        dim, done = self.order[stage], self.order[:stage]
        base = self.layout.first_slot(self.order, stage)
        out = []
        for step in range(1, self.layout.dims[dim]):
            slot = base + step - 1
            other = self.layout.shifted(self.own, dim, step if sending else -step)
            target = self.block(self.own if sending else other, done)
            source = self.piece() if sending and stage == 0 else target
            out.append(
                pltpu.make_async_remote_copy(
                    src_ref=source,
                    dst_ref=target,
                    send_sem=self.send_sems.at[slot],
                    recv_sem=self.recv_sems.at[slot],
                    device_id=self.layout.device(other),
                    device_id_type=MESH_ID,
                )
            )
        return out

    def local(self):
        return pltpu.make_async_copy(self.piece(), self.block(self.own, ()), self.local_sem)

    def advance(self, stage):
        if stage == 0:
            self.local().start()
        else:
            for copy in self.copies(stage - 1, False):
                copy.wait_recv()
            if stage == 1:
                self.local().wait()
        if stage < len(self.order):
            for copy in self.copies(stage, True):
                copy.start()

    def finish(self):
        for stage in range(len(self.order)):
            for copy in self.copies(stage, True):
                copy.wait_send()


def run_rounds(jobs, stages, width=2):
    rounds = []
    last = stages + (len(jobs) - 1) // width
    for step in range(last + 1):
        todo = []
        for index, job in enumerate(jobs):
            stage = step - index // width
            if 0 <= stage <= stages:
                todo.append((job, stage))
        rounds.append(todo)
    return rounds


class Sidecar:
    def __init__(self, jobs, entries, stages, offsets, place):
        self.jobs = jobs
        events = []
        for at, (job, entry) in enumerate(zip(jobs, entries)):
            for stage in range(stages + 1):
                after = offsets[stage] if len(offsets) == stages + 1 else 1.5 * stage
                events.append((entry + after, at, job, stage))
        events.sort(key=lambda event: event[:2])
        self.rounds = []
        for when, _, job, stage in events:
            here = place(when, events[-1][0])
            if not self.rounds or self.rounds[-1][0] != here:
                self.rounds.append((here, []))
            self.rounds[-1][1].append((job, stage))

    def visit(self, step, point):
        for place, todo in self.rounds:
            if place[1] == point:

                @pl.when(step == place[0])
                def _():
                    for job, stage in todo:
                        job.advance(stage)

    def finish(self):
        for job in self.jobs:
            job.finish()


def evenly(places):
    return lambda when, last: places[min(int(when * len(places) / last), len(places) - 1)]


class SumJob:
    def __init__(self, layout, own, start, lands, results, sems):
        self.layout, self.own, self.start = layout, own, start
        self.lands, self.results = lands, results
        self.send_sems, self.recv_sems = sems
        self.order = tuple(range(len(layout.dims)))

    def copies(self, stage):
        base = self.layout.first_slot(self.order, stage)
        source = self.start if stage == 0 else self.results[stage - 1]
        out = []
        for step in range(1, self.layout.dims[stage]):
            slot = base + step - 1
            out.append(
                pltpu.make_async_remote_copy(
                    src_ref=source,
                    dst_ref=self.lands.at[slot],
                    send_sem=self.send_sems.at[slot],
                    recv_sem=self.recv_sems.at[slot],
                    device_id=self.layout.device(self.layout.shifted(self.own, stage, step)),
                    device_id_type=MESH_ID,
                )
            )
        return out

    def advance(self, stage):
        if stage > 0:
            before = stage - 1
            value = self.start[...] if before == 0 else self.results[before - 1][...]
            base = self.layout.first_slot(self.order, before)
            for at, copy in enumerate(self.copies(before)):
                copy.wait_recv()
                value = value + self.lands[base + at]
            self.results[before][...] = value
        if stage < len(self.order):
            for copy in self.copies(stage):
                copy.start()

    def finish(self):
        for stage in range(len(self.order)):
            for copy in self.copies(stage):
                copy.wait_send()


class ScatterJob:
    def __init__(self, layout, own, order, part, sums, lands, result, sems, columns=None):
        self.layout, self.own, self.order = layout, own, order
        self.part, self.sums, self.lands, self.result = part, sums, lands, result
        self.send_sems, self.recv_sems, self.local_sem = sems
        self.columns = columns

    def tail(self):
        if self.columns is not None:
            return (slice(None), pl.ds(*self.columns))
        return ()

    def local(self):
        dim = self.order[0]
        index = [slice(None)] * len(self.layout.dims)
        index[dim] = self.own[dim]
        return pltpu.make_async_copy(
            self.part.at[tuple(index) + self.tail()], self.sums[0], self.local_sem
        )

    def copies(self, stage):
        dim = self.order[stage]
        base = self.layout.first_slot(self.order, stage)
        left = [d for d in range(len(self.layout.dims)) if d not in self.order[:stage]]
        out = []
        for step in range(1, self.layout.dims[dim]):
            slot = base + step - 1
            there = self.layout.shifted(self.own, dim, step)
            index = tuple(there[dim] if d == dim else slice(None) for d in left)
            if stage == 0:
                source = self.part.at[index + self.tail()]
            else:
                source = self.sums[stage - 1].at[index]
            out.append(
                pltpu.make_async_remote_copy(
                    src_ref=source,
                    dst_ref=self.lands[stage].at[step - 1],
                    send_sem=self.send_sems.at[slot],
                    recv_sem=self.recv_sems.at[slot],
                    device_id=self.layout.device(there),
                    device_id_type=MESH_ID,
                )
            )
        return out

    def add(self, stage):
        dim = self.order[stage]
        left = [d for d in range(len(self.layout.dims)) if d not in self.order[:stage]]
        rest = [d for d in left if d != dim]
        sizes = [self.layout.dims[d] for d in rest]
        total = 1
        for size in sizes:
            total *= size

        def body(flat):
            digits = []
            for size in reversed(sizes):
                digits.insert(0, flat % size)
                flat = flat // size
            if stage == 0:
                own_index = tuple(digits)
                value = self.sums[0][own_index].astype(jnp.float32)
            else:
                where = dict(zip(rest, digits))
                where[dim] = self.own[dim]
                value = self.sums[stage - 1][tuple(where[d] for d in left)].astype(jnp.float32)
            for step in range(1, self.layout.dims[dim]):
                value = value + self.lands[stage][(step - 1,) + tuple(digits)].astype(jnp.float32)
            if rest:
                target = self.sums[stage]
                target[tuple(digits)] = value.astype(target.dtype)
            elif self.columns is not None:
                self.result[:, pl.ds(*self.columns)] = value
            else:
                self.result[...] = value

        if total == 1:
            body(0)
        else:
            pl.loop(0, total)(body)

    def advance(self, stage):
        if stage == 0:
            self.local().start()
        else:
            for copy in self.copies(stage - 1):
                copy.wait_recv()
            if stage == 1:
                self.local().wait()
            self.add(stage - 1)
        if stage < len(self.order):
            for copy in self.copies(stage):
                copy.start()

    def finish(self):
        for stage in range(len(self.order)):
            for copy in self.copies(stage):
                copy.wait_send()


def scatter_buffers(layout, order, rows, columns, dtype):
    sums, lands = [], []
    for stage, dim in enumerate(order):
        rest = tuple(
            size for d, size in enumerate(layout.dims) if d not in order[: stage + 1]
        )
        lands.append(pltpu.VMEM((layout.dims[dim] - 1,) + rest + (rows, columns), dtype))
        if stage < len(order) - 1:
            sums.append(pltpu.VMEM(rest + (rows, columns), dtype))
    return sums + lands


ANYWHERE = pl.BlockSpec(memory_space=pltpu.HBM)


def job_sems(layout, plan):
    return [
        pltpu.SemaphoreType.DMA((len(plan), layout.sends)),
        pltpu.SemaphoreType.DMA((len(plan), layout.sends)),
        pltpu.SemaphoreType.DMA((len(plan),)),
    ]


def gather_jobs(layout, own, plan, shards, fulls, send_sems, recv_sems, local_sems):
    return [
        GatherJob(
            layout,
            own,
            layout.orders[way],
            shards[which],
            fulls[which],
            (send_sems.at[at], recv_sems.at[at], local_sems.at[at]),
            columns,
        )
        for at, (which, way, columns) in enumerate(plan)
    ]


def gather_shapes(layout, arrays):
    return [jax.ShapeDtypeStruct(layout.dims + a.shape, a.dtype) for a in arrays]


def scatter_jobs(layout, own, plan, parts, results, scratch, send_sems, recv_sems, local_sems):
    stages = len(layout.dims)
    buffers = 2 * stages - 1
    jobs = []
    for at, (which, way, columns) in enumerate(plan):
        mine = scratch[at * buffers : (at + 1) * buffers]
        jobs.append(
            ScatterJob(
                layout,
                own,
                layout.orders[way][::-1],
                parts[which],
                mine[: stages - 1],
                mine[stages - 1 :],
                results[which],
                (send_sems.at[at], recv_sems.at[at], local_sems.at[at]),
                columns,
            )
        )
    return jobs


def scatter_scratch(layout, plan, shapes):
    scratch = []
    for which, way, columns in plan:
        rows, width = shapes[which]
        width = width if columns is None else columns[1]
        scratch += scatter_buffers(layout, layout.orders[way][::-1], rows, width, jnp.bfloat16)
    return scratch


def gather_kernel(layout, plan, count, *refs):
    shards, fulls = refs[:count], refs[count : 2 * count]
    send_sems, recv_sems, local_sems = refs[2 * count :]
    own = layout.own()
    layout.greet(own)
    jobs = gather_jobs(layout, own, plan, shards, fulls, send_sems, recv_sems, local_sems)
    for todo in run_rounds(jobs, len(layout.dims), 5):
        for job, stage in todo:
            job.advance(stage)
    for job in jobs:
        job.finish()


def gather_all(layout, arrays, plan, collective_id):
    return pl.pallas_call(
        functools.partial(gather_kernel, layout, plan, len(arrays)),
        out_shape=gather_shapes(layout, arrays),
        in_specs=[ANYWHERE] * len(arrays),
        out_specs=[ANYWHERE] * len(arrays),
        scratch_shapes=job_sems(layout, plan),
        compiler_params=pltpu.CompilerParams(
            collective_id=collective_id, has_side_effects=True, vmem_limit_bytes=63 * MIB
        ),
    )(*arrays)


def cut(which, way, width, pieces):
    if width % (pieces * 128):
        return [(which, way, None)]
    step = width // pieces
    return [(which, way, (at * step, step)) for at in range(pieces)]


def weave(first, second):
    out = []
    for at in range(max(len(first), len(second))):
        out += first[at : at + 1] + second[at : at + 1]
    return out


def copy_kernel(count, *refs):
    for source, target in zip(refs[:count], refs[count:]):
        target[...] = source[...]


def copy_all(arrays):
    return pl.pallas_call(
        functools.partial(copy_kernel, len(arrays)),
        out_shape=[jax.ShapeDtypeStruct(a.shape, a.dtype) for a in arrays],
    )(*arrays)


def small_pack(layout, vectors):
    flat = jnp.concatenate([v.astype(jnp.float32).reshape(v.shape[0], -1) for v in vectors], 1)
    width = -(-flat.shape[1] // 1024) * 1024
    flat = jnp.pad(flat, ((0, 0), (0, width - flat.shape[1])))
    return flat.reshape(flat.shape[0], width // 128, 128)


def dot_plain(first_mat, second_mat):
    return jnp.dot(first_mat, second_mat, preferred_element_type=jnp.float32)


def dot_left_t(first_mat, second_mat):
    return lax.dot_general(
        first_mat, second_mat, (((0,), (0,)), ((), ())), preferred_element_type=jnp.float32
    )


def dot_right_t(first_mat, second_mat):
    return lax.dot_general(
        first_mat, second_mat, (((1,), (1,)), ((), ())), preferred_element_type=jnp.float32
    )


def row_mean(value):
    return jnp.sum(value, -1, keepdims=True) * (1.0 / value.shape[-1])


def norm_parts(row_data):
    centred = row_data - row_mean(row_data)
    inverse = lax.rsqrt(row_mean(centred * centred) + LN_EPS)
    return centred * inverse, inverse


def norm_backward(upstream, normed, inverse, gain_vec):
    scaled = upstream * gain_vec
    return inverse * (scaled - row_mean(scaled) - normed * row_mean(scaled * normed))


def column_sum(value):
    return jnp.sum(value, 0, keepdims=True)


def gelu_and_slope(inner_act):
    below = 0.5 * (1.0 + lax.erf(inner_act * 0.7071067811865476))
    bell = jnp.exp(-0.5 * inner_act * inner_act) * 0.3989422804014327
    return inner_act * below, below + inner_act * bell


GATHER_TIMES = (0, 1, 2, 3.5, 4.25)
SCATTER_TIMES = (0, 0.75, 2.75, 3.75, 6.75)
GROUP = 4
SPAN = GROUP * HEAD_DIM


def spread(rows, diag):
    return jnp.concatenate([rows] * GROUP, 0) * diag


def fold(square, seq_len):
    lane = lax.broadcasted_iota(jnp.int32, (seq_len, square.shape[1]), 1)
    out = square[:seq_len]
    for head in range(1, GROUP):
        block = square[head * seq_len : (head + 1) * seq_len]
        out = jnp.where(lane >= head * HEAD_DIM, block, out)
    return out


def probabilities(keys, wide_queries, length):
    scores = dot_right_t(keys, wide_queries) * HEAD_DIM ** (-0.5)
    at = lax.broadcasted_iota(jnp.int32, scores.shape, 0)
    scores = jnp.where(at < length, scores, MASKED)
    raised = jnp.exp(scores - jnp.max(scores, 0, keepdims=True))
    return raised * (1.0 / jnp.sum(raised, 0, keepdims=True))


def attend_kernel(
    layout,
    seq_len,
    plan,
    entries,
    count,
    steps,
    lengths_ref,
    x_ref,
    query_w,
    key_w,
    value_w,
    proj_w,
    vec_ref,
    diag_ref,
    *refs,
):
    shards, (q_ref, k_ref, v_ref, mix_ref, sum_ref, cls_ref) = refs[:count], refs[count : count + 6]
    fulls, sems = refs[count + 6 : 2 * count + 6], refs[2 * count + 6 :]
    rows, width = x_ref.shape
    held = rows // seq_len
    step = pl.program_id(0)
    first = step * held
    own = layout.own()

    @pl.when(step == 0)
    def _():
        layout.greet(own)

    jobs = gather_jobs(layout, own, plan, shards, fulls, *sems)
    places = [(at, point) for at in range(steps) for point in range(4)]
    sidecar = Sidecar(jobs, entries, len(layout.dims), GATHER_TIMES, evenly(places))
    sidecar.visit(step, 0)
    x = x_ref[...]
    q_ref[...] = (dot_plain(x, query_w[...]) + vec_ref[0:1, :]).astype(jnp.bfloat16)
    k_ref[...] = dot_plain(x, key_w[...]).astype(jnp.bfloat16)
    v_ref[...] = (dot_plain(x, value_w[...]) + vec_ref[1:2, :]).astype(jnp.bfloat16)
    diag = diag_ref[...]
    sidecar.visit(step, 1)

    def sentence(at):
        length = lengths_ref[first + at]
        here = pl.ds(at * seq_len, seq_len)
        for low in range(0, width, SPAN):
            cols = pl.ds(low, SPAN)
            wide = spread(q_ref[here, cols], diag)
            probs = probabilities(k_ref[here, cols], wide, length).astype(jnp.bfloat16)
            mixed = fold(dot_left_t(probs, v_ref[here, cols]), seq_len)
            mix_ref[here, cols] = mixed.astype(jnp.bfloat16)

    for at in range(held // 2):
        sentence(at)
    sidecar.visit(step, 2)
    for at in range(held // 2, held):
        sentence(at)
    sidecar.visit(step, 3)
    total = x.astype(jnp.float32) + dot_plain(mix_ref[...], proj_w[...]) + vec_ref[2:3, :]
    sum_ref[...] = total
    for at in range(held):
        cls_ref[0, at : at + 1, :] = total[at * seq_len : at * seq_len + 1]

    @pl.when(step == steps - 1)
    def _():
        sidecar.finish()


def whole(shape):
    return pl.BlockSpec(shape, lambda *_: (0,) * len(shape), pipeline_mode=pl.Buffered(1))


def attend(
    layout, x, lengths, weights, vec, diag, arrays, plan, entries, seq_len, rows, collective_id
):
    total, width = x.shape
    steps = total // rows
    held = rows // seq_len
    block = pl.BlockSpec((rows, width), lambda i: (i, 0))
    narrow = jax.ShapeDtypeStruct((total, width), jnp.bfloat16)
    return pl.pallas_call(
        functools.partial(attend_kernel, layout, seq_len, plan, entries, len(arrays), steps),
        grid=(steps,),
        out_shape=[
            narrow,
            narrow,
            narrow,
            narrow,
            jax.ShapeDtypeStruct((total, width), jnp.float32),
            jax.ShapeDtypeStruct((steps, held, width), jnp.float32),
        ]
        + gather_shapes(layout, arrays),
        in_specs=[pl.BlockSpec(memory_space=pltpu.SMEM), block]
        + [whole(w.shape) for w in weights]
        + [whole(vec.shape), whole(diag.shape)]
        + [ANYWHERE] * len(arrays),
        out_specs=[block] * 5
        + [pl.BlockSpec((1, held, width), lambda i: (i, 0, 0))]
        + [ANYWHERE] * len(arrays),
        scratch_shapes=job_sems(layout, plan),
        compiler_params=pltpu.CompilerParams(
            collective_id=collective_id, has_side_effects=True, vmem_limit_bytes=63 * MIB
        ),
    )(lengths, x, *weights, vec, diag, *arrays)


def feed_kernel(
    seq_len,
    blocks,
    pieces,
    sum_ref,
    tok_ref,
    mix_ref,
    cls_ref,
    inner_w,
    outer_w,
    vec_ref,
    bias_ref,
    out_ref,
    back_ref,
    inner_grad,
    outer_grad,
    proj_grad,
    vec_grad,
    bias_grad,
    slope,
    active,
    inner_b,
    hidden_b,
    second_b,
    proj_sum,
):
    step = pl.program_id(0)
    rows, width = sum_ref.shape
    piece = active.shape[2]

    @pl.when(step == 0)
    def _():
        vec_grad[...] = jnp.zeros_like(vec_grad)
        bias_grad[...] = jnp.zeros_like(bias_grad)
        proj_sum[...] = jnp.zeros_like(proj_sum)

    @pl.when(step < blocks)
    def _():
        here = pl.ds(pl.multiple_of(step * rows, rows), rows)
        gain_one, shift_one = vec_ref[3:4, :], vec_ref[4:5, :]
        gain_two, shift_two = vec_ref[6:7, :], vec_ref[7:8, :]
        normed_one, inverse_one = norm_parts(sum_ref[...])
        hidden = normed_one * gain_one + shift_one
        narrow = hidden.astype(jnp.bfloat16)
        hidden_b[here, :] = narrow
        second_sum = hidden + vec_ref[5:6, :]
        for at in range(pieces):
            cols = slice(at * piece, (at + 1) * piece)
            value, steep = gelu_and_slope(dot_plain(narrow, inner_w[:, cols]) + bias_ref[:, cols])
            value = value.astype(jnp.bfloat16)
            slope[at] = steep
            active[at, here, :] = value
            second_sum = second_sum + dot_plain(value, outer_w[cols, :])
        normed_two, inverse_two = norm_parts(second_sum)
        out_ref[...] = (normed_two * gain_two + shift_two).astype(jnp.bfloat16)
        grad = tok_ref[...].astype(jnp.float32).reshape(rows // seq_len, seq_len, width)
        place = lax.broadcasted_iota(jnp.int32, grad.shape, 1)
        extra = cls_ref[...].reshape(rows // seq_len, 1, width)
        grad = (grad + jnp.where(place == 0, extra, 0.0)).reshape(rows, width)
        vec_grad[6:7, :] += column_sum(grad * normed_two)
        vec_grad[7:8, :] += column_sum(grad)
        second = norm_backward(grad, normed_two, inverse_two, gain_two)
        vec_grad[5:6, :] += column_sum(second)
        narrow_two = second.astype(jnp.bfloat16)
        second_b[here, :] = narrow_two
        hidden_grad = second
        for at in range(pieces):
            cols = slice(at * piece, (at + 1) * piece)
            inner = dot_right_t(narrow_two, outer_w[cols, :]) * slope[at]
            bias_grad[:, cols] += column_sum(inner)
            inner = inner.astype(jnp.bfloat16)
            inner_b[at, here, :] = inner
            hidden_grad = hidden_grad + dot_right_t(inner, inner_w[:, cols])
        vec_grad[3:4, :] += column_sum(hidden_grad * normed_one)
        vec_grad[4:5, :] += column_sum(hidden_grad)
        first = norm_backward(hidden_grad, normed_one, inverse_one, gain_one)
        vec_grad[2:3, :] += column_sum(first)
        back_ref[...] = first
        proj_sum[...] += dot_left_t(mix_ref[...], first.astype(jnp.bfloat16))

        @pl.when(step == blocks - 1)
        def _():
            proj_grad[...] = proj_sum[...].astype(jnp.bfloat16)

    @pl.when(step >= blocks)
    def _():
        at = step - blocks
        outer_grad[...] = dot_left_t(active[at], second_b[...]).astype(jnp.bfloat16)
        inner_grad[...] = dot_left_t(hidden_b[...], inner_b[at]).astype(jnp.bfloat16)


def feed(
    first_sum, tokens_grad, mixture, cls_grad, inner_w, outer_w, vec, bias, seq_len, rows, piece
):
    total, width = first_sum.shape
    wide = inner_w.shape[1]
    blocks, pieces = total // rows, wide // piece
    held = rows // seq_len
    block = pl.BlockSpec((rows, width), lambda i: (jnp.minimum(i, blocks - 1), 0))
    return pl.pallas_call(
        functools.partial(feed_kernel, seq_len, blocks, pieces),
        grid=(blocks + pieces,),
        out_shape=[
            jax.ShapeDtypeStruct((total, width), jnp.bfloat16),
            jax.ShapeDtypeStruct((total, width), jnp.float32),
            jax.ShapeDtypeStruct(inner_w.shape, jnp.bfloat16),
            jax.ShapeDtypeStruct(outer_w.shape, jnp.bfloat16),
            jax.ShapeDtypeStruct((width, width), jnp.bfloat16),
            jax.ShapeDtypeStruct((8, width), jnp.float32),
            jax.ShapeDtypeStruct((1, wide), jnp.float32),
        ],
        in_specs=[
            block,
            block,
            block,
            pl.BlockSpec((1, held, width), lambda i: (jnp.minimum(i, blocks - 1), 0, 0)),
            whole(inner_w.shape),
            whole(outer_w.shape),
            whole(vec.shape),
            whole(bias.shape),
        ],
        out_specs=[
            block,
            block,
            pl.BlockSpec((width, piece), lambda i: (0, jnp.maximum(i - blocks, 0))),
            pl.BlockSpec((piece, width), lambda i: (jnp.maximum(i - blocks, 0), 0)),
            whole((width, width)),
            pl.BlockSpec((8, width), lambda i: (0, 0)),
            pl.BlockSpec((1, wide), lambda i: (0, 0)),
        ],
        scratch_shapes=[
            pltpu.VMEM((pieces, rows, piece), jnp.float32),
            pltpu.VMEM((pieces, total, piece), jnp.bfloat16),
            pltpu.VMEM((pieces, total, piece), jnp.bfloat16),
            pltpu.VMEM((total, width), jnp.bfloat16),
            pltpu.VMEM((total, width), jnp.bfloat16),
            pltpu.VMEM((width, width), jnp.float32),
        ],
        compiler_params=pltpu.CompilerParams(vmem_limit_bytes=63 * MIB),
    )(first_sum, tokens_grad, mixture, cls_grad, inner_w, outer_w, vec, bias)


def unflat(flat, dims):
    digits = []
    for size in reversed(dims):
        digits.insert(0, flat % size)
        flat = flat // size
    return tuple(digits)


def back_kernel(
    layout,
    seq_len,
    blocks,
    plan,
    entries,
    count,
    lengths_ref,
    x_ref,
    q_ref,
    k_ref,
    v_ref,
    first_ref,
    query_w,
    key_w,
    value_w,
    proj_w,
    diag_ref,
    feed_vec,
    feed_bias,
    pool_vec,
    *refs,
):
    step = pl.program_id(0)
    rows, width = x_ref.shape
    held = rows // seq_len
    scale = HEAD_DIM ** (-0.5)
    stages = len(layout.dims)
    parts, refs = refs[:count], refs[count:]
    (in_ref, vec_sum), refs = refs[:2], refs[2:]
    sums, refs = refs[: count + 3], refs[count + 3 :]
    (x_all, dq_all, dk_all, dv_all, dmix), refs = refs[:5], refs[5:]
    own_parts, refs = refs[:3], refs[3:]
    (vec_grad, vec_lands), refs = refs[:2], refs[2:]
    vec_steps, refs = refs[: stages - 1], refs[stages - 1 :]
    own = layout.own()
    vec_job = SumJob(layout, own, vec_grad, vec_lands, tuple(vec_steps) + (vec_sum,), refs[-2:])
    jobs = scatter_jobs(layout, own, plan, parts + own_parts, sums, refs[:-5], *refs[-5:-2])

    own_at = sorted({entry for entry, job in zip(entries, plan) if job[0] >= count})

    def place(when, last):
        if when < own_at[0]:
            half = int(when * 2 * blocks / own_at[0])
            return (half // 2, half % 2)
        for at, entry in enumerate(own_at):
            if when <= entry:
                return (blocks + at, 1)
        half = int((when - own_at[-1]) * blocks / (last - own_at[-1]))
        return (blocks + 3 + half, 0) if half < blocks else (2 * blocks + 2, 1)

    last_entry = max(entries)
    sidecar = Sidecar(jobs + [vec_job], list(entries) + [last_entry], stages, SCATTER_TIMES, place)

    @pl.when(step == 0)
    def _():
        layout.greet(own)
        vec_grad[0:2, :] = jnp.zeros_like(vec_grad[0:2, :])
        vec_grad[2:8, :] = feed_vec[2:8, :]
        vec_grad[8:9, :] = pool_vec[...]
        pieces = feed_bias.shape[1] // width
        vec_grad[9:, :] = jnp.zeros_like(vec_grad[9:, :])
        for at in range(pieces):
            vec_grad[9 + at : 10 + at, :] = feed_bias[:, at * width : (at + 1) * width]

    @pl.when(step < blocks)
    def _():
        here = pl.ds(pl.multiple_of(step * rows, rows), rows)
        sidecar.visit(step, 0)
        x_all[here, :] = x_ref[...]
        narrow = first_ref[...].astype(jnp.bfloat16)
        dmix[...] = dot_right_t(narrow, proj_w[...]).astype(jnp.bfloat16)
        diag = diag_ref[...]

        def sentence(at):
            length = lengths_ref[step * held + at]
            near = pl.ds(at * seq_len, seq_len)
            far = pl.ds(pl.multiple_of(step * rows + at * seq_len, seq_len), seq_len)
            for low in range(0, width, SPAN):
                cols = pl.ds(low, SPAN)
                keys = k_ref[near, cols]
                wide = spread(q_ref[near, cols], diag)
                wide_grad = spread(dmix[near, cols], diag)
                probs = probabilities(keys, wide, length)
                prob_grad = dot_right_t(v_ref[near, cols], wide_grad)
                dv_all[far, cols] = dot_plain(probs.astype(jnp.bfloat16), wide_grad).astype(
                    jnp.bfloat16
                )
                score_grad = probs * (prob_grad - column_sum(prob_grad * probs))
                score_grad = score_grad.astype(jnp.bfloat16)
                dk_all[far, cols] = (dot_plain(score_grad, wide) * scale).astype(jnp.bfloat16)
                dq_all[far, cols] = (fold(dot_left_t(score_grad, keys), seq_len) * scale).astype(
                    jnp.bfloat16
                )

        for at in range(held // 2):
            sentence(at)
        sidecar.visit(step, 1)
        for at in range(held // 2, held):
            sentence(at)
        vec_grad[0:1, :] += column_sum(dq_all[here, :].astype(jnp.float32))
        vec_grad[1:2, :] += column_sum(dv_all[here, :].astype(jnp.float32))

    for at, (right, part) in enumerate(zip((dq_all, dk_all, dv_all), own_parts)):

        @pl.when(step == blocks + at)
        def _():
            value = dot_left_t(x_all[...], right[...])
            share = part.shape[-2]
            for device in range(layout.count):
                piece = value[device * share : (device + 1) * share]
                part[unflat(device, layout.dims)] = piece.astype(jnp.bfloat16)
            sidecar.visit(step, 1)

    @pl.when(step >= blocks + 3)
    def _():
        sidecar.visit(step, 0)
        here = pl.ds(pl.multiple_of((step - blocks - 3) * rows, rows), rows)
        in_ref[...] = (
            first_ref[...]
            + dot_right_t(dq_all[here, :], query_w[...])
            + dot_right_t(dk_all[here, :], key_w[...])
            + dot_right_t(dv_all[here, :], value_w[...])
        )
        sidecar.visit(step, 1)

    @pl.when(step == 2 * blocks + 2)
    def _():
        sidecar.finish()


def back(
    layout,
    x,
    lengths,
    saved,
    first_grad,
    weights,
    diag,
    vectors,
    arrays,
    plan,
    entries,
    seq_len,
    rows,
    collective_id,
):
    total, width = x.shape
    blocks = total // rows
    stages = len(layout.dims)
    share = width // layout.count
    shapes = [a.shape[-2:] for a in arrays] + [(share, width)] * 3
    block = pl.BlockSpec((rows, width), lambda i: (jnp.minimum(i, blocks - 1), 0))
    twice = pl.BlockSpec(
        (rows, width),
        lambda i: (jnp.where(i < blocks, i, jnp.maximum(i - blocks - 3, 0)), 0),
    )
    out_block = pl.BlockSpec((rows, width), lambda i: (jnp.maximum(i - blocks - 3, 0), 0))
    small = pltpu.VMEM((16, width), jnp.float32)
    return pl.pallas_call(
        functools.partial(back_kernel, layout, seq_len, blocks, plan, entries, len(arrays)),
        grid=(2 * blocks + 3,),
        out_shape=[
            jax.ShapeDtypeStruct((total, width), jnp.float32),
            jax.ShapeDtypeStruct((16, width), jnp.float32),
        ]
        + [jax.ShapeDtypeStruct(s, jnp.float32) for s in shapes],
        in_specs=[pl.BlockSpec(memory_space=pltpu.SMEM)]
        + [block] * 4
        + [twice]
        + [whole(w.shape) for w in weights]
        + [whole(diag.shape)]
        + [whole(v.shape) for v in vectors]
        + [ANYWHERE] * len(arrays),
        out_specs=[out_block, whole((16, width))] + [whole(s) for s in shapes],
        scratch_shapes=[pltpu.VMEM((total, width), jnp.bfloat16)] * 4
        + [pltpu.VMEM((rows, width), jnp.bfloat16)]
        + [pltpu.VMEM(layout.dims + (share, width), jnp.bfloat16)] * 3
        + [small, pltpu.VMEM((layout.sends, 16, width), jnp.float32)]
        + [small] * (stages - 1)
        + scatter_scratch(layout, plan, shapes)
        + job_sems(layout, plan)
        + [pltpu.SemaphoreType.DMA((layout.sends,))] * 2,
        compiler_params=pltpu.CompilerParams(
            collective_id=collective_id, has_side_effects=True, vmem_limit_bytes=63 * MIB
        ),
    )(lengths, x, *saved, first_grad, *weights, diag, *vectors, *arrays)


def rank_kernel(
    layout,
    micros,
    node_dev,
    steps,
    sum_ref,
    inner_w,
    outer_w,
    pool_w,
    vec_ref,
    bias_ref,
    node_ref,
    cls_grad,
    pool_grad,
    shift_grad,
    hidden,
    total,
    mine,
    units,
    node_cols,
    totals,
    send_sems,
    recv_sems,
    local_sems,
):
    step = pl.program_id(0)
    sentences, width = sum_ref.shape
    own = layout.own()

    @pl.when(step == 0)
    def _():
        layout.greet(own)
        normed, _ = norm_parts(sum_ref[...])
        start = normed * vec_ref[3:4, :] + vec_ref[4:5, :]
        hidden[...] = start.astype(jnp.bfloat16)
        total[...] = start + vec_ref[5:6, :]
        node_cols[...] = node_ref[...].T

    value, _ = gelu_and_slope(dot_plain(hidden[...], inner_w[...]) + bias_ref[...])
    total[...] += dot_plain(value.astype(jnp.bfloat16), outer_w[...])

    @pl.when(step == steps - 1)
    def _():
        normed, _ = norm_parts(total[...])
        cls_rows = (normed * vec_ref[6:7, :] + vec_ref[7:8, :]).astype(jnp.bfloat16)
        pooled = jnp.tanh(dot_plain(cls_rows, pool_w[...]) + vec_ref[8:9, :])
        scale_inv = lax.rsqrt(jnp.sum(pooled * pooled, -1, keepdims=True) + UNIT_EPS)
        unit = pooled * scale_inv
        mine[...] = unit.astype(jnp.bfloat16)
        step_cols = width // len(layout.orders)
        plan = [(0, way, (way * step_cols, step_cols)) for way in range(len(layout.orders))]
        jobs = gather_jobs(layout, own, plan, [mine], [units], send_sems, recv_sems, local_sems)
        for stage in range(len(layout.dims) + 1):
            for job in jobs:
                job.advance(stage)
        for job in jobs:
            job.finish()

        device = own[0]
        for size, digit in zip(layout.dims[1:], own[1:]):
            device = device * size + digit
        at_home = pl.ds(pl.multiple_of(device * node_dev, node_dev), node_dev)
        count = layout.count * node_dev
        band = min(count, 512)
        every = units[...].reshape(layout.count, sentences, width)
        grads = []

        def scored(similar, tongue, place, side, tongue_row, place_row, side_row):
            across = side != side_row
            include = across & (tongue == tongue_row)
            positive = jnp.where(across & (place == place_row), 1.0, 0.0)
            return (
                jnp.where(include, SIM_SCALE * similar - SIM_SCALE * MARGIN * positive, MASKED),
                include,
                positive,
            )

        half = node_dev // 2

        def sides(shape, dim, offset):
            return (lax.broadcasted_iota(jnp.int32, shape, dim) + offset) // half % 2

        for micro in range(micros):
            here = slice(micro * node_dev, (micro + 1) * node_dev)
            nodes = every[:, here, :].reshape(count, width)
            tongue, place = node_cols[:, 2 * micro : 2 * micro + 1], node_cols[
                :, 2 * micro + 1 : 2 * micro + 2
            ]
            for low in range(0, count, band):
                cols = slice(low, low + band)
                similar = dot_right_t(nodes, nodes[cols])
                value, _, _ = scored(
                    similar,
                    tongue,
                    place,
                    sides((count, 1), 0, 0),
                    node_ref[2 * micro : 2 * micro + 1, cols],
                    node_ref[2 * micro + 1 : 2 * micro + 2, cols],
                    sides((1, band), 1, low),
                )
                peak = jnp.max(value, 0, keepdims=True)
                totals[:, cols] = jnp.log(column_sum(jnp.exp(value - peak))) + peak
            value, include, positive = scored(
                dot_right_t(mine[here, :], nodes),
                node_cols[at_home, 2 * micro : 2 * micro + 1],
                node_cols[at_home, 2 * micro + 1 : 2 * micro + 2],
                sides((node_dev, 1), 0, 0),
                node_ref[2 * micro : 2 * micro + 1, :],
                node_ref[2 * micro + 1 : 2 * micro + 2, :],
                sides((1, count), 1, 0),
            )
            peak = jnp.max(value, -1, keepdims=True)
            line = jnp.log(jnp.sum(jnp.exp(value - peak), -1, keepdims=True)) + peak
            grad_sim = jnp.where(
                include, jnp.exp(value - line) + jnp.exp(value - totals[...]), 0.0
            )
            grad_sim = (grad_sim - 2.0 * positive).astype(jnp.bfloat16)
            grads.append(SIM_SCALE * dot_plain(grad_sim, nodes))
        unit_grad = jnp.concatenate(grads, 0)
        pooled_grad = scale_inv * (
            unit_grad - unit * jnp.sum(unit_grad * unit, -1, keepdims=True)
        )
        pre_grad = pooled_grad * (1.0 - pooled * pooled)
        narrow = pre_grad.astype(jnp.bfloat16)
        pool_grad[...] = dot_left_t(cls_rows, narrow).astype(jnp.bfloat16)
        shift_grad[...] = column_sum(pre_grad)
        value = dot_right_t(narrow, pool_w[...])
        held = cls_grad.shape[1]
        for at in range(cls_grad.shape[0]):
            cls_grad[at] = value[at * held : (at + 1) * held]


def rank(
    layout, cls_sum, inner_w, outer_w, pool_w, vec, bias, nodes, micros, piece, held, collective_id
):
    sentences, width = cls_sum.shape
    wide = inner_w.shape[1]
    steps = wide // piece
    node_dev = sentences // micros
    return pl.pallas_call(
        functools.partial(rank_kernel, layout, micros, node_dev, steps),
        grid=(steps,),
        out_shape=[
            jax.ShapeDtypeStruct((sentences // held, held, width), jnp.float32),
            jax.ShapeDtypeStruct((width, width), jnp.bfloat16),
            jax.ShapeDtypeStruct((1, width), jnp.float32),
        ],
        in_specs=[
            whole(cls_sum.shape),
            pl.BlockSpec((width, piece), lambda i: (0, i)),
            pl.BlockSpec((piece, width), lambda i: (i, 0)),
            whole(pool_w.shape),
            whole(vec.shape),
            pl.BlockSpec((1, piece), lambda i: (0, i)),
            whole(nodes.shape),
        ],
        out_specs=[
            whole((sentences // held, held, width)),
            pl.BlockSpec((width, width), lambda i: (0, 0)),
            pl.BlockSpec((1, width), lambda i: (0, 0)),
        ],
        scratch_shapes=[
            pltpu.VMEM((sentences, width), jnp.bfloat16),
            pltpu.VMEM((sentences, width), jnp.float32),
            pltpu.VMEM((sentences, width), jnp.bfloat16),
            pltpu.VMEM(layout.dims + (sentences, width), jnp.bfloat16),
            pltpu.VMEM((nodes.shape[1], nodes.shape[0]), jnp.float32),
            pltpu.VMEM((1, nodes.shape[1]), jnp.float32),
        ]
        + job_sems(layout, layout.orders),
        compiler_params=pltpu.CompilerParams(
            collective_id=collective_id, has_side_effects=True, vmem_limit_bytes=63 * MIB
        ),
    )(cls_sum, inner_w, outer_w, pool_w, vec, bias, nodes)


def on_device(
    layout,
    hidden_in,
    lengths,
    partner,
    language,
    token_cotangent,
    query_weight,
    key_weight,
    value_weight,
    attn_out_weight,
    query_bias,
    value_bias,
    attn_out_bias,
    ln1_gain,
    ln1_shift,
    in_weight,
    in_bias,
    out_weight,
    out_bias,
    ln2_gain,
    ln2_shift,
    pool_weight,
    pool_bias,
):
    micro_count, sides, pair_dev, seq_len, model_width = hidden_in.shape
    inner_width = in_weight.shape[1]
    count = layout.count
    node_dev = sides * pair_dev
    sent_count = micro_count * node_dev
    row_count = sent_count * seq_len
    pair_count = partner.shape[1]
    device = lax.axis_index("dp") * (count // layout.slow) + lax.axis_index("fsdp")

    vectors = (
        query_bias,
        value_bias,
        attn_out_bias,
        ln1_gain,
        ln1_shift,
        out_bias,
        ln2_gain,
        ln2_shift,
        pool_bias,
        in_bias,
    )
    small = small_pack(layout, [v[None] for v in vectors])[0]
    arrays = [query_weight, key_weight, value_weight, attn_out_weight, small]
    plan = [(4, 0, None)]
    plan += weave(cut(0, 0, model_width, 2), cut(1, 1, model_width, 2))
    plan += weave(cut(2, 0, model_width, 2), cut(3, 1, model_width, 2))
    gathered = gather_all(layout, arrays, tuple(plan), 0)

    def joined(full, array):
        return full.reshape((count * array.shape[0],) + array.shape[1:])

    *weights, small_full = map(joined, gathered, arrays)
    small_rows = small_full.reshape(count, -1)
    share = query_bias.shape[0]
    rows_of = len(vectors) - 1
    vec = small_rows[:, : rows_of * share].reshape(count, rows_of, share)
    vec = jnp.moveaxis(vec, 1, 0).reshape(rows_of, model_width)
    vec = jnp.pad(vec, ((0, 16 - rows_of), (0, 0)))
    bias = small_rows[:, rows_of * share : rows_of * share + in_bias.shape[0]]
    bias = bias.reshape(1, inner_width)

    pair_ids = jnp.arange(pair_count, dtype=jnp.int32)
    hit = partner[:, :, None] == pair_ids[None, None, :]
    target_language = jnp.sum(jnp.where(hit, language[:, :, None], 0), 1)

    def split(value):
        return value.reshape(micro_count, count, 1, pair_dev)

    node_rows = jnp.stack(
        [
            jnp.concatenate([split(language), split(target_language)], 2),
            jnp.concatenate(
                [split(partner), split(jnp.broadcast_to(pair_ids, partner.shape))], 2
            ),
        ],
        1,
    )
    node_rows = node_rows.reshape(2 * micro_count, count * node_dev).astype(jnp.float32)
    node_rows = jnp.pad(node_rows, ((0, -2 * micro_count % 8), (0, 0)))
    block_at = jnp.arange(SPAN) // HEAD_DIM
    diag = (block_at[:, None] == block_at[None, :]).astype(jnp.bfloat16)

    x = hidden_in.reshape(row_count, model_width)
    sent_lengths = lengths.reshape(sent_count)
    arrays = [in_weight, out_weight, pool_weight]

    def halves(which):
        return cut(which, 0, model_width, 2)[:1] + cut(which, 1, model_width, 2)[1:]

    first_cuts, second_cuts = cut(0, 0, inner_width, 8), cut(1, 1, model_width, 6)
    plan = weave(first_cuts[:6], second_cuts)
    plan += halves(2) + first_cuts[6:]
    entries = tuple(0.4 * at for at in range(len(plan)))
    queries, keys, values, mixture, first_sum, cls_sum, *gathered = attend(
        layout, x, sent_lengths, weights, vec, diag, arrays, tuple(plan), entries, seq_len, 512, 1
    )
    inner_full, outer_full, pool_full = map(joined, gathered, arrays)
    cls_grad, grad_pool, grad_pool_shift = rank(
        layout,
        cls_sum.reshape(sent_count, model_width),
        inner_full,
        outer_full,
        pool_full,
        vec,
        bias,
        node_rows,
        micro_count,
        768,
        256 // seq_len,
        2,
    )
    block_out, first_grad, grad_inner, grad_outer, grad_proj, vec_grad, grad_bias = feed(
        first_sum,
        token_cotangent.reshape(row_count, model_width),
        mixture,
        cls_grad,
        inner_full,
        outer_full,
        vec,
        bias,
        seq_len,
        256,
        768,
    )

    def apart(part):
        return part.reshape(layout.dims + (-1, part.shape[1]))

    parts = list(map(apart, (grad_inner, grad_outer, grad_pool, grad_proj)))
    first_cuts, second_cuts = cut(0, 0, inner_width, 4), cut(1, 1, model_width, 3)
    plan = weave(first_cuts[:3], second_cuts) + first_cuts[3:]
    plan += weave(halves(2)[::-1], halves(3)[::-1])
    entries = [0.75 * (at // 2) for at in range(len(plan))]
    for which in (4, 5, 6):
        entries += [entries[-1] + 0.75] * 2
        plan += halves(which)
    input_grad, vec_sum, *sums = back(
        layout,
        x,
        sent_lengths,
        (queries, keys, values),
        first_grad,
        weights,
        diag,
        (vec_grad, grad_bias, grad_pool_shift),
        parts,
        tuple(plan),
        tuple(entries),
        seq_len,
        256,
        3,
    )
    block_out = block_out.reshape(hidden_in.shape)
    input_grad = input_grad.reshape(hidden_in.shape)
    sums = copy_all(sums)
    vec_own = lax.dynamic_slice_in_dim(vec_sum[:rows_of], device * share, share, 1)
    bias_sum = vec_sum[rows_of : rows_of + inner_width // model_width].reshape(-1)
    bias_own = lax.dynamic_slice_in_dim(bias_sum, device * in_bias.shape[0], in_bias.shape[0])
    (
        sum_query_shift,
        sum_value_shift,
        sum_proj_shift,
        sum_gain_one,
        sum_shift_one,
        sum_outer_shift,
        sum_gain_two,
        sum_shift_two,
        sum_pool_shift,
    ) = vec_own
    return (
        block_out,
        input_grad,
        sums[4],
        sums[5],
        sums[6],
        sums[3],
        sum_query_shift,
        sum_value_shift,
        sum_proj_shift,
        sum_gain_one,
        sum_shift_one,
        sums[0],
        bias_own,
        sums[1],
        sum_outer_shift,
        sum_gain_two,
        sum_shift_two,
        sums[2],
        sum_pool_shift,
    )


def solution(mesh):
    rows = P(("dp", "fsdp"), None)
    vector = P(("dp", "fsdp"))
    sentences = P(None, None, ("dp", "fsdp"), None, None)
    placed = (
        (sentences, P(None, None, ("dp", "fsdp")), P(), P(), sentences)
        + (rows,) * 4
        + (vector,) * 5
        + (rows, vector, rows)
        + (vector,) * 3
        + (rows, vector)
    )
    return jax.shard_map(
        functools.partial(on_device, Layout(mesh.shape)),
        mesh=mesh,
        in_specs=placed,
        out_specs=(sentences, sentences)
        + (rows,) * 4
        + (vector,) * 5
        + (rows, vector, rows)
        + (vector,) * 3
        + (rows, vector),
        check_vma=False,
    )
```
